32 devices in a mesh: batch: 2 (over core), seq: 16 (over z, y, x).
Axes of the slice: x: 2, y: 2, z: 4, core: 2. Of those that a mesh axis runs over, the one named last changes fastest.
Arguments:
- inputs: bfloat16 [2, 8192, 768], P('batch', 'seq'), may hold values from -8 to 8
- w_qkv: bfloat16 [768, 2304], replicated, may hold values from -0.21875 to 0.21875
- w_out: bfloat16 [768, 768], replicated, may hold values from -0.875 to 0.875
- w_fc: bfloat16 [768, 3072], replicated, may hold values from -0.21875 to 0.21875
- w_proj: bfloat16 [3072, 768], replicated, may hold values from -0.109375 to 0.109375
- map_query: bfloat16 [12, 64, 64], replicated, may hold values from -1.5 to 1.5
- map_key: bfloat16 [12, 64, 64], replicated, may hold values from -1.5 to 1.5
- gain_attn: float32 [768], replicated, may hold values from 0.1 to 1.9
- gain_mlp: float32 [768], replicated, may hold values from 0.1 to 1.9
- starts: int32 [2, 128], P('batch', 'seq'), may hold values from 0 to 1, as said below
- key_mask: int32 [2, 8192], P('batch', 'seq'), may hold values from 0 to 1, as said below
- cotangent: bfloat16 [2, 8192, 768], P('batch', 'seq'), may hold values from -6 to 6
Outputs:
- output: float32 [2, 8192, 768], P('batch', 'seq')
- grad_inputs: float32 [2, 8192, 768], P('batch', 'seq')
- grad_w_qkv: float32 [768, 2304], P(('batch', 'seq'))
- grad_w_out: float32 [768, 768], P(('batch', 'seq'))
- grad_w_fc: float32 [768, 3072], P(('batch', 'seq'))
- grad_w_proj: float32 [3072, 768], P(None, ('batch', 'seq'))
- grad_map_query: float32 [12, 64, 64], replicated
- grad_map_key: float32 [12, 64, 64], replicated
- grad_gain_attn: float32 [768], replicated
- grad_gain_mlp: float32 [768], replicated
The draws below stay inside these ranges and needn't reach their ends.
Inputs may be any that keep to these rules, and one draw needn't show every extreme that they name: starts[:, 0] = 1; in every stream one sequence begins within the first 512 tokens and ends within the last 512 tokens; every other sequence spans two or more groups of 64 tokens. `key_mask`: padding lies only at the end of the last 64 tokens of a sequence; the first token of every group of 64 tokens is real.
All inputs are finite; a program needn't handle non-finite values.
Results may differ from the reference program's by a relative error of at most 0.012.
Values sent between devices are 32-bit elements; how exact they have to be, the bound alone decides.
No kernel may reach another device: no remote copies, remote signals or barrier semaphores. Data moves between devices by JAX's collectives and lax.ppermute only.
A program may use at most 512 MiB of HBM per device.

```python
from functools import partial
import jax
import jax.numpy as jnp
from jax import lax

D = 768
H = 12
HS = 64
FF = 3072
TOK_DEV = 512
UNIT = 64
BLOCK = 512
STREAMS = 2
TOKENS = 8192
UNITS = 128


def length_chain(power_key, within_key, count):
    powers = jnp.left_shift(jnp.int32(1), jax.random.randint(power_key, (STREAMS, count), 1, 6))
    within = jax.random.randint(within_key, (STREAMS, count), 0, 32) % powers
    lengths = jnp.minimum(powers + within, 32).astype(jnp.int32)
    return jnp.cumsum(lengths, axis=1).astype(jnp.int32)


def segment_layout(key):
    front_power, front_within, back_power, back_within, pad_key = jax.random.split(key, 5)
    per_device = TOK_DEV // UNIT
    count = per_device + 1
    front_chain = length_chain(front_power, front_within, count)
    fronts = jnp.concatenate([jnp.zeros((STREAMS, 1), jnp.int32), front_chain[:, :-1]], axis=1)
    backs = UNITS - length_chain(back_power, back_within, count)
    place = jnp.arange(UNITS).astype(jnp.int32)[None, :, None]
    hit_front = jnp.any((place == fronts[:, None, :]) & (fronts[:, None, :] <= per_device - 1), axis=2)
    hit_back = jnp.any((place == backs[:, None, :]) & (backs[:, None, :] >= UNITS - per_device + 1), axis=2)
    begins = hit_front | hit_back | (place[:, :, 0] == 0)
    flag_grid = begins.astype(jnp.int32)
    following = jnp.concatenate([flag_grid[:, 1:], jnp.ones((STREAMS, 1), jnp.int32)], axis=1)
    padding = jax.random.randint(pad_key, (STREAMS, UNITS), 0, UNIT)
    offset = jnp.arange(UNIT)[None, None, :]
    cut = (following[:, :, None] == 1) & (offset >= UNIT - padding[:, :, None])
    mask_grid = 1 - cut.astype(jnp.int32)
    return (flag_grid, mask_grid.reshape(STREAMS, TOKENS))


def draw_starts(key, part):
    flag_grid, mask_grid = segment_layout(key)
    return flag_grid


def draw_key_mask(key, part):
    flag_grid, mask_grid = segment_layout(key)
    return mask_grid


def draw_inputs(key, part):
    key = jax.random.fold_in(key, 7)
    noise_key, shift_key = jax.random.split(key, 2)
    shifts = jax.random.truncated_normal(shift_key, -4.0, 4.0, (STREAMS, UNITS, 1, D))
    noise = jax.random.truncated_normal(noise_key, -4.0, 4.0, (STREAMS, UNITS, UNIT, D))
    return (noise + shifts).reshape(STREAMS, TOKENS, D).astype(jnp.bfloat16)


def raised(entries, key, source, target, blocks, factor):
    owner, partner = [(jnp.arange(entries.shape[dim]) // (entries.shape[dim] // blocks)).reshape([-1 if axis == dim else 1 for axis in range(entries.ndim)]) for dim in (source, target)]
    chosen = jax.random.permutation(key, blocks)[partner]
    strong = (owner == chosen) | (owner == (partner + blocks // 2) % blocks)
    return jnp.where(strong, factor * entries, entries)


def shard_levels(own_key, dims, cuts, low, high):
    def one(dim, parts):
        draws = jax.random.uniform(jax.random.fold_in(jax.random.fold_in(own_key, 6), dim), (parts,), jnp.float32, low / len(cuts), high / len(cuts))
        return jnp.repeat(jnp.exp(draws), dims[dim] // parts).reshape((-1,) + (1,) * (len(dims) - dim - 1))

    level = one(*cuts[0])
    for cut in cuts[1:]:
        level = level * one(*cut)
    return level


def normal_values(stream_key, shape, spread, reach, cuts=(), dtype=jnp.bfloat16):
    values = jax.random.normal(stream_key, shape, jnp.float32) * spread
    if len(cuts) > 0:
        values = shard_levels(stream_key, shape, cuts, -0.22, 0.18) * values
    return jnp.clip(values, min=-reach, max=reach).astype(dtype)


def gaussian_with(own_key, dims, scale, limit, shards, heavy, dtype=jnp.bfloat16):
    values = scale * jax.random.normal(own_key, dims, jnp.float32)
    if shards:
        values = values * shard_levels(own_key, dims, shards, -0.22, 0.18)
    return jnp.clip(raised(values, jax.random.fold_in(own_key, 3), *heavy), -limit, limit).astype(dtype)


def setup_inputs(seed: int = 0) -> dict:
    seeds = jax.random.split(jax.random.key(seed), 13)
    inputs = draw_inputs(jax.random.fold_in(seeds[12], 71), 0)
    w_qkv = normal_values(seeds[1], (D, 3 * D), D ** -0.5, 0.21875)
    w_out = normal_values(seeds[2], (D, D), (D // 16) ** -0.5, 0.875)
    w_fc = normal_values(seeds[3], (D, FF), D ** -0.5, 0.21875)
    w_proj = normal_values(seeds[4], (FF, D), FF ** -0.5, 0.109375)
    map_query = normal_values(seeds[5], (H, HS, HS), (HS // 4) ** -0.5, 1.5)
    map_key = normal_values(seeds[6], (H, HS, HS), (HS // 4) ** -0.5, 1.5)
    gain_attn = jnp.clip(1.0 + 0.18 * jax.random.normal(seeds[7], (D,), jnp.float32), 0.1, 1.9)
    gain_mlp = jnp.clip(1.0 + 0.18 * jax.random.normal(seeds[8], (D,), jnp.float32), 0.1, 1.9)
    starts = draw_starts(jax.random.fold_in(seeds[12], 71), 0)
    key_mask = draw_key_mask(jax.random.fold_in(seeds[12], 71), 0)
    cotangent = gaussian_with(seeds[11], (STREAMS, TOKENS, D), 1.0, 6.0, ((0, 2), (1, 16)), (1, 2, 16, 2.0))
    return {"inputs": inputs, "w_qkv": w_qkv, "w_out": w_out, "w_fc": w_fc, "w_proj": w_proj, "map_query": map_query, "map_key": map_key, "gain_attn": gain_attn, "gain_mlp": gain_mlp, "starts": starts, "key_mask": key_mask, "cotangent": cotangent}


EPSILON = 1e-05
EXACT_PRECISION = lax.Precision.HIGHEST

@jax.custom_vjp
def low(v):
    return lax.optimization_barrier(v.astype(jnp.bfloat16)).astype(jnp.float32)

@jax.custom_vjp
def reduced_backward(v):
    return v

def low_keep(v):
    return (low(v), None)

def low_pass(kept, grad):
    return (grad,)

def back_keep(v):
    return (v, None)

def back_low(kept, grad):
    return (low(grad),)
low.defvjp(low_keep, low_pass)
reduced_backward.defvjp(back_keep, back_low)

def normalize(states, gain_vec):
    centre = lax.optimization_barrier(jnp.mean(states, axis=-1, keepdims=True))
    offsets = states - centre
    variance = lax.optimization_barrier(jnp.mean(offsets * offsets, axis=-1, keepdims=True))
    return offsets * lax.rsqrt(variance + EPSILON) * gain_vec

def feature_map(pre_map):
    return jnp.concatenate([jax.nn.softmax(pre_map, axis=-1), jax.nn.softmax(-pre_map, axis=-1)], axis=-1)

def block_step(weights, carry_state, pieces):
    w_qkv, w_out, w_fc, w_proj, map_query, map_key, gain_attn, gain_mlp = weights
    rows_in, counts_blk, live_blk, before, last_count = pieces
    block_len = rows_in.shape[0]
    model_dim = rows_in.shape[1]
    n_heads = map_query.shape[0]
    head_dim = map_query.shape[1]
    attn_in = low(normalize(rows_in, gain_attn))
    qkv_all = low(reduced_backward(jnp.dot(attn_in, w_qkv, precision=EXACT_PRECISION, preferred_element_type=jnp.float32)))
    queries = qkv_all[:, :model_dim].reshape(block_len, n_heads, head_dim)
    keys_all = qkv_all[:, model_dim:2 * model_dim].reshape(block_len, n_heads, head_dim)
    every_value = qkv_all[:, 2 * model_dim:].reshape(block_len, n_heads, head_dim)
    pre_query = reduced_backward(jnp.einsum('thd,hde->the', queries, map_query, precision=EXACT_PRECISION))
    pre_key = reduced_backward(jnp.einsum('thd,hde->the', keys_all, map_key, precision=EXACT_PRECISION))
    query_feature_map = low(feature_map(pre_query))
    key_feature_map = low(feature_map(pre_key))
    position = jnp.arange(block_len)
    causal = position[None, :] <= position[:, None]
    same_seg = counts_blk[None, :] == counts_blk[:, None]
    permitted_pairs = (causal & same_seg).astype(jnp.float32) * live_blk[None, :]
    score_matrix = reduced_backward(jnp.einsum('oaz,eaz->aoe', query_feature_map, key_feature_map, precision=EXACT_PRECISION) * permitted_pairs[None])
    contin = (counts_blk == before).astype(jnp.float32)
    numerator = jnp.einsum('hqk,khd->qhd', low(score_matrix), every_value, precision=EXACT_PRECISION)
    numerator = numerator + contin[:, None, None] * jnp.einsum('qhf,hfd->qhd', query_feature_map, carry_state[0], precision=EXACT_PRECISION)
    denominator = lax.optimization_barrier(jnp.sum(score_matrix, axis=-1)).T
    denominator = denominator + contin[:, None] * jnp.einsum('qhf,hf->qh', query_feature_map, carry_state[1], precision=EXACT_PRECISION)
    numerator = reduced_backward(numerator)
    mixed = low((numerator / denominator[:, :, None]).reshape(block_len, model_dim))
    hidden = rows_in + reduced_backward(jnp.dot(mixed, w_out, precision=EXACT_PRECISION, preferred_element_type=jnp.float32))
    mlp_in = low(normalize(hidden, gain_mlp))
    pre_act = reduced_backward(jnp.dot(mlp_in, w_fc, precision=EXACT_PRECISION, preferred_element_type=jnp.float32))
    act_low = low(jax.nn.gelu(pre_act, approximate=True))
    output = hidden + reduced_backward(jnp.dot(act_low, w_proj, precision=EXACT_PRECISION, preferred_element_type=jnp.float32))
    tail_mark = (counts_blk == last_count).astype(jnp.float32) * live_blk
    trailing_keys = key_feature_map * tail_mark[:, None, None]
    trailing_state = jnp.einsum('wba,wbm->bam', trailing_keys, every_value, precision=EXACT_PRECISION)
    tail_sum = lax.optimization_barrier(jnp.sum(trailing_keys, axis=0))
    keep_rate = (last_count == before).astype(jnp.float32)
    return ((trailing_state + keep_rate * carry_state[0], tail_sum + keep_rate * carry_state[1]), output)

def stream_forward(weights, rows_in, flag_row, live_mask):
    tok_total = rows_in.shape[0]
    unit_len = tok_total // flag_row.shape[0]
    seg_count = jnp.repeat(jnp.cumsum(flag_row).astype(jnp.int32), unit_len)
    n_blocks = tok_total // BLOCK
    counts_blocks = seg_count.reshape(n_blocks, BLOCK)
    first_units = (jnp.arange(n_blocks) * (BLOCK // unit_len)).astype(jnp.int32)
    before = counts_blocks[:, 0] - flag_row[first_units].astype(jnp.int32)
    last_count = counts_blocks[:, BLOCK - 1]
    n_heads = weights[4].shape[0]
    head_dim = weights[4].shape[1]
    start_state = (jnp.zeros((n_heads, 2 * head_dim, head_dim), jnp.float32), jnp.zeros((n_heads, 2 * head_dim), jnp.float32))
    stepper = jax.checkpoint(partial(block_step, weights))
    final_state, outputs = lax.scan(stepper, start_state, (rows_in.reshape(n_blocks, BLOCK, -1), counts_blocks, live_mask.astype(jnp.float32).reshape(n_blocks, BLOCK), before, last_count))
    return outputs.reshape(tok_total, -1)

def reference(inputs, w_qkv, w_out, w_fc, w_proj, map_query, map_key, gain_attn, gain_mlp, starts, key_mask, cotangent):
    weights = (w_qkv.astype(jnp.float32), w_out.astype(jnp.float32), w_fc.astype(jnp.float32), w_proj.astype(jnp.float32), map_query.astype(jnp.float32), map_key.astype(jnp.float32), gain_attn.astype(jnp.float32), gain_mlp.astype(jnp.float32))
    out_rows = []
    grad_rows = []
    totals = jax.tree.map(jnp.zeros_like, weights)
    for stream in range(inputs.shape[0]):

        def forward(weight_set, rows_in):
            return stream_forward(weight_set, rows_in, starts[stream], key_mask[stream])
        result, backward = jax.vjp(forward, weights, inputs[stream].astype(jnp.float32))
        weight_grads, input_grad = backward(cotangent[stream].astype(jnp.float32))
        out_rows.append(result)
        grad_rows.append(input_grad)
        totals = jax.tree.map(jnp.add, totals, weight_grads)
    return (jnp.stack(out_rows), jnp.stack(grad_rows), totals[0], totals[1], totals[2], totals[3], totals[4], totals[5], totals[6], totals[7])
```

```python
import functools

import jax
import jax.numpy as jnp
from jax import lax
from jax.experimental import pallas as pl
from jax.experimental.pallas import tpu as pltpu
from jax.sharding import PartitionSpec as P

EPSILON = 1e-05
F32 = jnp.float32
BF16 = jnp.bfloat16
CORE, SEQ, MEMBER, PLANE, FLAGS = 0, 1, 2, 3, 4
STATE_ROWS = 72
MIB = 1024 * 1024


def mm(a, b):
    return lax.dot_general(a, b, (((1,), (0,)), ((), ())), preferred_element_type=F32)


def nt(a, b):
    return lax.dot_general(a, b, (((1,), (1,)), ((), ())), preferred_element_type=F32)


def tn(a, b):
    return lax.dot_general(a, b, (((0,), (0,)), ((), ())), preferred_element_type=F32)


def split(v):
    high = v.astype(BF16)
    return high, (v - high.astype(F32)).astype(BF16)


def iota(shape, dim):
    return lax.broadcasted_iota(jnp.int32, shape, dim)


def segment_ones(width):
    shape = (width, width)
    return (iota(shape, 0) // 64 == iota(shape, 1) // 64).astype(BF16)


def segment_sum(v, ones):
    high, low = split(v)
    return mm(high, ones) + mm(low, ones)


def moments(x):
    centre = jnp.mean(x, axis=-1, keepdims=True)
    offsets = x - centre
    variance = jnp.mean(offsets * offsets, axis=-1, keepdims=True)
    scale = lax.rsqrt(variance + EPSILON)
    return offsets * scale, scale


def norm_back(grad, normed, scale, gain):
    dn = grad * gain
    first = jnp.mean(dn, axis=-1, keepdims=True)
    second = jnp.mean(dn * normed, axis=-1, keepdims=True)
    return (dn - first - normed * second) * scale


def fill_maps(scr, map_ref):
    scr[...] = jnp.zeros(scr.shape, scr.dtype)
    for h in range(4):
        m = map_ref[h].astype(F32)
        scr[64 * h : 64 * h + 64, 128 * h : 128 * h + 128] = jnp.concatenate(
            [m, -m], axis=1
        ).astype(scr.dtype)


def features(pre, ones):
    low_half = iota(pre.shape, 1) < 64
    top = jnp.max(jnp.where(low_half, pre, -jnp.inf), axis=1, keepdims=True)
    bottom = jnp.max(jnp.where(low_half, -jnp.inf, pre), axis=1, keepdims=True)
    e = jnp.exp(pre - jnp.where(low_half, top, bottom))
    return e / segment_sum(e, ones)


def features_back(feat, grad, ones):
    weighted = feat * grad
    total = segment_sum(weighted, ones)
    mass = mm(feat.astype(BF16), ones)
    part = weighted - feat * (total / mass)
    return part - pltpu.roll(part, 64, 1)


def whole(shape):
    return pl.BlockSpec(shape, lambda *_: (0,) * len(shape))


def columns(rows, width):
    return pl.BlockSpec((rows, width), lambda j, _: (0, j))


ANYWHERE = pl.BlockSpec(memory_space=pl.ANY)


def run(kernel, scal, tok, grid, ins, outs, scratch=(), limit=48, flops=0):
    def body(*refs):
        sc = refs[0]
        n_in, n_out = len(ins), len(outs)
        kernel(
            sc,
            *refs[1 : 1 + n_in],
            *refs[2 + n_in : 2 + n_in + n_out],
            *refs[3 + n_in + n_out :],
        )

    moved = sum(a.size * a.dtype.itemsize for a, _ in ins)
    result = pl.pallas_call(
        body,
        grid_spec=pltpu.PrefetchScalarGridSpec(
            num_scalar_prefetch=1,
            grid=grid,
            in_specs=[spec for _, spec in ins] + [ANYWHERE],
            out_specs=[spec for _, _, spec in outs] + [ANYWHERE],
            scratch_shapes=list(scratch),
        ),
        out_shape=[jax.ShapeDtypeStruct(shape, dtype) for shape, dtype, _ in outs]
        + [jax.ShapeDtypeStruct((8, 128), F32)],
        compiler_params=pltpu.CompilerParams(vmem_limit_bytes=limit * MIB),
        cost_estimate=pl.CostEstimate(flops=flops, bytes_accessed=moved, transcendentals=0),
    )(scal, *[a for a, _ in ins], tok)
    return list(result[:-1]), result[-1]


def keys_kernel(sc, x_ref, gain_ref, wk_ref, wv_ref, map_ref, mask_ref,
                attn_ref, k_ref, v_ref, fk_ref, p0, p1, p2, p3,
                allow_ref, allow_t_ref, tail_ref, contin_ref,
                map_scr, state_scr):
    j = pl.program_id(0)
    tokens = x_ref.shape[0]
    n_flags = sc.shape[0] - FLAGS
    unit = tokens // n_flags

    def seg(shape, dim):
        place = iota(shape, dim)
        total = jnp.zeros(shape, jnp.int32)
        for u in range(n_flags):
            total = total + jnp.where(place >= unit * u, sc[FLAGS + u], 0)
        return total

    @pl.when(j == 0)
    def _():
        normed, _ = moments(x_ref[...].astype(F32))
        attn_ref[...] = (normed * gain_ref[...]).astype(BF16)
        last = sc[FLAGS]
        for u in range(1, n_flags):
            last = last + sc[FLAGS + u]
        mask_row = mask_ref[...].astype(F32)
        mask_col = jnp.transpose(jnp.broadcast_to(mask_row, (128, tokens)))
        seg_col = seg((tokens, 128), 0)
        tail_ref[...] = jnp.where(seg_col == last, mask_col, 0.0)
        contin_ref[...] = jnp.where(seg_col == 0, 1.0, 0.0)
        square = (tokens, tokens)
        same = seg(square, 0) == seg(square, 1)
        allow_ref[...] = jnp.where(same & (iota(square, 1) <= iota(square, 0)), mask_row, 0.0)
        wide_mask = jnp.concatenate([mask_col] * (tokens // 128), axis=1)
        allow_t_ref[...] = jnp.where(same & (iota(square, 0) <= iota(square, 1)), wide_mask, 0.0)

    fill_maps(map_scr, map_ref)
    attn = attn_ref[...]
    k4 = mm(attn, wk_ref[...]).astype(BF16)
    v4 = mm(attn, wv_ref[...]).astype(BF16)
    k_ref[...] = k4
    v_ref[...] = v4
    pre = mm(k4, map_scr[...])
    ones = segment_ones(128)
    v_t = jnp.transpose(v4.astype(F32)).astype(BF16)
    tail = tail_ref[...]
    row_ones = jnp.ones((16, tokens), BF16)
    for h in range(4):
        feat = features(pre[:, 128 * h : 128 * h + 128], ones).astype(BF16)
        fk_ref[:, 128 * h : 128 * h + 128] = feat
        kept = (feat.astype(F32) * tail).astype(BF16)
        state_scr[4 * j + h, 0:64, :] = mm(v_t[64 * h : 64 * h + 64], kept)
        state_scr[4 * j + h, 64:72, :] = mm(row_ones, kept)[0:8]

    @pl.when(j == pl.num_programs(0) - 1)
    def _():
        for k, piece in enumerate((p0, p1, p2, p3)):
            n = piece.shape[0]
            piece[...] = state_scr[pl.ds((sc[MEMBER] ^ k) * n, n)]


def queries_kernel(sc, attn_ref, wq_ref, map_ref, fk_ref, v_ref, allow_ref,
                   q_ref, fq_ref, nd_ref, map_scr):
    tokens = attn_ref.shape[0]
    half = tokens // 2
    fill_maps(map_scr, map_ref)
    q4 = mm(attn_ref[...], wq_ref[...]).astype(BF16)
    q_ref[...] = q4
    pre = mm(q4, map_scr[...])
    ones = segment_ones(128)
    low_half = iota((tokens, 128), 1) < 64
    for h in range(4):
        lanes = slice(128 * h, 128 * h + 128)
        feat = features(pre[:, lanes], ones).astype(BF16)
        fq_ref[:, lanes] = feat
        fk = fk_ref[:, lanes]
        pair = v_ref[:, 128 * (h // 2) : 128 * (h // 2) + 128].astype(F32)
        if h % 2:
            pair = pltpu.roll(pair, 64, 1)
        wide = jnp.where(low_half, pair, 1.0).astype(BF16)
        first = nt(feat[:half], fk[:half]) * allow_ref[:half, :half]
        nd_ref[:half, lanes] = mm(first.astype(BF16), wide[:half])
        second = nt(feat[half:], fk) * allow_ref[half:, :]
        nd_ref[half:, lanes] = mm(second.astype(BF16), wide)


def plane_sum_kernel(sc, *refs):
    *pieces, out = refs
    total = pieces[0][...]
    for piece in pieces[1:]:
        total = total + piece[...]
    out[...] = total


def scan_kernel(backward, planes, sc, *refs):
    own = refs[:4]
    others = refs[4:-4]
    outs = refs[-4:]
    member, plane = sc[MEMBER], sc[PLANE]
    total = jnp.zeros(own[0].shape, F32)
    for i, other in enumerate(others):
        if planes is None:
            total = total + other[...]
        else:
            there = plane + i + 1 < planes if backward else plane - i - 1 >= 0
            total = total + jnp.where(there, other[...], 0.0)
    for k, out in enumerate(outs):
        value = total
        target = member ^ k
        for i, piece in enumerate(own):
            source = member ^ i
            counts = source > target if backward else source < target
            value = value + jnp.where(counts, piece[...], 0.0)
        out[...] = value


def place_heads(sc, scr, pieces):
    for k, piece in enumerate(pieces):
        n = piece.shape[0]
        scr[pl.ds((sc[MEMBER] ^ k) * n, n)] = piece[...]


def mix_kernel(sc, x_ref, nd_ref, fq_ref, c0, c1, c2, c3, contin_ref, wo_ref, gain_ref,
               mixed_ref, mf_ref, rden_ref, hidden_ref, mlp_ref, carry_scr):
    j = pl.program_id(0)
    tokens = x_ref.shape[0]
    low_half = iota((tokens, 128), 1) < 64

    @pl.when(j == 0)
    def _():
        place_heads(sc, carry_scr, (c0, c1, c2, c3))
        hidden_ref[...] = x_ref[...].astype(F32)

    contin = contin_ref[...]
    for pair in range(2):
        quotients, inverses = [], []
        for side in range(2):
            h = 2 * pair + side
            lanes = slice(128 * h, 128 * h + 128)
            carry = carry_scr[4 * j + h]
            wide = jnp.concatenate([carry[:64], jnp.broadcast_to(carry[64:65], (64, 128))], axis=0)
            high, low = split(wide)
            fq = fq_ref[:, lanes]
            nd = nd_ref[:, lanes] + contin * (nt(fq, high) + nt(fq, low))
            inverse = 1.0 / nd
            turned = pltpu.roll(inverse, 64, 1)
            quotient = nd * turned
            if side:
                quotients.append(pltpu.roll(quotient, 64, 1))
                inverses.append(inverse)
            else:
                quotients.append(quotient)
                inverses.append(turned)
        lanes = slice(128 * pair, 128 * pair + 128)
        mf = jnp.where(low_half, *quotients)
        mf_ref[:, lanes] = mf
        mixed_ref[:, lanes] = mf.astype(BF16)
        rden_ref[:, lanes] = jnp.where(low_half, *inverses)
    hidden_ref[...] += mm(mixed_ref[...], wo_ref[...])

    @pl.when(j == pl.num_programs(0) - 1)
    def _():
        normed, _ = moments(hidden_ref[...])
        mlp_ref[...] = (normed * gain_ref[...]).astype(BF16)


GELU_A, GELU_C = 0.044715, 0.7978845608028654


def mlp_kernel(sc, mlp_ref, cot_ref, mlp_part, cot_part, wf_ref, wp_ref,
               act_ref, gp_ref, send_fc, send_proj, mlp_t, cot_t):
    @pl.when(pl.program_id(0) == 0)
    def _():
        mlp_t[...] = jnp.transpose(mlp_part[...].astype(F32)).astype(BF16)
        cot_t[...] = jnp.transpose(cot_part[...].astype(F32)).astype(BF16)

    u = mm(mlp_ref[...], wf_ref[...])
    square = u * u
    t = jnp.tanh(GELU_C * (u + GELU_A * (u * square)))
    half = 0.5 * (1.0 + t)
    act = (u * half).astype(BF16)
    act_ref[...] = act
    slope = half + (0.5 * GELU_C) * u * (1.0 - t * t) * (1.0 + (3.0 * GELU_A) * square)
    gp = (nt(cot_ref[...], wp_ref[...]) * slope).astype(BF16)
    gp_ref[...] = gp
    send_fc[...] = mm(mlp_t[...], gp)
    send_proj[...] = mm(cot_t[...], act)


def mlp_out_kernel(sc, act_ref, gp_ref, wf_ref, wp_ref, hidden_ref, cot_ref, gain_ref,
                   out_ref, gh_ref, gh_low_ref, gg_ref, back_scr):
    j = pl.program_id(0)

    @pl.when(j == 0)
    def _():
        out_ref[...] = hidden_ref[...]
        back_scr[...] = jnp.zeros(back_scr.shape, F32)

    out_ref[...] += mm(act_ref[...], wp_ref[...])
    back_scr[...] += nt(gp_ref[...], wf_ref[...])

    @pl.when(j == pl.num_programs(0) - 1)
    def _():
        normed, scale = moments(hidden_ref[...])
        grad = back_scr[...]
        gg_ref[...] = jnp.sum(grad * normed, axis=0, keepdims=True)
        gh = cot_ref[...].astype(F32) + norm_back(grad, normed, scale, gain_ref[...])
        gh_ref[...] = gh
        gh_low_ref[...] = gh.astype(BF16)


def numer_back_kernel(sc, gh_ref, wo_ref, mf_ref, rden_ref, fq_ref, contin_ref,
                      gn_ref, gd_ref, gd_t_ref, p0, p1, p2, p3, state_scr):
    j = pl.program_id(0)
    gm = nt(gh_ref[...], wo_ref[...]) * rden_ref[...]
    gn_ref[...] = gm.astype(BF16)
    gd = -segment_sum(gm * mf_ref[...], segment_ones(256))
    gd_ref[...] = gd
    gn_t = jnp.transpose(gm).astype(BF16)
    gd_t = jnp.transpose(gd)
    contin = contin_ref[...]
    for h in range(4):
        rows = gd_t[64 * h : 64 * h + 8]
        gd_t_ref[8 * h : 8 * h + 8, :] = rows
        kept = (fq_ref[:, 128 * h : 128 * h + 128].astype(F32) * contin).astype(BF16)
        state_scr[4 * j + h, 0:64, :] = mm(gn_t[64 * h : 64 * h + 64], kept)
        high, low = split(rows)
        both = jnp.concatenate([high.astype(F32), low.astype(F32)], axis=0).astype(BF16)
        sums = mm(both, kept)
        state_scr[4 * j + h, 64:72, :] = sums[0:8] + sums[8:16]

    @pl.when(j == pl.num_programs(0) - 1)
    def _():
        for k, piece in enumerate((p0, p1, p2, p3)):
            n = piece.shape[0]
            piece[...] = state_scr[pl.ds((sc[MEMBER] ^ k) * n, n)]


def side_rows(state, side):
    zeros = jnp.zeros((64, 128), F32)
    rows = state[:64]
    return jnp.concatenate([zeros, rows] if side else [rows, zeros], axis=0)


def scores_back_kernel(sc, q_ref, fq_ref, fk_ref, v_ref, gn_ref, gd_ref, gd_t_ref,
                       c0, c1, c2, c3, allow_ref, allow_t_ref, contin_ref, map_ref,
                       gq_ref, gfk_ref, gv_ref, gmap_ref, map_scr, carry_scr, d_scr):
    j = pl.program_id(0)
    tokens = q_ref.shape[0]
    half = tokens // 2

    @pl.when(j == 0)
    def _():
        place_heads(sc, carry_scr, (c0, c1, c2, c3))

    fill_maps(map_scr, map_ref)
    ones = segment_ones(128)
    low_half = iota((tokens, 128), 1) < 64
    contin = contin_ref[...]
    for pair in range(2):
        pair_lanes = slice(128 * pair, 128 * pair + 128)
        v_pair = v_ref[:, pair_lanes]
        gn_pair = gn_ref[:, pair_lanes].astype(F32)
        gd_pair = gd_ref[:, pair_lanes]
        gd_turned = pltpu.roll(gd_pair, 64, 1)
        gv_parts = []
        for side in range(2):
            h = 2 * pair + side
            lanes = slice(128 * h, 128 * h + 128)
            mine = ~low_half if side else low_half
            gn = jnp.where(mine, gn_pair, 0.0).astype(BF16)
            gd = jnp.where(mine, gd_pair, gd_turned)
            gd_row = gd_t_ref[8 * h : 8 * h + 1, :]
            fq, fk = fq_ref[:, lanes], fk_ref[:, lanes]
            gd_few = jnp.concatenate([gd] * (half // 128), axis=1)
            gd_many = jnp.concatenate([gd] * (tokens // 128), axis=1)
            g_top = ((nt(gn[:half], v_pair[:half]) + gd_few[:half]) * allow_ref[:half, :half]).astype(BF16)
            g_bot = ((nt(gn[half:], v_pair) + gd_many[half:]) * allow_ref[half:, :]).astype(BF16)
            carry = carry_scr[4 * j + h]
            high, low = split(side_rows(carry, side))
            inter = mm(gn, high) + mm(gn, low) + gd * carry[64:65]
            gfq = jnp.concatenate([mm(g_top, fk[:half]), mm(g_bot, fk)], axis=0) + contin * inter
            d_scr[:, lanes] = features_back(fq.astype(F32), gfq, ones).astype(BF16)

            at_top, at_bot = allow_t_ref[:half, :], allow_t_ref[half:, half:]
            gt_top = ((nt(v_pair[:half], gn) + gd_row) * at_top).astype(BF16)
            gt_bot = ((nt(v_pair[half:], gn[half:]) + gd_row[:, half:]) * at_bot).astype(BF16)
            gfk_ref[:half, lanes] = mm(gt_top, fq)
            gfk_ref[half:, lanes] = mm(gt_bot, fq[half:])
            st_top = (nt(fk[:half], fq) * at_top).astype(BF16)
            st_bot = (nt(fk[half:], fq[half:]) * at_bot).astype(BF16)
            gv_parts.append(jnp.concatenate([mm(st_top, gn), mm(st_bot, gn[half:])], axis=0))
        gv_ref[:, pair_lanes] = gv_parts[0] + gv_parts[1]
    d = d_scr[...]
    gq_ref[...] = (0.5 * nt(d, map_scr[...])).astype(BF16)
    gm = tn(q_ref[...], d)
    for h in range(4):
        gmap_ref[64 * h : 64 * h + 64, :] = gm[64 * h : 64 * h + 64, 128 * h : 128 * h + 128]


def keys_back_kernel(sc, k_ref, fk_ref, v_ref, gfk_ref, gv_ref, u0, u1, u2, u3, tail_ref, map_ref,
                     gk_ref, gvb_ref, gmap_ref, map_scr, up_scr, d_scr):
    j = pl.program_id(0)

    @pl.when(j == 0)
    def _():
        place_heads(sc, up_scr, (u0, u1, u2, u3))

    fill_maps(map_scr, map_ref)
    ones = segment_ones(128)
    tail = tail_ref[...]
    for pair in range(2):
        pair_lanes = slice(128 * pair, 128 * pair + 128)
        v_pair = v_ref[:, pair_lanes]
        gv = gv_ref[:, pair_lanes]
        for side in range(2):
            h = 2 * pair + side
            lanes = slice(128 * h, 128 * h + 128)
            up = up_scr[4 * j + h]
            high, low = split(side_rows(up, side))
            fk = fk_ref[:, lanes]
            key_term = mm(v_pair, high) + mm(v_pair, low) + up[64:65]
            gfk = gfk_ref[:, lanes] + tail * key_term
            gv = gv + tail * (nt(fk, high) + nt(fk, low))
            d_scr[:, lanes] = features_back(fk.astype(F32), gfk, ones).astype(BF16)
        gvb_ref[:, pair_lanes] = gv.astype(BF16)
    d = d_scr[...]
    gk_ref[...] = (0.5 * nt(d, map_scr[...])).astype(BF16)
    gm = tn(k_ref[...], d)
    for h in range(4):
        gmap_ref[64 * h : 64 * h + 64, :] = gm[64 * h : 64 * h + 64, 128 * h : 128 * h + 128]


def inputs_back_kernel(sc, gq_ref, gk_ref, gv_ref, w_ref, x_ref, gh_ref, gain_ref, gg_mlp_ref,
                       gmq_ref, gmk_ref, gx_ref, keep_ref, send_ref, acc, pack):
    j = pl.program_id(0)

    @pl.when(j == 0)
    def _():
        acc[...] = nt(gq_ref[...], w_ref[...])
        rows = gmq_ref.shape[0]
        low_half = iota(gmq_ref.shape, 1) < 64
        pack[:rows, :] = jnp.where(low_half, gmq_ref[...], pltpu.roll(gmk_ref[...], 64, 1))
        pack[rows:, :] = jnp.zeros((pack.shape[0] - rows, 128), F32)

    @pl.when(j == 1)
    def _():
        acc[...] += nt(gk_ref[...], w_ref[...])

    @pl.when(j == 2)
    def _():
        grad = acc[...] + nt(gv_ref[...], w_ref[...])
        normed, scale = moments(x_ref[...].astype(F32))
        gx_ref[...] = gh_ref[...] + norm_back(grad, normed, scale, gain_ref[...])
        gg = jnp.sum(grad * normed, axis=0, keepdims=True)
        rows = gmq_ref.shape[0]
        n = gg.shape[1] // 128
        for i in range(n):
            pack[rows + i : rows + i + 1, :] = gg[:, 128 * i : 128 * i + 128]
            pack[rows + n + i : rows + n + i + 1, :] = gg_mlp_ref[:, 128 * i : 128 * i + 128]
        size = keep_ref.shape[0]
        keep_ref[...] = pack[pl.ds(pl.multiple_of(sc[CORE] * size, 8), size), :]
        send_ref[...] = pack[pl.ds(pl.multiple_of((1 - sc[CORE]) * size, 8), size), :]


def add_kernel(sc, a_ref, b_ref, out_ref):
    out_ref[...] = a_ref[...] + b_ref[...]


def unpack_kernel(sc, mine_ref, other_ref, gmq_ref, gmk_ref, gains_ref, pack):
    size = mine_ref.shape[0]
    pack[pl.ds(pl.multiple_of(sc[CORE] * size, 8), size), :] = mine_ref[...]
    pack[pl.ds(pl.multiple_of((1 - sc[CORE]) * size, 8), size), :] = other_ref[...]
    heads = gmq_ref.shape[0]
    for h in range(heads):
        both = pack[64 * h : 64 * h + 64, :]
        gmq_ref[h] = both[:, :64]
        gmk_ref[h] = both[:, 64:]
    gains_ref[...] = pack[64 * heads :, :]


def send_half_kernel(sc, x_ref, y_ref, out_ref, x_t):
    @pl.when(pl.program_id(0) == 0)
    def _():
        x_t[...] = jnp.transpose(x_ref[...].astype(F32)).astype(BF16)

    out_ref[...] = mm(x_t[...], y_ref[...])


ORDERS = ((0, 1, 2, 3), (1, 0, 2, 3), (2, 3, 0, 1))


def keep_half_kernel(tiles, sc, x_ref, y_ref, r_ref, *rest):
    outs, (x_t, scr) = rest[:6], rest[6:]
    i = pl.program_id(0)

    @pl.when(i == 0)
    def _():
        x_t[...] = jnp.transpose(x_ref[...].astype(F32)).astype(BF16)

    value = mm(x_t[...], y_ref[...]) + r_ref[...]
    rows = value.shape[0] // 16
    half = value.shape[0] // 2
    lo = 0
    for kind, order in enumerate(ORDERS):

        @pl.when((i >= lo) & (i < lo + tiles[kind]))
        def _():
            for g in range(16):
                place = g ^ sc[SEQ]
                spot = 0
                for depth, bit in enumerate(order):
                    spot = spot + (((place >> bit) & 1) << (3 - depth))
                scr[pl.ds(pl.multiple_of(spot * rows, 8), rows), :] = value[rows * g : rows * g + rows]
            outs[2 * kind][...] = scr[half:, :]
            outs[2 * kind + 1][...] = scr[:half, :]

        lo += tiles[kind]


def fold_kernel(plan, sc, *refs):
    n_in = 2 * sum(n for n, _ in plan)
    ins, outs = refs[:n_in], list(refs[n_in:])
    at = 0
    for n, final in plan:
        targets = [outs.pop(0)] if final else [outs.pop(0), outs.pop(0)]
        lane = 0
        for _ in range(n):
            total = ins[at][...] + ins[at + 1][...]
            at += 2
            width = total.shape[1]
            if final:
                targets[0][:, lane : lane + width] = total
            else:
                half = total.shape[0] // 2
                targets[0][:, lane : lane + width] = total[half:]
                targets[1][:, lane : lane + width] = total[:half]
            lane += width


def core_hop(v):
    return lax.ppermute(v, "batch", [(0, 1), (1, 0)])


def local(inputs, w_qkv, w_out, w_fc, w_proj, map_query, map_key, gain_attn, gain_mlp,
          starts, key_mask, cotangent):
    T, D = inputs.shape[1], inputs.shape[2]
    H = map_query.shape[0]
    FF = w_fc.shape[1]
    n_seq = lax.axis_size("seq")
    planes = n_seq // 4
    quads = H // 4
    QW, FW = 4 * 64, 4 * 128
    half_rows = D // 2
    per = H // 4
    core = lax.axis_index("batch").astype(jnp.int32)
    seq = lax.axis_index("seq").astype(jnp.int32)
    scal = jnp.concatenate(
        [jnp.stack([core, seq, seq & 3, seq >> 2]), starts[0].astype(jnp.int32)]
    )
    tok = jnp.zeros((8, 128), F32)
    x, cot = inputs[0], cotangent[0]
    gain_a, gain_m = gain_attn.reshape(1, D), gain_mlp.reshape(1, D)

    def hop(v, bit):
        return lax.ppermute(v, "seq", [(i, i ^ (1 << bit)) for i in range(n_seq)])

    def to_member(v, k):
        return lax.ppermute(v, "seq", [(i, i ^ k) for i in range(n_seq)])

    def shift(v, by):
        return lax.ppermute(v, "seq", [(i, (i + by) % n_seq) for i in range(n_seq)])

    qcol = pl.BlockSpec((T, QW), lambda j, _: (0, j))
    fcol = pl.BlockSpec((T, FW), lambda j, _: (0, j))
    col128 = whole((T, 128))
    square = whole((T, T))
    full = whole((T, D))
    row = whole((1, D))
    maps = pl.BlockSpec((4, 64, 64), lambda j, _: (j, 0, 0))
    piece = (per, STATE_ROWS, 128)
    piece_spec = whole(piece)
    map_scr = pltpu.VMEM((QW, FW), BF16)
    state_scr = pltpu.VMEM((H, STATE_ROWS, 128), F32)

    def w_cols(part):
        return pl.BlockSpec((D, QW), lambda j, _: (0, part * quads + j))

    (attn, k, v, fk, s0, s1, s2, s3, allow, allow_t, tail, contin), tok = run(
        keys_kernel, scal, tok, (quads,),
        [(x, full), (gain_a, row), (w_qkv, w_cols(1)), (w_qkv, w_cols(2)), (map_key, maps),
         (key_mask, whole((1, T)))],
        [((T, D), BF16, full), ((T, D), BF16, qcol), ((T, D), BF16, qcol), ((T, 2 * D), BF16, fcol)]
        + [(piece, F32, piece_spec)] * 4
        + [((T, T), F32, square)] * 2 + [((T, 128), F32, col128)] * 2,
        [map_scr, state_scr],
    )

    def plane_exchange(pieces):
        return [pieces[0]] + [to_member(pieces[k], k) for k in range(1, 4)]

    def plane_total(own, tok):
        (total,), tok = run(
            plane_sum_kernel, scal, tok, (1,), [(p, piece_spec) for p in own],
            [(piece, F32, piece_spec)])
        return total, tok

    def across(total, backward):
        if planes <= 4:
            return [shift(total, (-4 if backward else 4) * i) for i in range(1, planes)]
        every = lax.all_gather(total, "seq").reshape((planes, 4) + piece)
        mine = lax.dynamic_index_in_dim(every, seq & 3, 1, keepdims=False)
        place = jnp.arange(planes)
        want = place > (seq >> 2) if backward else place < (seq >> 2)
        return [jnp.sum(jnp.where(want[:, None, None, None], mine, 0.0), axis=0)]

    def scanned(own, others, backward, tok):
        return run(
            functools.partial(scan_kernel, backward, planes if planes <= 4 else None), scal, tok, (1,),
            [(p, piece_spec) for p in own + others], [(piece, F32, piece_spec)] * 4)

    own = plane_exchange([s0, s1, s2, s3])

    (q, fq, nd), tok = run(
        queries_kernel, scal, tok, (quads,),
        [(attn, full), (w_qkv, w_cols(0)), (map_query, maps), (fk, fcol), (v, qcol), (allow, square)],
        [((T, D), BF16, qcol), ((T, 2 * D), BF16, fcol), ((T, 2 * D), F32, fcol)],
        [map_scr],
    )
    total, tok = plane_total(own, tok)
    others = across(total, False)
    carried, tok = scanned(own, others, False, tok)
    carry = plane_exchange(carried)

    (mixed, mf, rden, hidden, mlp_in), tok = run(
        mix_kernel, scal, tok, (quads,),
        [(x, full), (nd, fcol), (fq, fcol)] + [(c, piece_spec) for c in carry]
        + [(contin, col128), (w_out, pl.BlockSpec((QW, D), lambda j, _: (j, 0))), (gain_m, row)],
        [((T, D), BF16, qcol), ((T, D), F32, qcol), ((T, D), F32, qcol), ((T, D), F32, full),
         ((T, D), BF16, full)],
        [state_scr],
    )

    other_half = pl.BlockSpec((T, half_rows), lambda j, sc: (0, 1 - sc[CORE]))
    this_half = pl.BlockSpec((T, half_rows), lambda j, sc: (0, sc[CORE]))
    half_scr = pltpu.VMEM((half_rows, T), BF16)
    FT = 256
    (act, gp, send_fc, send_proj), tok = run(
        mlp_kernel, scal, tok, (FF // FT,),
        [(mlp_in, full), (cot, full), (mlp_in, other_half), (cot, other_half),
         (w_fc, columns(D, FT)), (w_proj, pl.BlockSpec((FT, D), lambda j, _: (j, 0)))],
        [((T, FF), BF16, columns(T, FT))] * 2 + [((half_rows, FF), F32, columns(half_rows, FT))] * 2,
        [half_scr, half_scr],
    )
    FT = 512
    (output, gh, gh_low, gg_mlp), tok = run(
        mlp_out_kernel, scal, tok, (FF // FT,),
        [(act, columns(T, FT)), (gp, columns(T, FT)), (w_fc, columns(D, FT)),
         (w_proj, pl.BlockSpec((FT, D), lambda j, _: (j, 0))), (hidden, full), (cot, full), (gain_m, row)],
        [((T, D), F32, full), ((T, D), F32, full), ((T, D), BF16, full), ((1, D), F32, row)],
        [pltpu.VMEM((T, D), F32)],
    )
    (gn, gd, gd_t, s0, s1, s2, s3), tok = run(
        numer_back_kernel, scal, tok, (quads,),
        [(gh_low, full), (w_out, pl.BlockSpec((QW, D), lambda j, _: (j, 0))), (mf, qcol), (rden, qcol),
         (fq, fcol), (contin, col128)],
        [((T, D), BF16, qcol), ((T, D), F32, qcol),
         ((8 * H, T), F32, pl.BlockSpec((32, T), lambda j, _: (j, 0)))] + [(piece, F32, piece_spec)] * 4,
        [state_scr],
    )
    own = plane_exchange([s0, s1, s2, s3])

    direct = n_seq == 16

    def send_half(xs, ys, tok):
        if not direct:
            return None, tok
        width = ys.shape[1]
        (out,), tok = run(
            send_half_kernel, scal, tok, (width // 256,), [(xs, other_half), (ys, columns(T, 256))],
            [((half_rows, width), F32, columns(half_rows, 256))], [half_scr])
        return core_hop(out), tok

    def keep_half(xs, ys, received, widths, tile, tok):
        tiles = tuple(w // tile for w in widths)
        out_specs = []
        lo = 0
        for kind in range(3):
            def place(i, _, lo=lo, n=tiles[kind]):
                return (0, jnp.clip(i - lo, 0, n - 1))
            out_specs += [((half_rows // 2, widths[kind]), F32, pl.BlockSpec((half_rows // 2, tile), place))] * 2
            lo += tiles[kind]
        return run(
            functools.partial(keep_half_kernel, tiles), scal, tok, (sum(tiles),),
            [(xs, this_half), (ys, columns(T, tile)), (received, columns(half_rows, tile))],
            out_specs, [half_scr, pltpu.VMEM((half_rows, tile), F32)])

    def fold(plan, pairs, tok):
        ins, outs = [], []
        at = 0
        for n, final in plan:
            width = sum(pairs[at + i][0].shape[1] for i in range(n))
            rows = pairs[at][0].shape[0]
            for i in range(n):
                ins += [(a, whole(a.shape)) for a in pairs[at + i]]
            at += n
            if final:
                outs.append(((rows, width), F32, whole((rows, width))))
            else:
                outs += [((rows // 2, width), F32, whole((rows // 2, width)))] * 2
        return run(functools.partial(fold_kernel, plan), scal, tok, (1,), ins, outs)

    class Reduction:
        def __init__(self, parts):
            sa, self.ka, sb, self.kb, sc_, self.kc = parts
            self.ra, self.rb, self.rc = hop(sa, 0), hop(sb, 1), hop(sc_, 2)
            self.stage = 0

        def step(self, tok):
            if self.stage == 0:
                (sa, self.ka, sb, self.kb, s3_, self.kc), tok = fold(
                    ((1, False),) * 3, [(self.ka, self.ra), (self.kb, self.rb), (self.kc, self.rc)], tok)
                self.ra, self.rb, self.rc = hop(sa, 1), hop(sb, 0), hop(s3_, 3)
            elif self.stage == 1:
                (s, self.k, s3_, self.kc), tok = fold(
                    ((2, False), (1, False)), [(self.ka, self.ra), (self.kb, self.rb), (self.kc, self.rc)], tok)
                self.r, self.rc = hop(s, 2), hop(s3_, 0)
            elif self.stage == 2:
                (s, self.k, s3_, self.kc), tok = fold(
                    ((1, False), (1, False)), [(self.k, self.r), (self.kc, self.rc)], tok)
                self.r, self.rc = hop(s, 3), hop(s3_, 1)
            else:
                (self.result,), tok = fold(((2, True),), [(self.k, self.r), (self.kc, self.rc)], tok)
            self.stage += 1
            return tok

    if direct:
        recv_proj, recv_fc = core_hop(send_proj), core_hop(send_fc)
        recv_out, tok = send_half(mixed, gh_low, tok)
        parts, tok = keep_half(cot, act, recv_proj, (1152, 1152, 768), 384, tok)
        red_proj = Reduction(parts)
        parts, tok = keep_half(mlp_in, gp, recv_fc, (1152, 1152, 768), 384, tok)
        red_fc = Reduction(parts)

    total, tok = plane_total(own, tok)
    others = across(total, True)

    (gq, gfk, gv_f, gmq), tok = run(
        scores_back_kernel, scal, tok, (quads,),
        [(q, qcol), (fq, fcol), (fk, fcol), (v, qcol), (gn, qcol), (gd, qcol),
         (gd_t, pl.BlockSpec((32, T), lambda j, _: (j, 0)))] + [(c, piece_spec) for c in carry]
        + [(allow, square), (allow_t, square), (contin, col128), (map_query, maps)],
        [((T, D), BF16, qcol), ((T, 2 * D), F32, fcol), ((T, D), F32, qcol),
         ((D, 128), F32, pl.BlockSpec((QW, 128), lambda j, _: (j, 0)))],
        [map_scr, state_scr, pltpu.VMEM((T, FW), BF16)],
    )
    carried, tok = scanned(own, others, True, tok)
    upstream = plane_exchange(carried)

    if direct:
        recv_q, tok = send_half(attn, gq, tok)
        tok = red_proj.step(tok)
        parts, tok = keep_half(mixed, gh_low, recv_out, (256, 256, 256), 256, tok)
        red_out = Reduction(parts)

    (gk, gv, gmk), tok = run(
        keys_back_kernel, scal, tok, (quads,),
        [(k, qcol), (fk, fcol), (v, qcol), (gfk, fcol), (gv_f, qcol)] + [(c, piece_spec) for c in upstream]
        + [(tail, col128), (map_key, maps)],
        [((T, D), BF16, qcol), ((T, D), BF16, qcol),
         ((D, 128), F32, pl.BlockSpec((QW, 128), lambda j, _: (j, 0)))],
        [map_scr, state_scr, pltpu.VMEM((T, FW), BF16)],
    )
    if direct:
        recv_k, tok = send_half(attn, gk, tok)
        recv_v, tok = send_half(attn, gv, tok)

    small = D + 16
    small_half = small // 2
    small_spec = whole((small_half, 128))
    (gx, keep, send), tok = run(
        inputs_back_kernel, scal, tok, (3,),
        [(gq, full), (gk, full), (gv, full), (w_qkv, columns(D, D)), (x, full), (gh, full), (gain_a, row),
         (gg_mlp, row), (gmq, whole((D, 128))), (gmk, whole((D, 128)))],
        [((T, D), F32, full)] + [((small_half, 128), F32, small_spec)] * 2,
        [pltpu.VMEM((T, D), F32), pltpu.VMEM((small, 128), F32)],
    )

    def add(a, b, tok):
        (out,), tok = run(add_kernel, scal, tok, (1,), [(a, small_spec), (b, small_spec)],
                          [((small_half, 128), F32, small_spec)])
        return out, tok

    got = core_hop(send)
    if direct:
        parts, tok = keep_half(attn, gq, recv_q, (256, 256, 256), 256, tok)
        red_q = Reduction(parts)
        parts, tok = keep_half(attn, gk, recv_k, (256, 256, 256), 256, tok)
        red_k = Reduction(parts)
        parts, tok = keep_half(attn, gv, recv_v, (256, 256, 256), 256, tok)
        red_v = Reduction(parts)
        mine, tok = add(keep, got, tok)
        got = hop(mine, 0)
        tok = red_fc.step(tok)
        mine, tok = add(mine, got, tok)
        got = hop(mine, 1)
        tok = red_proj.step(tok)
        tok = red_out.step(tok)
        tok = red_q.step(tok)
        tok = red_k.step(tok)
        tok = red_v.step(tok)
        mine, tok = add(mine, got, tok)
        got = hop(mine, 2)
        tok = red_fc.step(tok)
        tok = red_proj.step(tok)
        tok = red_out.step(tok)
        tok = red_q.step(tok)
        tok = red_k.step(tok)
        tok = red_v.step(tok)
        mine, tok = add(mine, got, tok)
        got = hop(mine, 3)
        tok = red_fc.step(tok)
        tok = red_proj.step(tok)
        tok = red_out.step(tok)
        tok = red_q.step(tok)
        tok = red_k.step(tok)
        tok = red_v.step(tok)
        mine, tok = add(mine, got, tok)
        got = core_hop(mine)
        tok = red_fc.step(tok)
        tok = red_out.step(tok)
        tok = red_q.step(tok)
        tok = red_k.step(tok)
        tok = red_v.step(tok)
        grad_w_qkv = jnp.concatenate([red_q.result, red_k.result, red_v.result], axis=1)
        grad_w_out, grad_w_fc = red_out.result, red_fc.result
        grad_proj_rows = red_proj.result
    else:
        mine, tok = add(keep, got, tok)
        mine = lax.psum(mine, "seq")
        got = core_hop(mine)
        summed = lax.psum_scatter(
            jnp.concatenate(
                [tn(attn, gq), tn(attn, gk), tn(attn, gv), tn(mixed, gh_low), tn(mlp_in, gp), tn(cot, act)],
                axis=1,
            ),
            ("batch", "seq"), scatter_dimension=0, tiled=True)
        grad_w_qkv = summed[:, : 3 * D]
        grad_w_out = summed[:, 3 * D : 4 * D]
        grad_w_fc = summed[:, 4 * D : 4 * D + FF]
        grad_proj_rows = summed[:, 4 * D + FF :]

    heads_shape = (H, 64, 64)
    (grad_map_query, grad_map_key, gains), tok = run(
        unpack_kernel, scal, tok, (1,), [(mine, small_spec), (got, small_spec)],
        [(heads_shape, F32, whole(heads_shape))] * 2 + [((16, 128), F32, whole((16, 128)))],
        [pltpu.VMEM((small, 128), F32)])
    n = D // 128
    return (
        output[None],
        gx[None],
        grad_w_qkv,
        grad_w_out,
        grad_w_fc,
        grad_proj_rows.T,
        grad_map_query,
        grad_map_key,
        gains[:n].reshape(D),
        gains[n : 2 * n].reshape(D),
    )


def solution(mesh):
    tokens = P("batch", "seq", None)
    flags = P("batch", "seq")
    rows = P(("batch", "seq"), None)
    return jax.shard_map(
        local,
        mesh=mesh,
        in_specs=(tokens,) + (P(),) * 8 + (flags, flags, tokens),
        out_specs=(tokens, tokens, rows, rows, rows, P(None, ("batch", "seq")), P(), P(), P(), P()),
        check_vma=False,
    )
```

```python
import functools

import jax
import jax.numpy as jnp
from jax import lax
from jax.experimental import pallas as pl
from jax.experimental.pallas import tpu as pltpu
from jax.sharding import PartitionSpec as P

EPSILON = 1e-05
F32 = jnp.float32
BF16 = jnp.bfloat16
STATE_ROWS = 72
SMALL_ROWS = 72
MIB = 1024 * 1024


def mm(a, b):
    return lax.dot_general(a, b, (((1,), (0,)), ((), ())), preferred_element_type=F32)


def nt(a, b):
    return lax.dot_general(a, b, (((1,), (1,)), ((), ())), preferred_element_type=F32)


def tn(a, b):
    return lax.dot_general(a, b, (((0,), (0,)), ((), ())), preferred_element_type=F32)


def split(v):
    high = v.astype(BF16)
    return high, (v - high.astype(F32)).astype(BF16)


def iota(shape, dim):
    return lax.broadcasted_iota(jnp.int32, shape, dim)


def segment_ones(width):
    shape = (width, width)
    return (iota(shape, 0) // 64 == iota(shape, 1) // 64).astype(BF16)


def segment_sum(v, ones):
    high, low = split(v)
    return mm(high, ones) + mm(low, ones)


def moments(x):
    centre = jnp.mean(x, axis=-1, keepdims=True)
    offsets = x - centre
    variance = jnp.mean(offsets * offsets, axis=-1, keepdims=True)
    scale = lax.rsqrt(variance + EPSILON)
    return offsets * scale, scale


def norm_back(grad, normed, scale, gain):
    dn = grad * gain
    first = jnp.mean(dn, axis=-1, keepdims=True)
    second = jnp.mean(dn * normed, axis=-1, keepdims=True)
    return (dn - first - normed * second) * scale


def fill_maps(scr, map_ref):
    scr[...] = jnp.zeros(scr.shape, scr.dtype)
    for h in range(4):
        m = map_ref[h].astype(F32)
        scr[64 * h : 64 * h + 64, 128 * h : 128 * h + 128] = jnp.concatenate(
            [m, -m], axis=1
        ).astype(scr.dtype)


def features(pre, ones):
    low_half = iota(pre.shape, 1) < 64
    top = jnp.max(jnp.where(low_half, pre, -jnp.inf), axis=1, keepdims=True)
    bottom = jnp.max(jnp.where(low_half, -jnp.inf, pre), axis=1, keepdims=True)
    e = jnp.exp(pre - jnp.where(low_half, top, bottom))
    return e / segment_sum(e, ones)


def features_back(feat, grad, ones):
    weighted = feat * grad
    total = segment_sum(weighted, ones)
    mass = mm(feat.astype(BF16), ones)
    part = weighted - feat * (total / mass)
    return part - pltpu.roll(part, 64, 1)


def whole(shape):
    return pl.BlockSpec(shape, lambda *_: (0,) * len(shape))


def columns(rows, width):
    return pl.BlockSpec((rows, width), lambda j: (0, j))


ANYWHERE = pl.BlockSpec(memory_space=pl.ANY)


def my_core():
    return lax.axis_index("batch")


def my_seq():
    return lax.axis_index("seq")


def nbytes(shape, dtype):
    total = jnp.dtype(dtype).itemsize
    for n in shape:
        total *= n
    return total


class Held:
    def __init__(self, array):
        self.array, self.shape, self.dtype = array, array.shape, array.dtype


class Near(Held):
    pass


def run(kernel, tok, grid, ins, outs, scratch=(), extra=4, aliases=None, us=1.0):
    n_in, n_out = len(ins), len(outs)
    linked = tok is not None
    outs = [tuple(out) + (False,) * (4 - len(out)) for out in outs]

    def body(*refs):
        kernel(*refs[:n_in], *refs[n_in + linked : n_in + linked + n_out], *refs[n_in + linked + n_out + 1 :])

    held = 0
    arrays = []
    for array, spec in ins:
        near = isinstance(array, Near)
        if spec.block_shape is not None and not near:
            held += (1 if spec.block_shape == array.shape else 2) * nbytes(spec.block_shape, array.dtype)
        if isinstance(array, Held):
            array = pltpu.with_memory_space_constraint(array.array, pltpu.VMEM if near else pltpu.HBM)
        arrays.append(array)
    for shape, dtype, spec, stays in outs:
        if stays is not Near:
            held += (1 if spec.block_shape == shape else 2) * nbytes(spec.block_shape, dtype)
    for item in scratch:
        held += nbytes(item.shape, item.dtype)
    result = pl.pallas_call(
        body,
        grid=grid,
        in_specs=[spec for _, spec in ins] + [ANYWHERE] * linked,
        out_specs=[spec for _, _, spec, _ in outs] + [ANYWHERE],
        scratch_shapes=list(scratch),
        out_shape=[
            pltpu.VMEM(shape, dtype) if stays is Near
            else pltpu.HBM(shape, dtype) if stays else jax.ShapeDtypeStruct(shape, dtype)
            for shape, dtype, _, stays in outs
        ]
        + [jax.ShapeDtypeStruct((8, 128), F32)],
        input_output_aliases=aliases or {},
        cost_estimate=pl.CostEstimate(flops=int(us * 1.15e9), bytes_accessed=0, transcendentals=0),
        compiler_params=pltpu.CompilerParams(vmem_limit_bytes=min(held + extra * MIB, 60 * MIB)),
    )(*arrays, *([tok] if linked else []))
    results = [Near(r) if out[3] is Near else Held(r) if out[3] else r for r, out in zip(result, outs)]
    return results, result[-1]


def keys_kernel(x_ref, gain_ref, wk_ref, wv_ref, map_ref, mask_ref, starts_ref,
                attn_ref, k_ref, v_ref, fk_ref, p0, p1, p2, p3,
                allow_ref, allow_t_ref, tail_ref, contin_ref,
                map_scr, state_scr):
    j = pl.program_id(0)
    tokens = x_ref.shape[0]
    n_flags = starts_ref.shape[1]
    unit = tokens // n_flags

    def seg(shape, dim):
        place = iota(shape, dim)
        total = jnp.zeros(shape, jnp.int32)
        for u in range(n_flags):
            total = total + jnp.where(place >= unit * u, starts_ref[0, u], 0)
        return total

    @pl.when(j == 0)
    def _():
        normed, _ = moments(x_ref[...].astype(F32))
        attn_ref[...] = (normed * gain_ref[...]).astype(BF16)
        last = starts_ref[0, 0]
        for u in range(1, n_flags):
            last = last + starts_ref[0, u]
        mask_row = mask_ref[...].astype(F32)
        mask_col = jnp.transpose(jnp.broadcast_to(mask_row, (128, tokens)))
        seg_col = seg((tokens, 128), 0)
        tail_ref[...] = jnp.where(seg_col == last, mask_col, 0.0)
        contin_ref[...] = jnp.where(seg_col == 0, 1.0, 0.0)
        square = (tokens, tokens)
        same = seg(square, 0) == seg(square, 1)
        allow_ref[...] = jnp.where(same & (iota(square, 1) <= iota(square, 0)), mask_row, 0.0)
        wide_mask = jnp.concatenate([mask_col] * (tokens // 128), axis=1)
        allow_t_ref[...] = jnp.where(same & (iota(square, 0) <= iota(square, 1)), wide_mask, 0.0)

    fill_maps(map_scr, map_ref)
    attn = attn_ref[...]
    k4 = mm(attn, wk_ref[...]).astype(BF16)
    v4 = mm(attn, wv_ref[...]).astype(BF16)
    k_ref[...] = k4
    v_ref[...] = v4
    pre = mm(k4, map_scr[...])
    ones = segment_ones(128)
    v_t = jnp.transpose(v4.astype(F32)).astype(BF16)
    tail = tail_ref[...]
    row_ones = jnp.ones((16, tokens), BF16)
    for h in range(4):
        feat = features(pre[:, 128 * h : 128 * h + 128], ones).astype(BF16)
        fk_ref[:, 128 * h : 128 * h + 128] = feat
        kept = (feat.astype(F32) * tail).astype(BF16)
        state_scr[4 * j + h, 0:64, :] = mm(v_t[64 * h : 64 * h + 64], kept)
        state_scr[4 * j + h, 64:72, :] = mm(row_ones, kept)[0:8]

    @pl.when(j == pl.num_programs(0) - 1)
    def _():
        for k, piece in enumerate((p0, p1, p2, p3)):
            n = piece.shape[0]
            piece[...] = state_scr[pl.ds(((my_seq() & 3) ^ k) * n, n)]


def queries_kernel(attn_ref, wq_ref, map_ref, fk_ref, v_ref, allow_ref,
                   q_ref, fq_ref, nd_ref, map_scr):
    tokens = attn_ref.shape[0]
    half = tokens // 2
    fill_maps(map_scr, map_ref)
    q4 = mm(attn_ref[...], wq_ref[...]).astype(BF16)
    q_ref[...] = q4
    pre = mm(q4, map_scr[...])
    ones = segment_ones(128)
    low_half = iota((tokens, 128), 1) < 64
    for h in range(4):
        lanes = slice(128 * h, 128 * h + 128)
        feat = features(pre[:, lanes], ones).astype(BF16)
        fq_ref[:, lanes] = feat
        fk = fk_ref[:, lanes]
        pair = v_ref[:, 128 * (h // 2) : 128 * (h // 2) + 128].astype(F32)
        if h % 2:
            pair = pltpu.roll(pair, 64, 1)
        wide = jnp.where(low_half, pair, 1.0).astype(BF16)
        first = nt(feat[:half], fk[:half]) * allow_ref[:half, :half]
        nd_ref[:half, lanes] = mm(first.astype(BF16), wide[:half])
        second = nt(feat[half:], fk) * allow_ref[half:, :]
        nd_ref[half:, lanes] = mm(second.astype(BF16), wide)


def plane_sum_kernel(*refs):
    *pieces, out = refs
    total = pieces[0][...]
    for piece in pieces[1:]:
        total = total + piece[...]
    out[...] = total


def scan_kernel(backward, planes, *refs):
    own = refs[:4]
    others = refs[4:-4]
    outs = refs[-4:]
    member, plane = my_seq() & 3, my_seq() >> 2
    total = jnp.zeros(own[0].shape, F32)
    for i, other in enumerate(others):
        if planes is None:
            total = total + other[...]
        else:
            there = plane + i + 1 < planes if backward else plane - i - 1 >= 0
            total = total + jnp.where(there, other[...], 0.0)
    for k, out in enumerate(outs):
        value = total
        target = member ^ k
        for i, piece in enumerate(own):
            source = member ^ i
            counts = source > target if backward else source < target
            value = value + jnp.where(counts, piece[...], 0.0)
        out[...] = value


def place_heads(scr, pieces):
    for k, piece in enumerate(pieces):
        n = piece.shape[0]
        scr[pl.ds(((my_seq() & 3) ^ k) * n, n)] = piece[...]


def mix_kernel(x_ref, nd_ref, fq_ref, c0, c1, c2, c3, contin_ref, wo_ref, gain_ref,
               mixed_ref, mf_ref, rden_ref, hidden_ref, mlp_ref, carry_scr):
    j = pl.program_id(0)
    tokens = x_ref.shape[0]
    low_half = iota((tokens, 128), 1) < 64

    @pl.when(j == 0)
    def _():
        place_heads(carry_scr, (c0, c1, c2, c3))
        hidden_ref[...] = x_ref[...].astype(F32)

    contin = contin_ref[...]
    for pair in range(2):
        quotients, inverses = [], []
        for side in range(2):
            h = 2 * pair + side
            lanes = slice(128 * h, 128 * h + 128)
            carry = carry_scr[4 * j + h]
            wide = jnp.concatenate([carry[:64], jnp.broadcast_to(carry[64:65], (64, 128))], axis=0)
            high, low = split(wide)
            fq = fq_ref[:, lanes]
            nd = nd_ref[:, lanes] + contin * (nt(fq, high) + nt(fq, low))
            inverse = 1.0 / nd
            turned = pltpu.roll(inverse, 64, 1)
            quotient = nd * turned
            if side:
                quotients.append(pltpu.roll(quotient, 64, 1))
                inverses.append(inverse)
            else:
                quotients.append(quotient)
                inverses.append(turned)
        lanes = slice(128 * pair, 128 * pair + 128)
        mf = jnp.where(low_half, *quotients)
        mf_ref[:, lanes] = mf
        mixed_ref[:, lanes] = mf.astype(BF16)
        rden_ref[:, lanes] = jnp.where(low_half, *inverses)
    hidden_ref[...] += mm(mixed_ref[...], wo_ref[...])

    @pl.when(j == pl.num_programs(0) - 1)
    def _():
        normed, _ = moments(hidden_ref[...])
        mlp_ref[...] = (normed * gain_ref[...]).astype(BF16)


GELU_A, GELU_C = 0.044715, 0.7978845608028654


def turn_kernel(kinds, x_ref, out_ref, scr):
    rows, half = out_ref.shape[2] // 16, out_ref.shape[2]
    for side in range(2):
        core = my_core() if side else 1 - my_core()
        turned = jnp.transpose(
            x_ref[:, pl.ds(pl.multiple_of(core * half, 128), half)].astype(F32)
        )
        for at, kind in enumerate(kinds):
            for g in range(16):
                place = g ^ my_seq()
                spot = 0
                for depth, bit in enumerate(ORDERS[kind]):
                    spot = spot + (((place >> bit) & 1) << (3 - depth))
                scr[pl.ds(pl.multiple_of(spot * rows, 8), rows), :] = turned[rows * g : rows * g + rows]
            out_ref[side, at] = scr[...].astype(BF16)


def act_back_kernel(cot_ref, wp_ref, ga_ref):
    ga_ref[...] = nt(cot_ref[...], wp_ref[...])


def mlp_kernel(mlp_ref, ga_ref, mlp_t, cot_t, wf_ref, act_ref, gp_ref, send_ref):
    j = pl.program_id(0)
    tokens = mlp_ref.shape[0]
    step = tokens // 4
    for r in range(4):
        rows = slice(step * r, step * r + step)
        u = mm(mlp_ref[rows, :], wf_ref[...])
        square = u * u
        t = jnp.tanh(GELU_C * (u + GELU_A * (u * square)))
        half = 0.5 * (1.0 + t)
        act_ref[rows, :] = (u * half).astype(BF16)
        slope = half + (0.5 * GELU_C) * u * (1.0 - t * t) * (1.0 + (3.0 * GELU_A) * square)
        gp_ref[rows, :] = (ga_ref[rows, :] * slope).astype(BF16)
    send_ref[0, 0] = mm(cot_t[0, j % 3], act_ref[...])
    send_ref[1, 0] = mm(mlp_t[0, (j + 1) // 2], gp_ref[...])


def mlp_out_kernel(act_ref, gp_ref, wf_ref, wp_ref, part_ref, hidden_ref, cot_ref, gain_ref,
                   out_ref, gh_ref, gh_low_ref, gg_ref, back_scr):
    j = pl.program_id(0)
    out_ref[...] = part_ref[...] + mm(act_ref[...], wp_ref[...])
    back_scr[j] = nt(gp_ref[...], wf_ref[...])

    @pl.when(j == pl.num_programs(0) - 1)
    def _():
        normed, scale = moments(hidden_ref[...])
        grad = jnp.concatenate([back_scr[i] for i in range(back_scr.shape[0])], axis=1)
        gg_ref[...] = jnp.sum(grad * normed, axis=0, keepdims=True)
        gh = cot_ref[...].astype(F32) + norm_back(grad, normed, scale, gain_ref[...])
        gh_ref[...] = gh
        gh_low_ref[...] = gh.astype(BF16)


def numer_back_kernel(gh_ref, wo_ref, mf_ref, rden_ref, fq_ref, contin_ref,
                      gn_ref, gd_ref, gd_t_ref, p0, p1, p2, p3, state_scr):
    j = pl.program_id(0)
    gm = nt(gh_ref[...], wo_ref[...]) * rden_ref[...]
    gn_ref[...] = gm.astype(BF16)
    gd = -segment_sum(gm * mf_ref[...], segment_ones(256))
    gd_ref[...] = gd
    gn_t = jnp.transpose(gm).astype(BF16)
    gd_t = jnp.transpose(gd)
    contin = contin_ref[...]
    for h in range(4):
        rows = gd_t[64 * h : 64 * h + 8]
        gd_t_ref[8 * h : 8 * h + 8, :] = rows
        kept = (fq_ref[:, 128 * h : 128 * h + 128].astype(F32) * contin).astype(BF16)
        state_scr[4 * j + h, 0:64, :] = mm(gn_t[64 * h : 64 * h + 64], kept)
        high, low = split(rows)
        both = jnp.concatenate([high.astype(F32), low.astype(F32)], axis=0).astype(BF16)
        sums = mm(both, kept)
        state_scr[4 * j + h, 64:72, :] = sums[0:8] + sums[8:16]

    @pl.when(j == pl.num_programs(0) - 1)
    def _():
        for k, piece in enumerate((p0, p1, p2, p3)):
            n = piece.shape[0]
            piece[...] = state_scr[pl.ds(((my_seq() & 3) ^ k) * n, n)]


def side_rows(state, side):
    zeros = jnp.zeros((64, 128), F32)
    rows = state[:64]
    return jnp.concatenate([zeros, rows] if side else [rows, zeros], axis=0)


def scores_back_kernel(j, q_ref, fq_ref, fk_ref, v_ref, gn_ref, gd_ref, gd_t_ref,
                       c0, c1, c2, c3, allow_ref, allow_t_ref, contin_ref, map_ref, *rest):
    gq_ref, gfk_ref, gv_ref, gmap_ref, map_scr, carry_scr, d_scr = rest[-7:]
    tokens = q_ref.shape[0]
    half = tokens // 2
    place_heads(carry_scr, (c0, c1, c2, c3))

    fill_maps(map_scr, map_ref)
    ones = segment_ones(128)
    low_half = iota((tokens, 128), 1) < 64
    contin = contin_ref[...]
    for pair in range(2):
        pair_lanes = slice(128 * pair, 128 * pair + 128)
        v_pair = v_ref[:, pair_lanes]
        gn_pair = gn_ref[:, pair_lanes].astype(F32)
        gd_pair = gd_ref[:, pair_lanes]
        gd_turned = pltpu.roll(gd_pair, 64, 1)
        gv_parts = []
        for side in range(2):
            h = 2 * pair + side
            lanes = slice(128 * h, 128 * h + 128)
            mine = ~low_half if side else low_half
            gn = jnp.where(mine, gn_pair, 0.0).astype(BF16)
            gd = jnp.where(mine, gd_pair, gd_turned)
            gd_row = gd_t_ref[8 * h : 8 * h + 1, :]
            fq, fk = fq_ref[:, lanes], fk_ref[:, lanes]
            gd_few = jnp.concatenate([gd] * (half // 128), axis=1)
            gd_many = jnp.concatenate([gd] * (tokens // 128), axis=1)
            g_top = ((nt(gn[:half], v_pair[:half]) + gd_few[:half]) * allow_ref[:half, :half]).astype(BF16)
            g_bot = ((nt(gn[half:], v_pair) + gd_many[half:]) * allow_ref[half:, :]).astype(BF16)
            carry = carry_scr[4 * j + h]
            high, low = split(side_rows(carry, side))
            inter = mm(gn, high) + mm(gn, low) + gd * carry[64:65]
            gfq = jnp.concatenate([mm(g_top, fk[:half]), mm(g_bot, fk)], axis=0) + contin * inter
            d_scr[:, lanes] = features_back(fq.astype(F32), gfq, ones).astype(BF16)

            at_top, at_bot = allow_t_ref[:half, :], allow_t_ref[half:, half:]
            gt_top = ((nt(v_pair[:half], gn) + gd_row) * at_top).astype(BF16)
            gt_bot = ((nt(v_pair[half:], gn[half:]) + gd_row[:, half:]) * at_bot).astype(BF16)
            gfk_ref[:half, lanes] = mm(gt_top, fq)
            gfk_ref[half:, lanes] = mm(gt_bot, fq[half:])
            st_top = (nt(fk[:half], fq) * at_top).astype(BF16)
            st_bot = (nt(fk[half:], fq[half:]) * at_bot).astype(BF16)
            gv_parts.append(jnp.concatenate([mm(st_top, gn), mm(st_bot, gn[half:])], axis=0))
        gv_ref[:, pair_lanes] = gv_parts[0] + gv_parts[1]
    d = d_scr[...]
    gq_ref[...] = (0.5 * nt(d, map_scr[...])).astype(BF16)
    gm = tn(q_ref[...], d)
    for h in range(4):
        gmap_ref[64 * h : 64 * h + 64, :] = gm[64 * h : 64 * h + 64, 128 * h : 128 * h + 128]


def keys_back_kernel(k_ref, fk_ref, v_ref, gfk_ref, gv_ref, u0, u1, u2, u3, tail_ref, map_ref,
                     gk_ref, gvb_ref, gmap_ref, map_scr, up_scr, d_scr):
    j = pl.program_id(0)

    @pl.when(j == 0)
    def _():
        place_heads(up_scr, (u0, u1, u2, u3))

    fill_maps(map_scr, map_ref)
    ones = segment_ones(128)
    tail = tail_ref[...]
    for pair in range(2):
        pair_lanes = slice(128 * pair, 128 * pair + 128)
        v_pair = v_ref[:, pair_lanes]
        gv = gv_ref[:, pair_lanes]
        for side in range(2):
            h = 2 * pair + side
            lanes = slice(128 * h, 128 * h + 128)
            up = up_scr[4 * j + h]
            high, low = split(side_rows(up, side))
            fk = fk_ref[:, lanes]
            key_term = mm(v_pair, high) + mm(v_pair, low) + up[64:65]
            gfk = gfk_ref[:, lanes] + tail * key_term
            gv = gv + tail * (nt(fk, high) + nt(fk, low))
            d_scr[:, lanes] = features_back(fk.astype(F32), gfk, ones).astype(BF16)
        gvb_ref[:, pair_lanes] = gv.astype(BF16)
    d = d_scr[...]
    gk_ref[...] = (0.5 * nt(d, map_scr[...])).astype(BF16)
    gm = tn(k_ref[...], d)
    for h in range(4):
        gmap_ref[64 * h : 64 * h + 64, :] = gm[64 * h : 64 * h + 64, 128 * h : 128 * h + 128]


def inputs_back_kernel(gq_ref, gk_ref, gv_ref, w_ref, x_ref, gh_ref, gain_ref, gg_mlp_ref,
                       gmq_ref, gmk_ref, gx_ref, keep_ref, send_ref, acc, pack):
    j = pl.program_id(0)

    @pl.when(j == 0)
    def _():
        acc[...] = nt(gq_ref[...], w_ref[...])
        rows = gmq_ref.shape[0]
        low_half = iota(gmq_ref.shape, 1) < 64
        pack[:rows, :] = jnp.where(low_half, gmq_ref[...], pltpu.roll(gmk_ref[...], 64, 1))
        pack[rows:, :] = jnp.zeros((pack.shape[0] - rows, 128), F32)

    @pl.when(j == 1)
    def _():
        acc[...] += nt(gk_ref[...], w_ref[...])

    @pl.when(j == 2)
    def _():
        grad = acc[...] + nt(gv_ref[...], w_ref[...])
        normed, scale = moments(x_ref[...].astype(F32))
        gx_ref[...] = gh_ref[...] + norm_back(grad, normed, scale, gain_ref[...])
        gg = jnp.sum(grad * normed, axis=0, keepdims=True)
        rows = gmq_ref.shape[0]
        n = gg.shape[1] // 128
        for i in range(n):
            pack[rows + i : rows + i + 1, :] = gg[:, 128 * i : 128 * i + 128]
            pack[rows + n + i : rows + n + i + 1, :] = gg_mlp_ref[:, 128 * i : 128 * i + 128]
        for out, core in ((keep_ref, my_core()), (send_ref, 1 - my_core())):
            for c in range(n):
                start = core * (n * SMALL_ROWS) + c * SMALL_ROWS
                out[:, 128 * c : 128 * c + 128] = pack[pl.ds(pl.multiple_of(start, 8), SMALL_ROWS), :]


def unpack_kernel(kept_ref, got_ref, other_ref, gmq_ref, gmk_ref, gains_ref, pack):
    n = kept_ref.shape[1] // 128
    for value, core in ((kept_ref[...], my_core()), (other_ref[...], 1 - my_core())):
        for c in range(n):
            start = core * (n * SMALL_ROWS) + c * SMALL_ROWS
            pack[pl.ds(pl.multiple_of(start, 8), SMALL_ROWS), :] = value[:, 128 * c : 128 * c + 128]
    heads = gmq_ref.shape[0]
    for h in range(heads):
        both = pack[64 * h : 64 * h + 64, :]
        gmq_ref[h] = both[:, :64]
        gmk_ref[h] = both[:, 64:]
    gains_ref[...] = pack[64 * heads : 64 * heads + 16, :]


ORDERS = ((0, 1, 2, 3), (1, 2, 0, 3), (2, 0, 1, 3))


def send_kernel(kinds, x_ref, *refs):
    out_ref = refs[-1]
    for i, kind in enumerate(kinds):
        out_ref[i] = mm(x_ref[0, kind], refs[i][...])


def wave_kernel(plan, *refs):
    i = pl.program_id(0)

    @pl.when(i == 0)
    def _():
        for kept, got, at, count, send, base, keep in plan["folds"]:
            rows = refs[kept].shape[0] // count
            half = rows // 2
            for p in range(count):
                total = (refs[kept][rows * p : rows * p + rows, :]
                         + refs[got][at + rows * p : at + rows * p + rows, :])
                refs[send][base + half * p : base + half * p + half, :] = total[half:]
                refs[keep][half * p : half * p + half, :] = total[:half]
        for kept, got, at, out, block in plan["ends"]:
            rows, width = refs[out].shape[0], refs[kept].shape[1]
            first, piece = block
            refs[out][:, width * first : width * first + width] = (
                refs[kept][rows * piece : rows * piece + rows, :]
                + refs[got][at + rows * piece : at + rows * piece + rows, :]
            )
        for kept, got, at, send, base, keep in plan["smalls"]:
            rows = refs[kept].shape[0]
            total = refs[kept][...] + refs[got][at : at + rows, :]
            refs[keep][...] = total
            if send is not None:
                refs[send][base : base + rows, :] = total

    for step, (x, entry, y, r, send, base, keep, at) in enumerate(plan["joins"]):

        @pl.when(i == step)
        def _():
            value = mm(refs[x][1, entry], refs[y][...]) + refs[r][0]
            half = value.shape[0] // 2
            refs[send][base : base + half, :] = value[half:]
            refs[keep][at : at + half, :] = value[:half]


def core_hop(v):
    return lax.ppermute(v, "batch", [(0, 1), (1, 0)])


def local(inputs, w_qkv, w_out, w_fc, w_proj, map_query, map_key, gain_attn, gain_mlp,
          starts, key_mask, cotangent):
    T, D = inputs.shape[1], inputs.shape[2]
    H = map_query.shape[0]
    FF = w_fc.shape[1]
    n_seq = lax.axis_size("seq")
    planes = n_seq // 4
    quads = H // 4
    QW, FW = 4 * 64, 4 * 128
    half_rows = D // 2
    per = H // 4
    seq = lax.axis_index("seq")
    tok = None
    x, cot = inputs[0], cotangent[0]
    gain_a, gain_m = gain_attn.reshape(1, D), gain_mlp.reshape(1, D)
    direct = n_seq == 16

    def hop(v, bit):
        return lax.ppermute(v, "seq", [(i, i ^ (1 << bit)) for i in range(n_seq)])

    def to_member(v, k):
        return lax.ppermute(v, "seq", [(i, i ^ k) for i in range(n_seq)])

    def shift(v, by):
        return lax.ppermute(v, "seq", [(i, (i + by) % n_seq) for i in range(n_seq)])

    qcol = pl.BlockSpec((T, QW), lambda j: (0, j))
    fcol = pl.BlockSpec((T, FW), lambda j: (0, j))
    col128 = whole((T, 128))
    square = whole((T, T))
    full = whole((T, D))
    row = whole((1, D))
    maps = pl.BlockSpec((4, 64, 64), lambda j: (j, 0, 0))
    piece = (per, STATE_ROWS, 128)
    piece_spec = whole(piece)
    map_scr = pltpu.VMEM((QW, FW), BF16)
    state_scr = pltpu.VMEM((H, STATE_ROWS, 128), F32)

    def w_cols(part):
        return pl.BlockSpec((D, QW), lambda j: (0, part * quads + j))

    (attn, k, v, fk, s0, s1, s2, s3, allow, allow_t, tail, contin), tok = run(
        keys_kernel, tok, (quads,),
        [(Held(x), full), (gain_a, row), (Held(w_qkv), w_cols(1)), (Held(w_qkv), w_cols(2)), (Held(map_key), maps),
         (Held(key_mask), whole((1, T))), (starts, pl.BlockSpec(memory_space=pltpu.SMEM))],
        [((T, D), BF16, full), ((T, D), BF16, qcol), ((T, D), BF16, qcol), ((T, 2 * D), BF16, fcol)]
        + [(piece, F32, piece_spec)] * 4
        + [((T, T), F32, square)] * 2 + [((T, 128), F32, col128)] * 2,
        [map_scr, state_scr], us=8.0)

    def plane_exchange(pieces):
        return [pieces[0]] + [to_member(pieces[k], k) for k in range(1, 4)]

    def plane_total(own, tok):
        (total,), tok = run(
            plane_sum_kernel, tok, (1,), [(p, piece_spec) for p in own], [(piece, F32, piece_spec)])
        return total, tok

    def across(total, backward):
        if planes <= 4:
            return [shift(total, (-4 if backward else 4) * i) for i in range(1, planes)]
        every = lax.all_gather(total, "seq").reshape((planes, 4) + piece)
        mine = lax.dynamic_index_in_dim(every, seq & 3, 1, keepdims=False)
        place = jnp.arange(planes)
        want = place > (seq >> 2) if backward else place < (seq >> 2)
        return [jnp.sum(jnp.where(want[:, None, None, None], mine, 0.0), axis=0)]

    def scanned(own, others, backward, tok):
        return run(
            functools.partial(scan_kernel, backward, planes if planes <= 4 else None), tok, (1,),
            [(p, piece_spec) for p in own + others], [(piece, F32, piece_spec)] * 4)

    def turn(x, kinds, tok):
        shape = (2, len(kinds), half_rows, T)
        if not direct:
            return jnp.zeros(shape, BF16), tok
        (out,), tok = run(
            functools.partial(turn_kernel, kinds), tok, (1,), [(x, full)], [(shape, BF16, whole(shape))],
            [pltpu.VMEM((half_rows, T), F32)])
        return out, tok

    own = plane_exchange([s0, s1, s2, s3])

    (q, fq, nd), tok = run(
        queries_kernel, tok, (quads,),
        [(attn, full), (w_qkv, w_cols(0)), (map_query, maps), (fk, fcol), (v, qcol), (allow, square)],
        [((T, D), BF16, qcol), ((T, 2 * D), BF16, fcol), ((T, 2 * D), F32, fcol)],
        [map_scr], us=9.0)
    total, tok = plane_total(own, tok)
    others = across(total, False)
    (ga,), tok = run(
        act_back_kernel, tok, (FF // D,), [(cot, full), (w_proj, pl.BlockSpec((D, D), lambda j: (j, 0)))],
        [((T, FF), F32, columns(T, D), True)], us=4.0)
    carried, tok = scanned(own, others, False, tok)
    carry = plane_exchange(carried)
    cot_t, tok = turn(cot, (0, 1, 2), tok)
    attn_t, tok = turn(attn, (0, 1, 2), tok)

    (mixed, mf, rden, hidden, mlp_in), tok = run(
        mix_kernel, tok, (quads,),
        [(x, full), (nd, fcol), (fq, fcol)] + [(c, piece_spec) for c in carry]
        + [(contin, col128), (w_out, pl.BlockSpec((QW, D), lambda j: (j, 0))), (gain_m, row)],
        [((T, D), BF16, qcol), ((T, D), F32, qcol), ((T, D), F32, qcol), ((T, D), F32, full),
         ((T, D), BF16, full)],
        [state_scr], us=4.5)
    mlp_t, tok = turn(mlp_in, (0, 1, 2), tok)

    n_ff = FF // D
    turned_spec = whole((2, 3, half_rows, T))
    send_shape = (2, n_ff, half_rows, D)
    (act, gp, send_mlp), tok = run(
        mlp_kernel, tok, (n_ff,),
        [(mlp_in, full), (ga, columns(T, D)), (mlp_t, turned_spec), (cot_t, turned_spec), (w_fc, columns(D, D))],
        [((T, FF), BF16, columns(T, D))] * 2
        + [(send_shape, F32, pl.BlockSpec((2, 1, half_rows, D), lambda j: (0, j, 0, 0)))], us=10.0)
    if direct:
        recv_mlp = core_hop(send_mlp).reshape(2 * n_ff, half_rows, D)
    (output, gh, gh_low, gg_mlp), tok = run(
        mlp_out_kernel, tok, (quads,),
        [(act, whole((T, FF))), (gp, whole((T, FF))), (w_fc, pl.BlockSpec((QW, FF), lambda j: (j, 0))),
         (w_proj, columns(FF, QW)), (hidden, qcol), (hidden, full), (cot, full), (gain_m, row)],
        [((T, D), F32, qcol), ((T, D), F32, full), ((T, D), BF16, full), ((1, D), F32, row)],
        [pltpu.VMEM((quads, T, QW), F32)], us=8.0)
    def send_half(x_t, kinds, ys, tok):
        shape = (len(kinds), half_rows, D)
        (out,), tok = run(
            functools.partial(send_kernel, kinds), tok, (1,),
            [(x_t, whole(x_t.shape))] + [(y, full) for y in ys], [(shape, F32, whole(shape))], us=30.0)
        return core_hop(out), tok

    class Group:
        def __init__(self, counts, layout, widths):
            self.counts, self.layout, self.widths = counts, layout, widths
            self.stage, self.small = -1, None

    def wave(folds, join, tok, us=30.0):
        ins, outs, sends = [], [], {}
        plan = {"folds": [], "ends": [], "smalls": [], "joins": []}
        after = []

        def take(array, spec=None):
            for n, (other, other_spec) in enumerate(ins):
                if other is array and spec is None:
                    return n
            ins.append((array, spec or whole(array.shape)))
            return len(ins) - 1

        def place(bit, rows):
            base = sends.get(bit, 0)
            sends[bit] = base + rows
            return base

        def give(shape, put, not_last=True):
            outs.append((shape, F32, whole(shape), not_last and Near))
            after.append((len(outs) - 1, put))
            return ("out", len(outs) - 1)

        steps = 1
        for g in folds:
            g.stage += 1
            if g.stage == 4:
                rows = half_rows // 16
                g.result = [None] * len(g.widths)
                made = []
                for n, width in enumerate(g.widths):
                    def put(array, n=n, g=g):
                        g.result[n] = array
                    made.append(give((rows, width), put, False))
                n = 0
                for kind in range(3):
                    if g.counts[kind] == 0:
                        continue
                    got, at = g.got[kind]
                    for p in range(g.counts[kind]):
                        out, block = g.layout[n]
                        plan["ends"].append((take(g.keeps[kind]), take(got), at, made[out], (block, p)))
                        n += 1
            else:
                old_keeps, g.keeps = g.keeps, [None] * 3
                old_got, g.got = g.got, [None] * 3
                for kind in range(3):
                    if g.counts[kind] == 0:
                        continue
                    bit = ORDERS[kind][g.stage]
                    rows = old_keeps[kind].shape[0] // 2
                    base = place(bit, rows)
                    def put(array, kind=kind, g=g):
                        g.keeps[kind] = array
                    keep = give((rows, D), put)
                    got, at = old_got[kind]
                    plan["folds"].append(
                        (take(old_keeps[kind]), take(got), at, g.counts[kind], ("send", bit), base, keep))
                    g.got[kind] = (bit, base)
            if g.small is not None:
                got, at = g.small_got
                bit = ORDERS[0][g.stage] if g.stage < 4 else None
                base = place(bit, SMALL_ROWS) if g.stage < 4 else 0
                def put(array, g=g):
                    g.small = array
                keep = give(small_shape, put)
                plan["smalls"].append(
                    (take(g.small), take(got), at, ("send", bit) if g.stage < 4 else None, base, keep))
                g.small_got = (bit, base)
        if join is not None:
            g, xs, ys, segments, small = join
            g.stage = 0
            g.keeps, g.got, offset = [None] * 3, [None] * 3, [0, 0, 0]
            at_x = [take(x) for x in xs]
            at_y, at_r = [], []
            for n, (y, r, block, y_block) in enumerate(ys):
                mine = [i for i, seg in enumerate(segments) if seg[2] == n]
                first, count = mine[0], len(mine)
                at_y.append(take(y, pl.BlockSpec(
                    (T, D), lambda i, first=first, count=count, block=y_block:
                    (0, block + jnp.clip(i - first, 0, count - 1)))))
                at_r.append(take(r, pl.BlockSpec(
                    (1, half_rows, D), lambda i, first=first, count=count, block=block:
                    (block + jnp.clip(i - first, 0, count - 1), 0, 0))))
            half = half_rows // 2
            for kind in range(3):
                if g.counts[kind] == 0:
                    continue
                bit = ORDERS[kind][0]
                g.got[kind] = (bit, place(bit, half * g.counts[kind]))
                def put(array, kind=kind, g=g):
                    g.keeps[kind] = array
                g.keeps[kind] = give((half * g.counts[kind], D), put)
            for x, entry, y, kind in segments:
                bit, base = g.got[kind]
                plan["joins"].append(
                    (at_x[x], entry, at_y[y], at_r[y], ("send", bit), base + offset[kind], g.keeps[kind], offset[kind]))
                offset[kind] += half
            steps = len(segments)
            if small is not None:
                bit = ORDERS[0][0]
                base = place(bit, SMALL_ROWS)
                def put(array, g=g):
                    g.small = array
                keep = give(small_shape, put)
                plan["smalls"].append((take(small[0]), take(small[1]), 0, ("send", bit), base, keep))
                g.small, g.small_got = True, (bit, base)
        first_send = len(outs)
        bits = sorted(sends)
        for bit in bits:
            outs.append(((sends[bit], D), F32, whole((sends[bit], D)), Near))
        n_in = len(ins)

        def ref(item):
            if isinstance(item, tuple) and item[0] == "out":
                return n_in + item[1]
            if isinstance(item, tuple) and item[0] == "send":
                return n_in + first_send + bits.index(item[1])
            return item

        plan = {name: tuple(tuple(ref(x) for x in entry) for entry in entries) for name, entries in plan.items()}
        results, tok = run(functools.partial(wave_kernel, plan), tok, (steps,), ins, outs, us=us, extra=9)
        for n, put in after:
            put(results[n])
        moved = {bit: Near(hop(results[first_send + n].array, bit)) for n, bit in enumerate(bits)}
        for g in folds + ([join[0]] if join else []):
            if g.stage < 4:
                g.got = [item and (moved[item[0]], item[1]) for item in g.got]
                if g.small is not None:
                    g.small_got = (moved[g.small_got[0]], g.small_got[1])
        return tok

    small_shape = (SMALL_ROWS, D)
    early = Group((1, 1, 1), [(0, i) for i in range(3)], (3 * D,))
    main = Group((2, 2, 1), [(0, 0)] + [(1, i) for i in range(n_ff)], (D, FF))
    wide = Group((0, 0, 1), [(0, 0)], (D,))
    last = Group((1, 1, 1), [(0, i) for i in range(3)], (3 * D,))
    if direct:
        tok = wave([], (early, [cot_t], [(act, recv_mlp, 0, 0)], [(0, kind, 0, kind) for kind in range(3)], None), tok, 4.0)

    (gn, gd, gd_t, s0, s1, s2, s3), tok = run(
        numer_back_kernel, tok, (quads,),
        [(gh_low, full), (w_out, pl.BlockSpec((QW, D), lambda j: (j, 0))), (mf, qcol), (rden, qcol),
         (fq, fcol), (contin, col128)],
        [((T, D), BF16, qcol), ((T, D), F32, qcol),
         ((8 * H, T), F32, pl.BlockSpec((32, T), lambda j: (j, 0)))] + [(piece, F32, piece_spec)] * 4,
        [state_scr], us=5.0)
    own = plane_exchange([s0, s1, s2, s3])
    if direct:
        tok = wave(
            [early],
            (main, [cot_t, mlp_t], [(act, recv_mlp, n_ff - 1, n_ff - 1), (gp, recv_mlp, n_ff, 0)],
             [(0, 0, 0, 0)] + [(1, kind, 1, kind) for kind in (0, 1, 1, 2)], None), tok, 7.0)
    total, tok = plane_total(own, tok)
    others = across(total, True)

    def fixed(shape, quad):
        return pl.BlockSpec(shape, lambda i: (0, quad))

    def fixed_rows(shape, quad):
        return pl.BlockSpec(shape, lambda i: (quad,) + (0,) * (len(shape) - 1))

    def scores_back(quad, before, tok):
        ins = [(q, fixed((T, QW), quad)), (fq, fixed((T, FW), quad)), (fk, fixed((T, FW), quad)),
               (v, fixed((T, QW), quad)), (gn, fixed((T, QW), quad)), (gd, fixed((T, QW), quad)),
               (gd_t, fixed_rows((32, T), quad))] + [(c, piece_spec) for c in carry]
        ins += [(allow, square), (allow_t, square), (contin, col128), (map_query, fixed_rows((4, 64, 64), quad))]
        aliases = {len(ins) + i: i for i in range(4)} if before else None
        ins += [(a, ANYWHERE) for a in before]
        return run(
            functools.partial(scores_back_kernel, quad), tok, (1,), ins,
            [((T, D), BF16, fixed((T, QW), quad)), ((T, 2 * D), F32, fixed((T, FW), quad)),
             ((T, D), F32, fixed((T, QW), quad)), ((D, 128), F32, fixed_rows((QW, 128), quad))],
            [map_scr, state_scr, pltpu.VMEM((T, FW), BF16)], extra=12, aliases=aliases, us=4.5)

    backs, tok = scores_back(0, [], tok)
    backs, tok = scores_back(1, backs, tok)
    backs, tok = scores_back(2, backs, tok)
    gq, gfk, gv_f, gmq = backs
    carried, tok = scanned(own, others, True, tok)
    upstream = plane_exchange(carried)
    if direct:
        mixed_t, tok = turn(mixed, (2,), tok)
        recv_out, tok = send_half(mixed_t, (0,), [gh_low], tok)
        tok = wave(
            [early, main], (wide, [mixed_t], [(gh_low, recv_out, 0, 0)], [(0, 0, 0, 2)], None), tok, 2.0)

    (gk, gv, gmk), tok = run(
        keys_back_kernel, tok, (quads,),
        [(k, qcol), (fk, fcol), (v, qcol), (gfk, fcol), (gv_f, qcol)] + [(c, piece_spec) for c in upstream]
        + [(tail, col128), (map_key, maps)],
        [((T, D), BF16, qcol), ((T, D), BF16, qcol),
         ((D, 128), F32, pl.BlockSpec((QW, 128), lambda j: (j, 0)))],
        [map_scr, state_scr, pltpu.VMEM((T, FW), BF16)], us=60.0)
    if direct:
        recv_qkv, tok = send_half(attn_t, (0, 1, 2), [gq, gk, gv], tok)

    small_spec = whole(small_shape)
    packed = 2 * SMALL_ROWS * (D // 128)
    (gx, keep, send), tok = run(
        inputs_back_kernel, tok, (3,),
        [(gq, full), (gk, full), (gv, full), (w_qkv, columns(D, D)), (x, full), (gh, full), (gain_a, row),
         (gg_mlp, row), (gmq, whole((D, 128))), (gmk, whole((D, 128)))],
        [((T, D), F32, full)] + [(small_shape, F32, small_spec)] * 2,
        [pltpu.VMEM((T, D), F32), pltpu.VMEM((packed, 128), F32)], us=60.0)

    got = core_hop(send)
    if direct:
        tok = wave(
            [], (last, [attn_t], [(gq, recv_qkv, 0, 0), (gk, recv_qkv, 1, 0), (gv, recv_qkv, 2, 0)],
                 [(0, kind, kind, kind) for kind in range(3)], (keep, got)), tok, 4.0)
        tok = wave([early, main, wide], None, tok)
        tok = wave([last], None, tok)
        tok = wave([early, main, wide], None, tok)
        tok = wave([last], None, tok)
        tok = wave([main, wide], None, tok)
        tok = wave([last], None, tok)
        tok = wave([wide], None, tok)
        tok = wave([last], None, tok)
        mine = last.small.array
        got = core_hop(mine)
        (grad_w_qkv,) = last.result
        proj_last, grad_w_fc = main.result
        (grad_w_out,) = wide.result
        grad_proj_rows = jnp.concatenate([early.result[0], proj_last], axis=1)
    else:
        mine = lax.psum(keep + got, "seq")
        got = core_hop(mine)
        summed = lax.psum_scatter(
            jnp.concatenate(
                [tn(attn, gq), tn(attn, gk), tn(attn, gv), tn(mixed, gh_low), tn(mlp_in, gp), tn(cot, act)],
                axis=1,
            ),
            ("batch", "seq"), scatter_dimension=0, tiled=True)
        grad_w_qkv = summed[:, : 3 * D]
        grad_w_out = summed[:, 3 * D : 4 * D]
        grad_w_fc = summed[:, 4 * D : 4 * D + FF]
        grad_proj_rows = summed[:, 4 * D + FF :]

    heads_shape = (H, 64, 64)
    (grad_map_query, grad_map_key, gains), tok = run(
        unpack_kernel, tok, (1,), [(mine, small_spec), (mine, small_spec), (got, small_spec)],
        [(heads_shape, F32, whole(heads_shape))] * 2 + [((16, 128), F32, whole((16, 128)))],
        [pltpu.VMEM((packed, 128), F32)])
    n = D // 128
    return (
        output[None],
        gx[None],
        grad_w_qkv,
        grad_w_out,
        grad_w_fc,
        grad_proj_rows.T,
        grad_map_query,
        grad_map_key,
        gains[:n].reshape(D),
        gains[n : 2 * n].reshape(D),
    )


def solution(mesh):
    tokens = P("batch", "seq", None)
    flags = P("batch", "seq")
    rows = P(("batch", "seq"), None)
    return jax.shard_map(
        local,
        mesh=mesh,
        in_specs=(tokens,) + (P(),) * 8 + (flags, flags, tokens),
        out_specs=(tokens, tokens, rows, rows, rows, P(None, ("batch", "seq")), P(), P(), P(), P()),
        check_vma=False,
    )
```

```python
import functools

import jax
import jax.numpy as jnp
from jax import lax
from jax.experimental import pallas as pl
from jax.experimental.pallas import tpu as pltpu
from jax.sharding import PartitionSpec as P

EPSILON = 1e-05
F32 = jnp.float32
BF16 = jnp.bfloat16
STATE_ROWS = 72
SMALL_ROWS = 72
MIB = 1024 * 1024


def mm(a, b):
    return lax.dot_general(a, b, (((1,), (0,)), ((), ())), preferred_element_type=F32)


def nt(a, b):
    return lax.dot_general(a, b, (((1,), (1,)), ((), ())), preferred_element_type=F32)


def tn(a, b):
    return lax.dot_general(a, b, (((0,), (0,)), ((), ())), preferred_element_type=F32)


def split(v):
    high = v.astype(BF16)
    return high, (v - high.astype(F32)).astype(BF16)


def iota(shape, dim):
    return lax.broadcasted_iota(jnp.int32, shape, dim)


def segment_ones(width):
    shape = (width, width)
    return (iota(shape, 0) // 64 == iota(shape, 1) // 64).astype(BF16)


def segment_sum(v, ones):
    high, low = split(v)
    return mm(high, ones) + mm(low, ones)


def moments(x):
    centre = jnp.mean(x, axis=-1, keepdims=True)
    offsets = x - centre
    variance = jnp.mean(offsets * offsets, axis=-1, keepdims=True)
    scale = lax.rsqrt(variance + EPSILON)
    return offsets * scale, scale


def norm_back(grad, normed, scale, gain):
    dn = grad * gain
    first = jnp.mean(dn, axis=-1, keepdims=True)
    second = jnp.mean(dn * normed, axis=-1, keepdims=True)
    return (dn - first - normed * second) * scale


def fill_maps(scr, map_ref):
    scr[...] = jnp.zeros(scr.shape, scr.dtype)
    for h in range(4):
        m = map_ref[h].astype(F32)
        scr[64 * h : 64 * h + 64, 128 * h : 128 * h + 128] = jnp.concatenate(
            [m, -m], axis=1
        ).astype(scr.dtype)


def half_sums(v, low_half):
    top = jnp.sum(jnp.where(low_half, v, 0.0), axis=1, keepdims=True)
    bottom = jnp.sum(jnp.where(low_half, 0.0, v), axis=1, keepdims=True)
    return jnp.where(low_half, top, bottom)


def features(pre):
    low_half = iota(pre.shape, 1) < 64
    top = jnp.max(jnp.where(low_half, pre, -jnp.inf), axis=1, keepdims=True)
    bottom = jnp.max(jnp.where(low_half, -jnp.inf, pre), axis=1, keepdims=True)
    e = jnp.exp(pre - jnp.where(low_half, top, bottom))
    return e / half_sums(e, low_half)


def features_back(feat, grad, ones):
    low_half = iota(feat.shape, 1) < 64
    weighted = feat * grad
    mass = mm(feat.astype(BF16), ones)
    part = weighted - feat * (half_sums(weighted, low_half) / mass)
    return part - pltpu.roll(part, 64, 1)


def whole(shape):
    return pl.BlockSpec(shape, lambda *_: (0,) * len(shape))


def columns(rows, width):
    return pl.BlockSpec((rows, width), lambda j: (0, j))


ANYWHERE = pl.BlockSpec(memory_space=pl.ANY)


def my_core():
    return lax.axis_index("batch")


def my_seq():
    return lax.axis_index("seq")


def nbytes(shape, dtype):
    total = jnp.dtype(dtype).itemsize
    for n in shape:
        total *= n
    return total


class Held:
    def __init__(self, array):
        self.array, self.shape, self.dtype = array, array.shape, array.dtype


class Near(Held):
    pass


def run(kernel, tok, grid, ins, outs, scratch=(), extra=4, aliases=None, us=1.0):
    n_in, n_out = len(ins), len(outs)
    linked = tok is not None
    outs = [tuple(out) + (False,) * (4 - len(out)) for out in outs]

    def body(*refs):
        kernel(*refs[:n_in], *refs[n_in + linked : n_in + linked + n_out], *refs[n_in + linked + n_out + 1 :])

    held = 0
    arrays = []
    for array, spec in ins:
        near = isinstance(array, Near)
        if spec.block_shape is not None and not (near and spec.block_shape == array.shape):
            held += (1 if spec.block_shape == array.shape else 2) * nbytes(spec.block_shape, array.dtype)
        if isinstance(array, Held):
            array = pltpu.with_memory_space_constraint(array.array, pltpu.VMEM if near else pltpu.HBM)
        arrays.append(array)
    for shape, dtype, spec, stays in outs:
        if not (stays is Near and spec.block_shape == shape):
            held += (1 if spec.block_shape == shape else 2) * nbytes(spec.block_shape, dtype)
    for item in scratch:
        held += nbytes(item.shape, item.dtype)
    result = pl.pallas_call(
        body,
        grid=grid,
        in_specs=[spec for _, spec in ins] + [ANYWHERE] * linked,
        out_specs=[spec for _, _, spec, _ in outs] + [ANYWHERE],
        scratch_shapes=list(scratch),
        out_shape=[
            pltpu.VMEM(shape, dtype) if stays is Near
            else pltpu.HBM(shape, dtype) if stays else jax.ShapeDtypeStruct(shape, dtype)
            for shape, dtype, _, stays in outs
        ]
        + [jax.ShapeDtypeStruct((8, 128), F32)],
        input_output_aliases=aliases or {},
        cost_estimate=pl.CostEstimate(flops=int(us * 1.15e9), bytes_accessed=0, transcendentals=0),
        compiler_params=pltpu.CompilerParams(vmem_limit_bytes=min(held + extra * MIB, 60 * MIB)),
    )(*arrays, *([tok] if linked else []))
    results = [Near(r) if out[3] is Near else Held(r) if out[3] else r for r, out in zip(result, outs)]
    return results, result[-1]


def keys_kernel(x_ref, gain_ref, wk_ref, wv_ref, map_ref, mask_ref, starts_ref,
                attn_ref, k_ref, v_ref, fk_ref, p0, p1, p2, p3,
                allow_ref, allow_t_ref, tail_ref, contin_ref,
                map_scr, state_scr):
    j = pl.program_id(0)
    tokens = x_ref.shape[0]
    n_flags = starts_ref.shape[1]
    unit = tokens // n_flags

    def seg(shape, dim):
        place = iota(shape, dim)
        total = jnp.zeros(shape, jnp.int32)
        for u in range(n_flags):
            total = total + jnp.where(place >= unit * u, starts_ref[0, u], 0)
        return total

    @pl.when(j == 0)
    def _():
        normed, _ = moments(x_ref[...].astype(F32))
        attn_ref[...] = (normed * gain_ref[...]).astype(BF16)
        last = starts_ref[0, 0]
        for u in range(1, n_flags):
            last = last + starts_ref[0, u]
        mask_row = mask_ref[...].astype(F32)
        mask_col = jnp.transpose(jnp.broadcast_to(mask_row, (128, tokens)))
        seg_col = seg((tokens, 128), 0)
        tail_ref[...] = jnp.where(seg_col == last, mask_col, 0.0)
        contin_ref[...] = jnp.where(seg_col == 0, 1.0, 0.0)
        square = (tokens, tokens)
        same = seg(square, 0) == seg(square, 1)
        allow_ref[...] = jnp.where(same & (iota(square, 1) <= iota(square, 0)), mask_row, 0.0)
        wide_mask = jnp.concatenate([mask_col] * (tokens // 128), axis=1)
        allow_t_ref[...] = jnp.where(same & (iota(square, 0) <= iota(square, 1)), wide_mask, 0.0)

    fill_maps(map_scr, map_ref)
    attn = attn_ref[...]
    k4 = mm(attn, wk_ref[...]).astype(BF16)
    v4 = mm(attn, wv_ref[...]).astype(BF16)
    k_ref[...] = k4
    v_ref[...] = v4
    pre = mm(k4, map_scr[...])
    ones = segment_ones(128)
    v_t = jnp.transpose(v4.astype(F32)).astype(BF16)
    tail = tail_ref[...]
    row_ones = jnp.ones((16, tokens), BF16)
    for h in range(4):
        feat = features(pre[:, 128 * h : 128 * h + 128]).astype(BF16)
        fk_ref[:, 128 * h : 128 * h + 128] = feat
        kept = (feat.astype(F32) * tail).astype(BF16)
        rows = jnp.concatenate([v_t[64 * h : 64 * h + 64], row_ones], axis=0)
        state_scr[4 * j + h] = mm(rows, kept)[0:STATE_ROWS]

    @pl.when(j == pl.num_programs(0) - 1)
    def _():
        for k, piece in enumerate((p0, p1, p2, p3)):
            n = piece.shape[0]
            piece[...] = state_scr[pl.ds(((my_seq() & 3) ^ k) * n, n)]


def queries_kernel(attn_ref, wq_ref, map_ref, fk_ref, v_ref, allow_ref,
                   q_ref, fq_ref, nd_ref, map_scr):
    tokens = attn_ref.shape[0]
    half = tokens // 2
    fill_maps(map_scr, map_ref)
    q4 = mm(attn_ref[...], wq_ref[...]).astype(BF16)
    q_ref[...] = q4
    pre = mm(q4, map_scr[...])
    ones = segment_ones(128)
    low_half = iota((tokens, 128), 1) < 64
    for h in range(4):
        lanes = slice(128 * h, 128 * h + 128)
        feat = features(pre[:, lanes]).astype(BF16)
        fq_ref[:, lanes] = feat
        fk = fk_ref[:, lanes]
        pair = v_ref[:, 128 * (h // 2) : 128 * (h // 2) + 128].astype(F32)
        if h % 2:
            pair = pltpu.roll(pair, 64, 1)
        wide = jnp.where(low_half, pair, 1.0).astype(BF16)
        first = nt(feat[:half], fk[:half]) * allow_ref[:half, :half]
        nd_ref[:half, lanes] = mm(first.astype(BF16), wide[:half])
        second = nt(feat[half:], fk) * allow_ref[half:, :]
        nd_ref[half:, lanes] = mm(second.astype(BF16), wide)


def plane_sum_kernel(*refs):
    *pieces, out = refs
    total = pieces[0][...]
    for piece in pieces[1:]:
        total = total + piece[...]
    out[...] = total


def scan_kernel(backward, planes, *refs):
    own = refs[:4]
    others = refs[4:-4]
    outs = refs[-4:]
    member, plane = my_seq() & 3, my_seq() >> 2
    total = jnp.zeros(own[0].shape, F32)
    for i, other in enumerate(others):
        if planes is None:
            total = total + other[...]
        else:
            there = plane + i + 1 < planes if backward else plane - i - 1 >= 0
            total = total + jnp.where(there, other[...], 0.0)
    for k, out in enumerate(outs):
        value = total
        target = member ^ k
        for i, piece in enumerate(own):
            source = member ^ i
            counts = source > target if backward else source < target
            value = value + jnp.where(counts, piece[...], 0.0)
        out[...] = value


def later_kernel(planes, own0, own1, own2, own3, *refs):
    own, others, (mine, x_pair, y_one) = (own0, own1, own2, own3), refs[:-3], refs[-3:]
    member, plane = my_seq() & 3, my_seq() >> 2
    total = jnp.zeros(own0.shape, F32)
    for i, other in enumerate(others):
        if planes is None:
            total = total + other[...]
        else:
            total = total + jnp.where(plane + i + 1 < planes, other[...], 0.0)
    n = own0.shape[0]
    for k in range(4):
        value = total
        for i, piece in enumerate(own):
            value = value + jnp.where((member ^ i) > (member ^ k), piece[...], 0.0)
        if k == 0:
            mine[...] = value
        elif k == 2:
            y_one[...] = value
        else:
            x_pair[n * (k // 2) : n * (k // 2) + n] = value


def place_heads(scr, pieces):
    for k, piece in enumerate(pieces):
        n = piece.shape[0]
        scr[pl.ds(((my_seq() & 3) ^ k) * n, n)] = piece[...]


def mix_kernel(x_ref, nd_ref, fq_ref, c0, c1, c2, c3, contin_ref, wo_ref, gain_ref,
               mixed_ref, mf_ref, rden_ref, hidden_ref, mlp_ref, carry_scr):
    j = pl.program_id(0)
    tokens = x_ref.shape[0]
    low_half = iota((tokens, 128), 1) < 64

    @pl.when(j == 0)
    def _():
        place_heads(carry_scr, (c0, c1, c2, c3))
        hidden_ref[...] = x_ref[...].astype(F32)

    contin = contin_ref[...]
    for pair in range(2):
        quotients, inverses = [], []
        for side in range(2):
            h = 2 * pair + side
            lanes = slice(128 * h, 128 * h + 128)
            carry = carry_scr[4 * j + h]
            wide = jnp.concatenate([carry[:64], jnp.broadcast_to(carry[64:65], (64, 128))], axis=0)
            high, low = split(wide)
            fq = fq_ref[:, lanes]
            nd = nd_ref[:, lanes] + contin * (nt(fq, high) + nt(fq, low))
            inverse = 1.0 / nd
            turned = pltpu.roll(inverse, 64, 1)
            quotient = nd * turned
            if side:
                quotients.append(pltpu.roll(quotient, 64, 1))
                inverses.append(inverse)
            else:
                quotients.append(quotient)
                inverses.append(turned)
        lanes = slice(128 * pair, 128 * pair + 128)
        mf = jnp.where(low_half, *quotients)
        mf_ref[:, lanes] = mf
        mixed_ref[:, lanes] = mf.astype(BF16)
        rden_ref[:, lanes] = jnp.where(low_half, *inverses)
    hidden_ref[...] += mm(mixed_ref[...], wo_ref[...])

    @pl.when(j == pl.num_programs(0) - 1)
    def _():
        normed, _ = moments(hidden_ref[...])
        mlp_ref[...] = (normed * gain_ref[...]).astype(BF16)


GELU_A, GELU_C = 0.044715, 0.7978845608028654


def turn_kernel(kinds, x_ref, out_ref, scr):
    rows, half = out_ref.shape[2] // 16, out_ref.shape[2]
    for side in range(2):
        core = my_core() if side else 1 - my_core()
        turned = jnp.transpose(
            x_ref[:, pl.ds(pl.multiple_of(core * half, 128), half)].astype(F32)
        )
        for at, kind in enumerate(kinds):
            for g in range(16):
                place = g ^ my_seq()
                spot = 0
                for depth, bit in enumerate(ORDERS[kind]):
                    spot = spot + (((place >> bit) & 1) << (3 - depth))
                scr[pl.ds(pl.multiple_of(spot * rows, 8), rows), :] = turned[rows * g : rows * g + rows]
            out_ref[side, at] = scr[...].astype(BF16)


def act_back_kernel(cot_ref, wp_ref, ga_ref):
    width = wp_ref.shape[0]
    start = pl.multiple_of(pl.program_id(0) * width, 128)
    ga_ref[:, pl.ds(start, width)] = nt(cot_ref[...], wp_ref[...])


def mlp_kernel(mlp_ref, ga_ref, mlp_t, cot_t, wf_ref, act_ref, gp_ref, send_ref):
    j = pl.program_id(0)
    tokens, width = mlp_ref.shape[0], wf_ref.shape[1]
    lanes = slice(0, width)
    step = tokens // 4
    for r in range(4):
        rows = slice(step * r, step * r + step)
        u = mm(mlp_ref[rows, :], wf_ref[...])
        square = u * u
        t = jnp.tanh(GELU_C * (u + GELU_A * (u * square)))
        half = 0.5 * (1.0 + t)
        act_ref[rows, lanes] = (u * half).astype(BF16)
        slope = half + (0.5 * GELU_C) * u * (1.0 - t * t) * (1.0 + (3.0 * GELU_A) * square)
        gp_ref[rows, lanes] = (ga_ref[rows, lanes] * slope).astype(BF16)
    send_ref[0, 0] = mm(cot_t[0, j % 3], act_ref[:, lanes])
    send_ref[1, 0] = mm(mlp_t[0, (j + 1) // 2], gp_ref[:, lanes])


def mlp_out_kernel(act_ref, gp_ref, wf_ref, wp_ref, part_ref, hidden_ref, cot_ref, gain_ref,
                   out_ref, gh_ref, gh_low_ref, gg_ref, back_scr):
    j = pl.program_id(0)
    out_ref[...] = part_ref[...] + mm(act_ref[...], wp_ref[...])
    back_scr[j] = nt(gp_ref[...], wf_ref[...])

    @pl.when(j == pl.num_programs(0) - 1)
    def _():
        normed, scale = moments(hidden_ref[...])
        grad = jnp.concatenate([back_scr[i] for i in range(back_scr.shape[0])], axis=1)
        gg_ref[...] = jnp.sum(grad * normed, axis=0, keepdims=True)
        gh = cot_ref[...].astype(F32) + norm_back(grad, normed, scale, gain_ref[...])
        gh_ref[...] = gh
        gh_low_ref[...] = gh.astype(BF16)


def numer_back_kernel(gh_ref, wo_ref, mf_ref, rden_ref, fq_ref, contin_ref,
                      gn_ref, gd_ref, gd_t_ref, p0, p1, p2, p3, state_scr):
    j = pl.program_id(0)
    gm = nt(gh_ref[...], wo_ref[...]) * rden_ref[...]
    gn_ref[...] = gm.astype(BF16)
    gd = -segment_sum(gm * mf_ref[...], segment_ones(256))
    gd_ref[...] = gd
    gn_t = jnp.transpose(gm).astype(BF16)
    gd_t = jnp.transpose(gd)
    contin = contin_ref[...]
    for h in range(4):
        rows = gd_t[64 * h : 64 * h + 8]
        gd_t_ref[8 * h : 8 * h + 8, :] = rows
        kept = (fq_ref[:, 128 * h : 128 * h + 128].astype(F32) * contin).astype(BF16)
        high, low = split(rows)
        both = jnp.concatenate([high.astype(F32), low.astype(F32)], axis=0).astype(BF16)
        sums = mm(jnp.concatenate([gn_t[64 * h : 64 * h + 64], both], axis=0), kept)
        state_scr[4 * j + h, 0:64, :] = sums[0:64]
        state_scr[4 * j + h, 64:72, :] = sums[64:72] + sums[72:80]

    @pl.when(j == pl.num_programs(0) - 1)
    def _():
        for k, piece in enumerate((p0, p1, p2, p3)):
            n = piece.shape[0]
            piece[...] = state_scr[pl.ds(((my_seq() & 3) ^ k) * n, n)]


def side_rows(state, side):
    zeros = jnp.zeros((64, 128), F32)
    rows = state[:64]
    return jnp.concatenate([zeros, rows] if side else [rows, zeros], axis=0)


def scores_back_kernel(j, q_ref, fq_ref, fk_ref, v_ref, gn_ref, gd_ref, gd_t_ref,
                       c0, c1, c2, c3, allow_ref, allow_t_ref, contin_ref, map_ref, *rest):
    gq_ref, gfk_ref, gv_ref, gmap_ref, map_scr, carry_scr, d_scr = rest[-7:]
    tokens = q_ref.shape[0]
    half = tokens // 2
    place_heads(carry_scr, (c0, c1, c2, c3))

    fill_maps(map_scr, map_ref)
    ones = segment_ones(128)
    low_half = iota((tokens, 128), 1) < 64
    contin = contin_ref[...]
    for pair in range(2):
        pair_lanes = slice(128 * pair, 128 * pair + 128)
        v_pair = v_ref[:, pair_lanes]
        gn_pair = gn_ref[:, pair_lanes].astype(F32)
        gd_pair = gd_ref[:, pair_lanes]
        gd_turned = pltpu.roll(gd_pair, 64, 1)
        gv_parts = []
        for side in range(2):
            h = 2 * pair + side
            lanes = slice(128 * h, 128 * h + 128)
            mine = ~low_half if side else low_half
            gn = jnp.where(mine, gn_pair, 0.0).astype(BF16)
            gd = jnp.where(mine, gd_pair, gd_turned)
            gd_row = gd_t_ref[8 * h : 8 * h + 1, :]
            fq, fk = fq_ref[:, lanes], fk_ref[:, lanes]
            gd_few = jnp.concatenate([gd] * (half // 128), axis=1)
            gd_many = jnp.concatenate([gd] * (tokens // 128), axis=1)
            g_top = ((nt(gn[:half], v_pair[:half]) + gd_few[:half]) * allow_ref[:half, :half]).astype(BF16)
            g_bot = ((nt(gn[half:], v_pair) + gd_many[half:]) * allow_ref[half:, :]).astype(BF16)
            carry = carry_scr[4 * j + h]
            high, low = split(side_rows(carry, side))
            inter = mm(gn, high) + mm(gn, low) + gd * carry[64:65]
            gfq = jnp.concatenate([mm(g_top, fk[:half]), mm(g_bot, fk)], axis=0) + contin * inter
            d_scr[:, lanes] = features_back(fq.astype(F32), gfq, ones).astype(BF16)

            at_top, at_bot = allow_t_ref[:half, :], allow_t_ref[half:, half:]
            gt_top = ((nt(v_pair[:half], gn) + gd_row) * at_top).astype(BF16)
            gt_bot = ((nt(v_pair[half:], gn[half:]) + gd_row[:, half:]) * at_bot).astype(BF16)
            gfk_ref[:half, lanes] = mm(gt_top, fq)
            gfk_ref[half:, lanes] = mm(gt_bot, fq[half:])
            st_top = (nt(fk[:half], fq) * at_top).astype(BF16)
            st_bot = (nt(fk[half:], fq[half:]) * at_bot).astype(BF16)
            gv_parts.append(jnp.concatenate([mm(st_top, gn), mm(st_bot, gn[half:])], axis=0))
        gv_ref[:, pair_lanes] = gv_parts[0] + gv_parts[1]
    d = d_scr[...]
    gq_ref[...] = (0.5 * nt(d, map_scr[...])).astype(BF16)
    gm = tn(q_ref[...], d)
    for h in range(4):
        gmap_ref[64 * h : 64 * h + 64, :] = gm[64 * h : 64 * h + 64, 128 * h : 128 * h + 128]


def keys_back_kernel(k_ref, fk_ref, v_ref, gfk_ref, gv_ref, u0, u1, u2, u3, tail_ref, map_ref,
                     gk_ref, gvb_ref, gmap_ref, map_scr, up_scr, d_scr):
    j = pl.program_id(0)

    @pl.when(j == 0)
    def _():
        place_heads(up_scr, (u0, u1, u2, u3))

    fill_maps(map_scr, map_ref)
    ones = segment_ones(128)
    tail = tail_ref[...]
    for pair in range(2):
        pair_lanes = slice(128 * pair, 128 * pair + 128)
        v_pair = v_ref[:, pair_lanes]
        gv = gv_ref[:, pair_lanes]
        for side in range(2):
            h = 2 * pair + side
            lanes = slice(128 * h, 128 * h + 128)
            up = up_scr[4 * j + h]
            high, low = split(side_rows(up, side))
            fk = fk_ref[:, lanes]
            key_term = mm(v_pair, high) + mm(v_pair, low) + up[64:65]
            gfk = gfk_ref[:, lanes] + tail * key_term
            gv = gv + tail * (nt(fk, high) + nt(fk, low))
            d_scr[:, lanes] = features_back(fk.astype(F32), gfk, ones).astype(BF16)
        gvb_ref[:, pair_lanes] = gv.astype(BF16)
    d = d_scr[...]
    gk_ref[...] = (0.5 * nt(d, map_scr[...])).astype(BF16)
    gm = tn(k_ref[...], d)
    for h in range(4):
        gmap_ref[64 * h : 64 * h + 64, :] = gm[64 * h : 64 * h + 64, 128 * h : 128 * h + 128]


def inputs_back_kernel(gq_ref, gk_ref, gv_ref, w_ref, x_ref, gh_ref, gain_ref, gg_mlp_ref,
                       gmq_ref, gmk_ref, gx_ref, keep_ref, send_ref, acc, pack):
    j = pl.program_id(0)

    @pl.when(j == 0)
    def _():
        acc[...] = nt(gq_ref[...], w_ref[...])
        rows = gmq_ref.shape[0]
        low_half = iota(gmq_ref.shape, 1) < 64
        pack[:rows, :] = jnp.where(low_half, gmq_ref[...], pltpu.roll(gmk_ref[...], 64, 1))
        pack[rows:, :] = jnp.zeros((pack.shape[0] - rows, 128), F32)

    @pl.when(j == 1)
    def _():
        acc[...] += nt(gk_ref[...], w_ref[...])

    @pl.when(j == 2)
    def _():
        grad = acc[...] + nt(gv_ref[...], w_ref[...])
        normed, scale = moments(x_ref[...].astype(F32))
        gx_ref[...] = gh_ref[...] + norm_back(grad, normed, scale, gain_ref[...])
        gg = jnp.sum(grad * normed, axis=0, keepdims=True)
        rows = gmq_ref.shape[0]
        n = gg.shape[1] // 128
        for i in range(n):
            pack[rows + i : rows + i + 1, :] = gg[:, 128 * i : 128 * i + 128]
            pack[rows + n + i : rows + n + i + 1, :] = gg_mlp_ref[:, 128 * i : 128 * i + 128]
        for out, core in ((keep_ref, my_core()), (send_ref, 1 - my_core())):
            for c in range(n):
                start = core * (n * SMALL_ROWS) + c * SMALL_ROWS
                out[:, 128 * c : 128 * c + 128] = pack[pl.ds(pl.multiple_of(start, 8), SMALL_ROWS), :]


def add_kernel(a_ref, b_ref, out_ref):
    out_ref[...] = a_ref[...] + b_ref[...]


def unpack_kernel(kept_ref, other_ref, gmq_ref, gmk_ref, gains_ref, pack):
    n = kept_ref.shape[1] // 128
    for value, core in ((kept_ref[...], my_core()), (other_ref[...], 1 - my_core())):
        for c in range(n):
            start = core * (n * SMALL_ROWS) + c * SMALL_ROWS
            pack[pl.ds(pl.multiple_of(start, 8), SMALL_ROWS), :] = value[:, 128 * c : 128 * c + 128]
    heads = gmq_ref.shape[0]
    for h in range(heads):
        both = pack[64 * h : 64 * h + 64, :]
        gmq_ref[h] = both[:, :64]
        gmk_ref[h] = both[:, 64:]
    gains_ref[...] = pack[64 * heads : 64 * heads + 16, :]


ORDERS = ((0, 1, 2, 3), (1, 2, 0, 3), (2, 0, 1, 3))
SMALL_ORDER = (3, 0, 1, 2)


def send_kernel(kinds, x_ref, *refs):
    out_ref = refs[-1]
    for i, kind in enumerate(kinds):
        out_ref[i] = mm(x_ref[0, kind], refs[i][...])


def wave_kernel(plan, *refs):
    i = pl.program_id(0)

    @pl.when(i == 0)
    def _():
        for kept, got, at, count, send, base, keep in plan["folds"]:
            rows = refs[kept].shape[0] // count
            half = rows // 2
            for p in range(count):
                total = (refs[kept][rows * p : rows * p + rows, :]
                         + refs[got][at + rows * p : at + rows * p + rows, :])
                refs[send][base + half * p : base + half * p + half, :] = total[half:]
                refs[keep][half * p : half * p + half, :] = total[:half]
        for whence, out in plan["copies"]:
            refs[out][:, : refs[whence].shape[1]] = refs[whence][...]
        for kept, got, at, out, block in plan["ends"]:
            rows, width = refs[out].shape[0], refs[kept].shape[1]
            first, piece = block
            refs[out][:, width * first : width * first + width] = (
                refs[kept][rows * piece : rows * piece + rows, :]
                + refs[got][at + rows * piece : at + rows * piece + rows, :]
            )
        for kept, got, at, send, base, keep in plan["smalls"]:
            rows = refs[kept].shape[0]
            total = refs[kept][...] + refs[got][at : at + rows, :]
            refs[keep][...] = total
            refs[send][base : base + rows, :] = total

    for step, (x, entry, y, r, send, base, keep, at) in enumerate(plan["joins"]):

        @pl.when(i == step)
        def _():
            value = mm(refs[x][1, entry], refs[y][...]) + refs[r][0]
            half = value.shape[0] // 2
            refs[send][base : base + half, :] = value[half:]
            refs[keep][at : at + half, :] = value[:half]


def core_hop(v):
    return lax.ppermute(v, "batch", [(0, 1), (1, 0)])


def local(inputs, w_qkv, w_out, w_fc, w_proj, map_query, map_key, gain_attn, gain_mlp,
          starts, key_mask, cotangent):
    T, D = inputs.shape[1], inputs.shape[2]
    H = map_query.shape[0]
    FF = w_fc.shape[1]
    n_seq = lax.axis_size("seq")
    planes = n_seq // 4
    quads = H // 4
    QW, FW = 4 * 64, 4 * 128
    half_rows = D // 2
    per = H // 4
    seq = lax.axis_index("seq")
    tok = None
    x, cot = inputs[0], cotangent[0]
    gain_a, gain_m = gain_attn.reshape(1, D), gain_mlp.reshape(1, D)
    direct = n_seq == 16

    def hop(v, bit):
        return lax.ppermute(v, "seq", [(i, i ^ (1 << bit)) for i in range(n_seq)])

    def to_member(v, k):
        return lax.ppermute(v, "seq", [(i, i ^ k) for i in range(n_seq)])

    def shift(v, by):
        return lax.ppermute(v, "seq", [(i, (i + by) % n_seq) for i in range(n_seq)])

    qcol = pl.BlockSpec((T, QW), lambda j: (0, j))
    fcol = pl.BlockSpec((T, FW), lambda j: (0, j))
    col128 = whole((T, 128))
    square = whole((T, T))
    full = whole((T, D))
    row = whole((1, D))
    maps = pl.BlockSpec((4, 64, 64), lambda j: (j, 0, 0))
    piece = (per, STATE_ROWS, 128)
    piece_spec = whole(piece)
    map_scr = pltpu.VMEM((QW, FW), BF16)
    state_scr = pltpu.VMEM((H, STATE_ROWS, 128), F32)

    def w_cols(part):
        return pl.BlockSpec((D, QW), lambda j: (0, part * quads + j))

    (attn, k, v, fk, s0, s1, s2, s3, allow, allow_t, tail, contin), tok = run(
        keys_kernel, tok, (quads,),
        [(Held(x), full), (gain_a, row), (Held(w_qkv), w_cols(1)), (Held(w_qkv), w_cols(2)), (Held(map_key), maps),
         (Held(key_mask), whole((1, T))), (starts, pl.BlockSpec(memory_space=pltpu.SMEM))],
        [((T, D), BF16, full), ((T, D), BF16, qcol), ((T, D), BF16, qcol), ((T, 2 * D), BF16, fcol)]
        + [(piece, F32, piece_spec)] * 4
        + [((T, T), F32, square)] * 2 + [((T, 128), F32, col128)] * 2,
        [map_scr, state_scr], us=8.0)

    def plane_exchange(pieces):
        return [pieces[0]] + [to_member(pieces[k], k) for k in range(1, 4)]

    def plane_total(own, tok):
        (total,), tok = run(
            plane_sum_kernel, tok, (1,), [(p, piece_spec) for p in own], [(piece, F32, piece_spec)])
        return total, tok

    def across(total, backward):
        if planes <= 4:
            return [shift(total, (-4 if backward else 4) * i) for i in range(1, planes)]
        every = lax.all_gather(total, "seq").reshape((planes, 4) + piece)
        mine = lax.dynamic_index_in_dim(every, seq & 3, 1, keepdims=False)
        place = jnp.arange(planes)
        want = place > (seq >> 2) if backward else place < (seq >> 2)
        return [jnp.sum(jnp.where(want[:, None, None, None], mine, 0.0), axis=0)]

    def scanned(own, others, backward, tok):
        return run(
            functools.partial(scan_kernel, backward, planes if planes <= 4 else None), tok, (1,),
            [(p, piece_spec) for p in own + others], [(piece, F32, piece_spec)] * 4)

    def later(own, others, tok):
        pair = (2 * per,) + piece[1:]
        (mine, x_pair, y_one), tok = run(
            functools.partial(later_kernel, planes if planes <= 4 else None), tok, (1,),
            [(p, piece_spec) for p in own + others],
            [(piece, F32, piece_spec), (pair, F32, whole(pair)), (piece, F32, piece_spec)])
        x_pair, y_one = to_member(x_pair, 1), to_member(y_one, 2)
        return [mine, x_pair, y_one, to_member(x_pair[per:], 2)], tok

    def turn(x, kinds, tok):
        shape = (2, len(kinds), half_rows, T)
        if not direct:
            return jnp.zeros(shape, BF16), tok
        (out,), tok = run(
            functools.partial(turn_kernel, kinds), tok, (1,), [(x, full)], [(shape, BF16, whole(shape))],
            [pltpu.VMEM((half_rows, T), F32)])
        return out, tok

    own = plane_exchange([s0, s1, s2, s3])

    (q, fq, nd), tok = run(
        queries_kernel, tok, (quads,),
        [(attn, full), (w_qkv, w_cols(0)), (map_query, maps), (fk, fcol), (v, qcol), (allow, square)],
        [((T, D), BF16, qcol), ((T, 2 * D), BF16, fcol), ((T, 2 * D), F32, fcol)],
        [map_scr], us=9.0)
    total, tok = plane_total(own, tok)
    others = across(total, False)
    (ga,), tok = run(
        act_back_kernel, tok, (FF // D,), [(cot, full), (w_proj, pl.BlockSpec((D, D), lambda j: (j, 0)))],
        [((T, FF), F32, whole((T, FF)), Near)], us=4.0)
    carried, tok = scanned(own, others, False, tok)
    carry = plane_exchange(carried)
    cot_t, tok = turn(cot, (0, 1, 2), tok)
    attn_t, tok = turn(attn, (0, 1, 2), tok)

    (mixed, mf, rden, hidden, mlp_in), tok = run(
        mix_kernel, tok, (quads,),
        [(x, full), (nd, fcol), (fq, fcol)] + [(c, piece_spec) for c in carry]
        + [(contin, col128), (w_out, pl.BlockSpec((QW, D), lambda j: (j, 0))), (gain_m, row)],
        [((T, D), BF16, qcol), ((T, D), F32, qcol), ((T, D), F32, qcol), ((T, D), F32, full),
         ((T, D), BF16, full)],
        [state_scr], us=4.5)
    mlp_t, tok = turn(mlp_in, (0, 1, 2), tok)

    n_ff = FF // D
    turned_spec = whole((2, 3, half_rows, T))
    send_shape = (2, n_ff, half_rows, D)
    (act, gp, send_mlp), tok = run(
        mlp_kernel, tok, (n_ff,),
        [(mlp_in, full), (ga, columns(T, D)), (mlp_t, turned_spec), (cot_t, turned_spec), (Held(w_fc), columns(D, D))],
        [((T, FF), BF16, columns(T, D), Near)] * 2
        + [(send_shape, F32, pl.BlockSpec((2, 1, half_rows, D), lambda j: (0, j, 0, 0)), True)], us=10.0)
    if direct:
        recv_mlp = core_hop(send_mlp.array).reshape(2 * n_ff, half_rows, D)
    (output, gh, gh_low, gg_mlp), tok = run(
        mlp_out_kernel, tok, (quads,),
        [(act, whole((T, FF))), (gp, whole((T, FF))), (Held(w_fc), pl.BlockSpec((QW, FF), lambda j: (j, 0))),
         (Held(w_proj), columns(FF, QW)), (hidden, qcol), (hidden, full), (Held(cot), full), (gain_m, row)],
        [((T, D), F32, qcol), ((T, D), F32, full), ((T, D), BF16, full), ((1, D), F32, row)],
        [pltpu.VMEM((quads, T, QW), F32)], us=8.0)
    def send_half(x_t, kinds, ys, tok):
        shape = (len(kinds), half_rows, D)
        (out,), tok = run(
            functools.partial(send_kernel, kinds), tok, (1,),
            [(x_t, whole(x_t.shape))] + [(y, full) for y in ys], [(shape, F32, whole(shape))], us=30.0)
        return core_hop(out), tok

    class Group:
        def __init__(self, counts, layout, widths):
            self.counts, self.layout, self.widths = counts, layout, widths
            self.stage, self.small = -1, None

    def wave(folds, join, tok, us=30.0):
        ins, outs, sends = [], [], {}
        plan = {"folds": [], "ends": [], "smalls": [], "joins": [], "copies": []}
        after = []

        def take(array, spec=None):
            for n, (other, other_spec) in enumerate(ins):
                if other is array and spec is None:
                    return n
            ins.append((array, spec or whole(array.shape)))
            return len(ins) - 1

        def place(bit, rows):
            base = sends.get(bit, 0)
            sends[bit] = base + rows
            return base

        def give(shape, put, not_last=True):
            outs.append((shape, F32, whole(shape), not_last and Near))
            after.append((len(outs) - 1, put))
            return ("out", len(outs) - 1)

        steps = 1
        for g in folds:
            g.stage += 1
            if g.stage == 4:
                rows = half_rows // 16
                g.result = [None] * len(g.widths)
                made = []
                if g is main:
                    plan["copies"] = [(take(early.result[0]), ("out", len(outs)))]
                for n, width in enumerate(g.widths):
                    def put(array, n=n, g=g):
                        g.result[n] = array
                    made.append(give((rows, width), put, False))
                n = 0
                for kind in range(3):
                    if g.counts[kind] == 0:
                        continue
                    got, at = g.got[kind]
                    for p in range(g.counts[kind]):
                        out, block = g.layout[n]
                        plan["ends"].append((take(g.keeps[kind]), take(got), at, made[out], (block, p)))
                        n += 1
            else:
                old_keeps, g.keeps = g.keeps, [None] * 3
                old_got, g.got = g.got, [None] * 3
                for kind in range(3):
                    if g.counts[kind] == 0:
                        continue
                    bit = ORDERS[kind][g.stage]
                    rows = old_keeps[kind].shape[0] // 2
                    base = place(bit, rows)
                    def put(array, kind=kind, g=g):
                        g.keeps[kind] = array
                    keep = give((rows, D), put)
                    got, at = old_got[kind]
                    plan["folds"].append(
                        (take(old_keeps[kind]), take(got), at, g.counts[kind], ("send", bit), base, keep))
                    g.got[kind] = (bit, base)
            if g.small is not None and g.stage < 4:
                got, at = g.small_got
                bit = SMALL_ORDER[g.stage]
                base = place(bit, SMALL_ROWS)
                def put(array, g=g):
                    g.small = array
                keep = give(small_shape, put)
                plan["smalls"].append((take(g.small), take(got), at, ("send", bit), base, keep))
                g.small_got = (bit, base)
        if join is not None:
            g, xs, ys, segments, small = join
            g.stage = 0
            g.keeps, g.got, offset = [None] * 3, [None] * 3, [0, 0, 0]
            at_x = [take(x) for x in xs]
            at_y, at_r = [], []
            for n, (y, r, block, y_block) in enumerate(ys):
                mine = [i for i, seg in enumerate(segments) if seg[2] == n]
                first, count = mine[0], len(mine)
                at_y.append(take(y, pl.BlockSpec(
                    (T, D), lambda i, first=first, count=count, block=y_block:
                    (0, block + jnp.clip(i - first, 0, count - 1)))))
                at_r.append(take(r, pl.BlockSpec(
                    (1, half_rows, D), lambda i, first=first, count=count, block=block:
                    (block + jnp.clip(i - first, 0, count - 1), 0, 0))))
            half = half_rows // 2
            for kind in range(3):
                if g.counts[kind] == 0:
                    continue
                bit = ORDERS[kind][0]
                g.got[kind] = (bit, place(bit, half * g.counts[kind]))
                def put(array, kind=kind, g=g):
                    g.keeps[kind] = array
                g.keeps[kind] = give((half * g.counts[kind], D), put)
            for x, entry, y, kind in segments:
                bit, base = g.got[kind]
                plan["joins"].append(
                    (at_x[x], entry, at_y[y], at_r[y], ("send", bit), base + offset[kind], g.keeps[kind], offset[kind]))
                offset[kind] += half
            steps = len(segments)
            if small is not None:
                bit = SMALL_ORDER[0]
                base = place(bit, SMALL_ROWS)
                def put(array, g=g):
                    g.small = array
                keep = give(small_shape, put)
                plan["smalls"].append((take(small[0]), take(small[1]), 0, ("send", bit), base, keep))
                g.small, g.small_got = True, (bit, base)
        first_send = len(outs)
        bits = sorted(sends)
        for bit in bits:
            outs.append(((sends[bit], D), F32, whole((sends[bit], D)), Near))
        n_in = len(ins)

        def ref(item):
            if isinstance(item, tuple) and item[0] == "out":
                return n_in + item[1]
            if isinstance(item, tuple) and item[0] == "send":
                return n_in + first_send + bits.index(item[1])
            return item

        plan = {name: tuple(tuple(ref(x) for x in entry) for entry in entries) for name, entries in plan.items()}
        results, tok = run(functools.partial(wave_kernel, plan), tok, (steps,), ins, outs, us=us, extra=9)
        for n, put in after:
            put(results[n])
        moved = {bit: Near(hop(results[first_send + n].array, bit)) for n, bit in enumerate(bits)}
        for g in folds + ([join[0]] if join else []):
            if g.stage < 4:
                g.got = [item and (moved[item[0]], item[1]) for item in g.got]
                if g.small is not None:
                    g.small_got = (moved[g.small_got[0]], g.small_got[1])
        return tok

    small_shape = (SMALL_ROWS, D)
    early = Group((1, 1, 1), [(0, i) for i in range(3)], (3 * D,))
    main = Group((2, 2, 1), [(0, n_ff - 1)] + [(1, i) for i in range(n_ff)], (FF, FF))
    wide = Group((1, 0, 0), [(0, 0)], (D,))
    last = Group((1, 1, 1), [(0, i) for i in range(3)], (3 * D,))
    if direct:
        tok = wave([], (early, [cot_t], [(act, recv_mlp, 0, 0)], [(0, kind, 0, kind) for kind in range(3)], None), tok, 4.0)

    (gn, gd, gd_t, s0, s1, s2, s3), tok = run(
        numer_back_kernel, tok, (quads,),
        [(gh_low, full), (w_out, pl.BlockSpec((QW, D), lambda j: (j, 0))), (mf, qcol), (rden, qcol),
         (fq, fcol), (contin, col128)],
        [((T, D), BF16, qcol), ((T, D), F32, qcol),
         ((8 * H, T), F32, pl.BlockSpec((32, T), lambda j: (j, 0)))] + [(piece, F32, piece_spec)] * 4,
        [state_scr], us=5.0)
    own = plane_exchange([s0, s1, s2, s3])
    if direct:
        tok = wave(
            [early],
            (main, [cot_t, mlp_t], [(act, recv_mlp, n_ff - 1, n_ff - 1), (gp, recv_mlp, n_ff, 0)],
             [(0, 0, 0, 0)] + [(1, kind, 1, kind) for kind in (0, 1, 1, 2)], None), tok, 7.0)
    total, tok = plane_total(own, tok)
    others = across(total, True)

    def fixed(shape, quad):
        return pl.BlockSpec(shape, lambda i: (0, quad))

    def fixed_rows(shape, quad):
        return pl.BlockSpec(shape, lambda i: (quad,) + (0,) * (len(shape) - 1))

    def scores_back(quad, before, tok):
        ins = [(q, fixed((T, QW), quad)), (fq, fixed((T, FW), quad)), (fk, fixed((T, FW), quad)),
               (v, fixed((T, QW), quad)), (gn, fixed((T, QW), quad)), (gd, fixed((T, QW), quad)),
               (gd_t, fixed_rows((32, T), quad))] + [(c, piece_spec) for c in carry]
        ins += [(allow, square), (allow_t, square), (contin, col128), (map_query, fixed_rows((4, 64, 64), quad))]
        aliases = {len(ins) + i: i for i in range(4)} if before else None
        ins += [(a, ANYWHERE) for a in before]
        return run(
            functools.partial(scores_back_kernel, quad), tok, (1,), ins,
            [((T, D), BF16, fixed((T, QW), quad)), ((T, 2 * D), F32, fixed((T, FW), quad)),
             ((T, D), F32, fixed((T, QW), quad)), ((D, 128), F32, fixed_rows((QW, 128), quad))],
            [map_scr, state_scr, pltpu.VMEM((T, FW), BF16)], extra=12, aliases=aliases, us=4.5)

    backs, tok = scores_back(0, [], tok)
    backs, tok = scores_back(1, backs, tok)
    backs, tok = scores_back(2, backs, tok)
    gq, gfk, gv_f, gmq = backs
    upstream, tok = later(own, others, tok)
    if direct:
        mixed_t, tok = turn(mixed, (0,), tok)
        recv_out, tok = send_half(mixed_t, (0,), [gh_low], tok)
        tok = wave(
            [early, main], (wide, [mixed_t], [(gh_low, recv_out, 0, 0)], [(0, 0, 0, 0)], None), tok, 2.0)

    (gk, gv, gmk), tok = run(
        keys_back_kernel, tok, (quads,),
        [(k, qcol), (fk, fcol), (v, qcol), (gfk, fcol), (gv_f, qcol)] + [(c, piece_spec) for c in upstream]
        + [(tail, col128), (map_key, maps)],
        [((T, D), BF16, qcol), ((T, D), BF16, qcol),
         ((D, 128), F32, pl.BlockSpec((QW, 128), lambda j: (j, 0)))],
        [map_scr, state_scr, pltpu.VMEM((T, FW), BF16)], us=60.0)
    if direct:
        recv_qkv, tok = send_half(attn_t, (0, 1, 2), [gq, gk, gv], tok)

    small_spec = whole(small_shape)
    packed = 2 * SMALL_ROWS * (D // 128)
    (gx, keep, send), tok = run(
        inputs_back_kernel, tok, (3,),
        [(gq, full), (gk, full), (gv, full), (w_qkv, columns(D, D)), (x, full), (gh, full), (gain_a, row),
         (gg_mlp, row), (gmq, whole((D, 128))), (gmk, whole((D, 128)))],
        [((T, D), F32, full)] + [(small_shape, F32, small_spec)] * 2,
        [pltpu.VMEM((T, D), F32), pltpu.VMEM((packed, 128), F32)], us=60.0)

    got = core_hop(send)
    if direct:
        tok = wave(
            [], (last, [attn_t], [(gq, recv_qkv, 0, 0), (gk, recv_qkv, 1, 0), (gv, recv_qkv, 2, 0)],
                 [(0, kind, kind, kind) for kind in range(3)], (keep, got)), tok, 4.0)
        tok = wave([early, main, wide], None, tok)
        tok = wave([last], None, tok)
        tok = wave([early, main, wide], None, tok)
        tok = wave([last], None, tok)
        tok = wave([main, wide], None, tok)
        tok = wave([last], None, tok)
        (mine,), tok = run(
            add_kernel, tok, (1,), [(last.small, small_spec), (last.small_got[0], small_spec)],
            [(small_shape, F32, small_spec, Near)], us=0.1)
        got = core_hop(mine.array)
        tok = wave([wide, last], None, tok)
        (grad_w_qkv,) = last.result
        grad_proj_rows, grad_w_fc = main.result
        (grad_w_out,) = wide.result
    else:
        mine = lax.psum(keep + got, "seq")
        got = core_hop(mine)
        summed = lax.psum_scatter(
            jnp.concatenate(
                [tn(attn, gq), tn(attn, gk), tn(attn, gv), tn(mixed, gh_low), tn(mlp_in, gp.array), tn(cot, act.array)],
                axis=1,
            ),
            ("batch", "seq"), scatter_dimension=0, tiled=True)
        grad_w_qkv = summed[:, : 3 * D]
        grad_w_out = summed[:, 3 * D : 4 * D]
        grad_w_fc = summed[:, 4 * D : 4 * D + FF]
        grad_proj_rows = summed[:, 4 * D + FF :]

    heads_shape = (H, 64, 64)
    (grad_map_query, grad_map_key, gains), tok = run(
        unpack_kernel, tok, (1,), [(mine, small_spec), (got, small_spec)],
        [(heads_shape, F32, whole(heads_shape))] * 2 + [((16, 128), F32, whole((16, 128)))],
        [pltpu.VMEM((packed, 128), F32)], us=0.1)
    n = D // 128
    return (
        output[None],
        gx[None],
        grad_w_qkv,
        grad_w_out,
        grad_w_fc,
        grad_proj_rows.T,
        grad_map_query,
        grad_map_key,
        gains[:n].reshape(D),
        gains[n : 2 * n].reshape(D),
    )


def solution(mesh):
    tokens = P("batch", "seq", None)
    flags = P("batch", "seq")
    rows = P(("batch", "seq"), None)
    return jax.shard_map(
        local,
        mesh=mesh,
        in_specs=(tokens,) + (P(),) * 8 + (flags, flags, tokens),
        out_specs=(tokens, tokens, rows, rows, rows, P(None, ("batch", "seq")), P(), P(), P(), P()),
        check_vma=False,
    )
```

```python
import functools

import jax
import jax.numpy as jnp
from jax import lax
from jax.experimental import pallas as pl
from jax.experimental.pallas import tpu as pltpu
from jax.sharding import PartitionSpec as P

EPSILON = 1e-05
F32 = jnp.float32
BF16 = jnp.bfloat16
STATE_ROWS = 72
SMALL_ROWS = 72
MIB = 1024 * 1024


def mm(a, b):
    return lax.dot_general(a, b, (((1,), (0,)), ((), ())), preferred_element_type=F32)


def nt(a, b):
    return lax.dot_general(a, b, (((1,), (1,)), ((), ())), preferred_element_type=F32)


def tn(a, b):
    return lax.dot_general(a, b, (((0,), (0,)), ((), ())), preferred_element_type=F32)


def split(v):
    high = v.astype(BF16)
    return high, (v - high.astype(F32)).astype(BF16)


def iota(shape, dim):
    return lax.broadcasted_iota(jnp.int32, shape, dim)


def segment_ones(width):
    shape = (width, width)
    return (iota(shape, 0) // 64 == iota(shape, 1) // 64).astype(BF16)


def segment_sum(v, ones):
    high, low = split(v)
    return mm(high, ones) + mm(low, ones)


def moments(x):
    centre = jnp.mean(x, axis=-1, keepdims=True)
    offsets = x - centre
    variance = jnp.mean(offsets * offsets, axis=-1, keepdims=True)
    scale = lax.rsqrt(variance + EPSILON)
    return offsets * scale, scale


def norm_back(grad, normed, scale, gain):
    dn = grad * gain
    first = jnp.mean(dn, axis=-1, keepdims=True)
    second = jnp.mean(dn * normed, axis=-1, keepdims=True)
    return (dn - first - normed * second) * scale


def fill_maps(scr, map_ref):
    scr[...] = jnp.zeros(scr.shape, scr.dtype)
    for h in range(4):
        m = map_ref[h].astype(F32)
        scr[64 * h : 64 * h + 64, 128 * h : 128 * h + 128] = jnp.concatenate(
            [m, -m], axis=1
        ).astype(scr.dtype)


def half_sums(v, low_half):
    top = jnp.sum(jnp.where(low_half, v, 0.0), axis=1, keepdims=True)
    bottom = jnp.sum(jnp.where(low_half, 0.0, v), axis=1, keepdims=True)
    return jnp.where(low_half, top, bottom)


def features(pre):
    low_half = iota(pre.shape, 1) < 64
    top = jnp.max(jnp.where(low_half, pre, -jnp.inf), axis=1, keepdims=True)
    bottom = jnp.max(jnp.where(low_half, -jnp.inf, pre), axis=1, keepdims=True)
    e = jnp.exp(pre - jnp.where(low_half, top, bottom))
    return e / half_sums(e, low_half)


def features_back(feat, grad, ones):
    low_half = iota(feat.shape, 1) < 64
    weighted = feat * grad
    mass = mm(feat.astype(BF16), ones)
    part = weighted - feat * (half_sums(weighted, low_half) / mass)
    return part - pltpu.roll(part, 64, 1)


def whole(shape):
    return pl.BlockSpec(shape, lambda *_: (0,) * len(shape))


def columns(rows, width):
    return pl.BlockSpec((rows, width), lambda j: (0, j))


ANYWHERE = pl.BlockSpec(memory_space=pl.ANY)


def my_core():
    return lax.axis_index("batch")


def my_seq():
    return lax.axis_index("seq")


def nbytes(shape, dtype):
    total = jnp.dtype(dtype).itemsize
    for n in shape:
        total *= n
    return total


class Held:
    def __init__(self, array):
        self.array, self.shape, self.dtype = array, array.shape, array.dtype


class Near(Held):
    pass


def run(kernel, tok, grid, ins, outs, scratch=(), extra=3, aliases=None, us=1.0):
    n_in, n_out = len(ins), len(outs)
    linked = tok is not None
    outs = [tuple(out) + (False,) * (4 - len(out)) for out in outs]

    def body(*refs):
        kernel(*refs[:n_in], *refs[n_in + linked : n_in + linked + n_out], *refs[n_in + linked + n_out + 1 :])

    held = 0
    arrays = []
    for array, spec in ins:
        near = isinstance(array, Near)
        if spec.block_shape is not None and not (near and spec.block_shape == array.shape):
            held += (1 if spec.block_shape == array.shape else 2) * nbytes(spec.block_shape, array.dtype)
        if isinstance(array, Held):
            array = pltpu.with_memory_space_constraint(array.array, pltpu.VMEM if near else pltpu.HBM)
        arrays.append(array)
    for shape, dtype, spec, stays in outs:
        if not (stays is Near and spec.block_shape == shape):
            held += (1 if spec.block_shape == shape else 2) * nbytes(spec.block_shape, dtype)
    for item in scratch:
        held += nbytes(item.shape, item.dtype)
    result = pl.pallas_call(
        body,
        grid=grid,
        in_specs=[spec for _, spec in ins] + [ANYWHERE] * linked,
        out_specs=[spec for _, _, spec, _ in outs] + [ANYWHERE],
        scratch_shapes=list(scratch),
        out_shape=[
            pltpu.VMEM(shape, dtype) if stays is Near
            else pltpu.HBM(shape, dtype) if stays else jax.ShapeDtypeStruct(shape, dtype)
            for shape, dtype, _, stays in outs
        ]
        + [jax.ShapeDtypeStruct((8, 128), F32)],
        input_output_aliases=aliases or {},
        cost_estimate=pl.CostEstimate(flops=int(us * 1.15e9), bytes_accessed=0, transcendentals=0),
        compiler_params=pltpu.CompilerParams(vmem_limit_bytes=min(held + extra * MIB, 60 * MIB)),
    )(*arrays, *([tok] if linked else []))
    results = [Near(r) if out[3] is Near else Held(r) if out[3] else r for r, out in zip(result, outs)]
    return results, result[-1]


def keys_kernel(x_ref, gain_ref, wk_ref, wv_ref, map_ref, mask_ref, starts_ref,
                attn_ref, k_ref, v_ref, fk_ref, p0, p1, p2, p3,
                allow_ref, allow_t_ref, tail_ref, contin_ref,
                map_scr, state_scr):
    j = pl.program_id(0)
    tokens = x_ref.shape[0]
    n_flags = starts_ref.shape[1]
    unit = tokens // n_flags

    def seg(shape, dim):
        place = iota(shape, dim)
        total = jnp.zeros(shape, jnp.int32)
        for u in range(n_flags):
            total = total + jnp.where(place >= unit * u, starts_ref[0, u], 0)
        return total

    @pl.when(j == 0)
    def _():
        normed, _ = moments(x_ref[...].astype(F32))
        attn_ref[...] = (normed * gain_ref[...].reshape(1, -1)).astype(BF16)
        last = starts_ref[0, 0]
        for u in range(1, n_flags):
            last = last + starts_ref[0, u]
        mask_row = mask_ref[...].astype(F32)
        mask_col = jnp.transpose(jnp.broadcast_to(mask_row, (128, tokens)))
        seg_col = seg((tokens, 128), 0)
        tail_ref[...] = jnp.where(seg_col == last, mask_col, 0.0)
        contin_ref[...] = jnp.where(seg_col == 0, 1.0, 0.0)
        square = (tokens, tokens)
        same = seg(square, 0) == seg(square, 1)
        allow_ref[...] = jnp.where(same & (iota(square, 1) <= iota(square, 0)), mask_row, 0.0)
        wide_mask = jnp.concatenate([mask_col] * (tokens // 128), axis=1)
        allow_t_ref[...] = jnp.where(same & (iota(square, 0) <= iota(square, 1)), wide_mask, 0.0)

    fill_maps(map_scr, map_ref)
    attn = attn_ref[...]
    k4 = mm(attn, wk_ref[...]).astype(BF16)
    v4 = mm(attn, wv_ref[...]).astype(BF16)
    k_ref[...] = k4
    v_ref[...] = v4
    pre = mm(k4, map_scr[...])
    ones = segment_ones(128)
    v_t = jnp.transpose(v4.astype(F32)).astype(BF16)
    tail = tail_ref[...]
    row_ones = jnp.ones((16, tokens), BF16)
    for h in range(4):
        feat = features(pre[:, 128 * h : 128 * h + 128]).astype(BF16)
        fk_ref[:, 128 * h : 128 * h + 128] = feat
        kept = (feat.astype(F32) * tail).astype(BF16)
        rows = jnp.concatenate([v_t[64 * h : 64 * h + 64], row_ones], axis=0)
        state_scr[4 * j + h] = mm(rows, kept)[0:STATE_ROWS]

    @pl.when(j == pl.num_programs(0) - 1)
    def _():
        for k, piece in enumerate((p0, p1, p2, p3)):
            n = piece.shape[0]
            piece[...] = state_scr[pl.ds(((my_seq() & 3) ^ k) * n, n)]


def queries_kernel(attn_ref, wq_ref, map_ref, fk_ref, v_ref, allow_ref,
                   q_ref, fq_ref, nd_ref, map_scr):
    tokens = attn_ref.shape[0]
    half = tokens // 2
    fill_maps(map_scr, map_ref)
    q4 = mm(attn_ref[...], wq_ref[...]).astype(BF16)
    q_ref[...] = q4
    pre = mm(q4, map_scr[...])
    ones = segment_ones(128)
    low_half = iota((tokens, 128), 1) < 64
    for h in range(4):
        lanes = slice(128 * h, 128 * h + 128)
        feat = features(pre[:, lanes]).astype(BF16)
        fq_ref[:, lanes] = feat
        fk = fk_ref[:, lanes]
        pair = v_ref[:, 128 * (h // 2) : 128 * (h // 2) + 128].astype(F32)
        if h % 2:
            pair = pltpu.roll(pair, 64, 1)
        wide = jnp.where(low_half, pair, 1.0).astype(BF16)
        first = nt(feat[:half], fk[:half]) * allow_ref[:half, :half]
        nd_ref[:half, lanes] = mm(first.astype(BF16), wide[:half])
        second = nt(feat[half:], fk) * allow_ref[half:, :]
        nd_ref[half:, lanes] = mm(second.astype(BF16), wide)


def plane_sum_kernel(*refs):
    *pieces, out = refs
    total = pieces[0][...]
    for piece in pieces[1:]:
        total = total + piece[...]
    out[...] = total


def scan_kernel(backward, planes, *refs):
    own = refs[:4]
    others = refs[4:-4]
    outs = refs[-4:]
    member, plane = my_seq() & 3, my_seq() >> 2
    total = jnp.zeros(own[0].shape, F32)
    for i, other in enumerate(others):
        if planes is None:
            total = total + other[...]
        else:
            there = plane + i + 1 < planes if backward else plane - i - 1 >= 0
            total = total + jnp.where(there, other[...], 0.0)
    for k, out in enumerate(outs):
        value = total
        target = member ^ k
        for i, piece in enumerate(own):
            source = member ^ i
            counts = source > target if backward else source < target
            value = value + jnp.where(counts, piece[...], 0.0)
        out[...] = value


def later_kernel(planes, own0, own1, own2, own3, *refs):
    own, others, (mine, x_pair, y_one) = (own0, own1, own2, own3), refs[:-3], refs[-3:]
    member, plane = my_seq() & 3, my_seq() >> 2
    total = jnp.zeros(own0.shape, F32)
    for i, other in enumerate(others):
        if planes is None:
            total = total + other[...]
        else:
            total = total + jnp.where(plane + i + 1 < planes, other[...], 0.0)
    n = own0.shape[0]
    for k in range(4):
        value = total
        for i, piece in enumerate(own):
            value = value + jnp.where((member ^ i) > (member ^ k), piece[...], 0.0)
        if k == 0:
            mine[...] = value
        elif k == 2:
            y_one[...] = value
        else:
            x_pair[n * (k // 2) : n * (k // 2) + n] = value


def place_heads(scr, pieces):
    for k, piece in enumerate(pieces):
        n = piece.shape[0]
        scr[pl.ds(((my_seq() & 3) ^ k) * n, n)] = piece[...]


def mix_kernel(x_ref, nd_ref, fq_ref, c0, c1, c2, c3, contin_ref, wo_ref, gain_ref,
               mixed_ref, mf_ref, rden_ref, hidden_ref, mlp_ref, carry_scr):
    j = pl.program_id(0)
    tokens = x_ref.shape[0]
    low_half = iota((tokens, 128), 1) < 64

    @pl.when(j == 0)
    def _():
        place_heads(carry_scr, (c0, c1, c2, c3))
        hidden_ref[...] = x_ref[...].astype(F32)

    contin = contin_ref[...]
    for pair in range(2):
        quotients, inverses = [], []
        for side in range(2):
            h = 2 * pair + side
            lanes = slice(128 * h, 128 * h + 128)
            carry = carry_scr[4 * j + h]
            wide = jnp.concatenate([carry[:64], jnp.broadcast_to(carry[64:65], (64, 128))], axis=0)
            high, low = split(wide)
            fq = fq_ref[:, lanes]
            nd = nd_ref[:, lanes] + contin * (nt(fq, high) + nt(fq, low))
            inverse = 1.0 / nd
            turned = pltpu.roll(inverse, 64, 1)
            quotient = nd * turned
            if side:
                quotients.append(pltpu.roll(quotient, 64, 1))
                inverses.append(inverse)
            else:
                quotients.append(quotient)
                inverses.append(turned)
        lanes = slice(128 * pair, 128 * pair + 128)
        mf = jnp.where(low_half, *quotients)
        mf_ref[:, lanes] = mf
        mixed_ref[:, lanes] = mf.astype(BF16)
        rden_ref[:, lanes] = jnp.where(low_half, *inverses)
    hidden_ref[...] += mm(mixed_ref[...], wo_ref[...])

    @pl.when(j == pl.num_programs(0) - 1)
    def _():
        normed, _ = moments(hidden_ref[...])
        mlp_ref[...] = (normed * gain_ref[...].reshape(1, -1)).astype(BF16)


GELU_A, GELU_C = 0.044715, 0.7978845608028654


def turn_kernel(kinds, x_ref, out_ref, scr):
    rows, half = out_ref.shape[2] // 16, out_ref.shape[2]
    for side in range(2):
        core = my_core() if side else 1 - my_core()
        turned = jnp.transpose(
            x_ref[:, pl.ds(pl.multiple_of(core * half, 128), half)].astype(F32)
        )
        for at, kind in enumerate(kinds):
            for g in range(16):
                place = g ^ my_seq()
                spot = 0
                for depth, bit in enumerate(ORDERS[kind]):
                    spot = spot + (((place >> bit) & 1) << (3 - depth))
                scr[pl.ds(pl.multiple_of(spot * rows, 8), rows), :] = turned[rows * g : rows * g + rows]
            out_ref[side, at] = scr[...].astype(BF16)


def act_back_kernel(cot_ref, wp_ref, ga_ref):
    width = wp_ref.shape[0]
    start = pl.multiple_of(pl.program_id(0) * width, 128)
    ga_ref[:, pl.ds(start, width)] = nt(cot_ref[...], wp_ref[...])


def mlp_kernel(mlp_ref, ga_ref, mlp_t, cot_t, wf_ref, act_ref, gp_ref, send_ref):
    j = pl.program_id(0)
    tokens, width = mlp_ref.shape[0], wf_ref.shape[1]
    lanes = slice(0, width)
    step = tokens // 4
    for r in range(4):
        rows = slice(step * r, step * r + step)
        u = mm(mlp_ref[rows, :], wf_ref[...])
        square = u * u
        t = jnp.tanh(GELU_C * (u + GELU_A * (u * square)))
        half = 0.5 * (1.0 + t)
        act_ref[rows, lanes] = (u * half).astype(BF16)
        slope = half + (0.5 * GELU_C) * u * (1.0 - t * t) * (1.0 + (3.0 * GELU_A) * square)
        gp_ref[rows, lanes] = (ga_ref[rows, lanes] * slope).astype(BF16)
    send_ref[0, 0] = mm(cot_t[0, j % 3], act_ref[:, lanes])
    send_ref[1, 0] = mm(mlp_t[0, (j + 1) // 2], gp_ref[:, lanes])


def mlp_out_kernel(act_ref, gp_ref, wf_ref, wp_ref, part_ref, hidden_ref, cot_ref, gain_ref,
                   out_ref, gh_ref, gh_low_ref, gg_ref, back_scr):
    j = pl.program_id(0)
    out_ref[...] = part_ref[...] + mm(act_ref[...], wp_ref[...])
    back_scr[j] = nt(gp_ref[...], wf_ref[...])

    @pl.when(j == pl.num_programs(0) - 1)
    def _():
        normed, scale = moments(hidden_ref[...])
        grad = jnp.concatenate([back_scr[i] for i in range(back_scr.shape[0])], axis=1)
        gg_ref[...] = jnp.sum(grad * normed, axis=0, keepdims=True)
        gh = cot_ref[...].astype(F32) + norm_back(grad, normed, scale, gain_ref[...].reshape(1, -1))
        gh_ref[...] = gh
        gh_low_ref[...] = gh.astype(BF16)


def numer_back_kernel(gh_ref, wo_ref, mf_ref, rden_ref, fq_ref, contin_ref,
                      gn_ref, gd_ref, gd_t_ref, p0, p1, p2, p3, state_scr):
    j = pl.program_id(0)
    gm = nt(gh_ref[...], wo_ref[...]) * rden_ref[...]
    gn_ref[...] = gm.astype(BF16)
    gd = -segment_sum(gm * mf_ref[...], segment_ones(256))
    gd_ref[...] = gd
    gn_t = jnp.transpose(gm).astype(BF16)
    gd_t = jnp.transpose(gd)
    contin = contin_ref[...]
    for h in range(4):
        rows = gd_t[64 * h : 64 * h + 8]
        gd_t_ref[8 * h : 8 * h + 8, :] = rows
        kept = (fq_ref[:, 128 * h : 128 * h + 128].astype(F32) * contin).astype(BF16)
        high, low = split(rows)
        both = jnp.concatenate([high.astype(F32), low.astype(F32)], axis=0).astype(BF16)
        sums = mm(jnp.concatenate([gn_t[64 * h : 64 * h + 64], both], axis=0), kept)
        state_scr[4 * j + h, 0:64, :] = sums[0:64]
        state_scr[4 * j + h, 64:72, :] = sums[64:72] + sums[72:80]

    @pl.when(j == pl.num_programs(0) - 1)
    def _():
        for k, piece in enumerate((p0, p1, p2, p3)):
            n = piece.shape[0]
            piece[...] = state_scr[pl.ds(((my_seq() & 3) ^ k) * n, n)]


def side_rows(state, side):
    zeros = jnp.zeros((64, 128), F32)
    rows = state[:64]
    return jnp.concatenate([zeros, rows] if side else [rows, zeros], axis=0)


def scores_back_kernel(j, q_ref, fq_ref, fk_ref, v_ref, gn_ref, gd_ref, gd_t_ref,
                       c0, c1, c2, c3, allow_ref, allow_t_ref, contin_ref, map_ref, *rest):
    gq_ref, gfk_ref, gv_ref, gmap_ref, map_scr, carry_scr, d_scr = rest[-7:]
    tokens = q_ref.shape[0]
    half = tokens // 2
    place_heads(carry_scr, (c0, c1, c2, c3))

    fill_maps(map_scr, map_ref)
    ones = segment_ones(128)
    low_half = iota((tokens, 128), 1) < 64
    contin = contin_ref[...]
    for pair in range(2):
        pair_lanes = slice(128 * pair, 128 * pair + 128)
        v_pair = v_ref[:, pair_lanes]
        gn_pair = gn_ref[:, pair_lanes].astype(F32)
        gd_pair = gd_ref[:, pair_lanes]
        gd_turned = pltpu.roll(gd_pair, 64, 1)
        gv_parts = []
        for side in range(2):
            h = 2 * pair + side
            lanes = slice(128 * h, 128 * h + 128)
            mine = ~low_half if side else low_half
            gn = jnp.where(mine, gn_pair, 0.0).astype(BF16)
            gd = jnp.where(mine, gd_pair, gd_turned)
            gd_row = gd_t_ref[8 * h : 8 * h + 1, :]
            fq, fk = fq_ref[:, lanes], fk_ref[:, lanes]
            gd_few = jnp.concatenate([gd] * (half // 128), axis=1)
            gd_many = jnp.concatenate([gd] * (tokens // 128), axis=1)
            g_top = ((nt(gn[:half], v_pair[:half]) + gd_few[:half]) * allow_ref[:half, :half]).astype(BF16)
            g_bot = ((nt(gn[half:], v_pair) + gd_many[half:]) * allow_ref[half:, :]).astype(BF16)
            carry = carry_scr[4 * j + h]
            high, low = split(side_rows(carry, side))
            inter = mm(gn, high) + mm(gn, low) + gd * carry[64:65]
            gfq = jnp.concatenate([mm(g_top, fk[:half]), mm(g_bot, fk)], axis=0) + contin * inter
            d_scr[:, lanes] = features_back(fq.astype(F32), gfq, ones).astype(BF16)

            at_top, at_bot = allow_t_ref[:half, :], allow_t_ref[half:, half:]
            gt_top = ((nt(v_pair[:half], gn) + gd_row) * at_top).astype(BF16)
            gt_bot = ((nt(v_pair[half:], gn[half:]) + gd_row[:, half:]) * at_bot).astype(BF16)
            gfk_ref[:half, lanes] = mm(gt_top, fq)
            gfk_ref[half:, lanes] = mm(gt_bot, fq[half:])
            st_top = (nt(fk[:half], fq) * at_top).astype(BF16)
            st_bot = (nt(fk[half:], fq[half:]) * at_bot).astype(BF16)
            gv_parts.append(jnp.concatenate([mm(st_top, gn), mm(st_bot, gn[half:])], axis=0))
        gv_ref[:, pair_lanes] = gv_parts[0] + gv_parts[1]
    d = d_scr[...]
    gq_ref[...] = (0.5 * nt(d, map_scr[...])).astype(BF16)
    gm = tn(q_ref[...], d)
    for h in range(4):
        gmap_ref[64 * h : 64 * h + 64, :] = gm[64 * h : 64 * h + 64, 128 * h : 128 * h + 128]


def keys_back_kernel(k_ref, fk_ref, v_ref, gfk_ref, gv_ref, u0, u1, u2, u3, tail_ref, map_ref,
                     gk_ref, gvb_ref, gmap_ref, map_scr, up_scr, d_scr):
    j = pl.program_id(0)

    @pl.when(j == 0)
    def _():
        place_heads(up_scr, (u0, u1, u2, u3))

    fill_maps(map_scr, map_ref)
    ones = segment_ones(128)
    tail = tail_ref[...]
    for pair in range(2):
        pair_lanes = slice(128 * pair, 128 * pair + 128)
        v_pair = v_ref[:, pair_lanes]
        gv = gv_ref[:, pair_lanes]
        for side in range(2):
            h = 2 * pair + side
            lanes = slice(128 * h, 128 * h + 128)
            up = up_scr[4 * j + h]
            high, low = split(side_rows(up, side))
            fk = fk_ref[:, lanes]
            key_term = mm(v_pair, high) + mm(v_pair, low) + up[64:65]
            gfk = gfk_ref[:, lanes] + tail * key_term
            gv = gv + tail * (nt(fk, high) + nt(fk, low))
            d_scr[:, lanes] = features_back(fk.astype(F32), gfk, ones).astype(BF16)
        gvb_ref[:, pair_lanes] = gv.astype(BF16)
    d = d_scr[...]
    gk_ref[...] = (0.5 * nt(d, map_scr[...])).astype(BF16)
    gm = tn(k_ref[...], d)
    for h in range(4):
        gmap_ref[64 * h : 64 * h + 64, :] = gm[64 * h : 64 * h + 64, 128 * h : 128 * h + 128]


def inputs_back_kernel(gq_ref, gk_ref, gv_ref, w_ref, x_ref, gh_ref, gain_ref, gg_mlp_ref,
                       gmq_ref, gmk_ref, gx_ref, keep_ref, send_ref, acc, pack):
    j = pl.program_id(0)

    @pl.when(j == 0)
    def _():
        acc[...] = nt(gq_ref[...], w_ref[...])
        rows = gmq_ref.shape[0]
        low_half = iota(gmq_ref.shape, 1) < 64
        pack[:rows, :] = jnp.where(low_half, gmq_ref[...], pltpu.roll(gmk_ref[...], 64, 1))
        pack[rows:, :] = jnp.zeros((pack.shape[0] - rows, 128), F32)

    @pl.when(j == 1)
    def _():
        acc[...] += nt(gk_ref[...], w_ref[...])

    @pl.when(j == 2)
    def _():
        grad = acc[...] + nt(gv_ref[...], w_ref[...])
        normed, scale = moments(x_ref[...].astype(F32))
        gx_ref[...] = gh_ref[...] + norm_back(grad, normed, scale, gain_ref[...].reshape(1, -1))
        gg = jnp.sum(grad * normed, axis=0, keepdims=True)
        rows = gmq_ref.shape[0]
        n = gg.shape[1] // 128
        for i in range(n):
            pack[rows + i : rows + i + 1, :] = gg[:, 128 * i : 128 * i + 128]
            pack[rows + n + i : rows + n + i + 1, :] = gg_mlp_ref[:, 128 * i : 128 * i + 128]
        for out, core in ((keep_ref, my_core()), (send_ref, 1 - my_core())):
            for c in range(n):
                start = core * (n * SMALL_ROWS) + c * SMALL_ROWS
                out[:, 128 * c : 128 * c + 128] = pack[pl.ds(pl.multiple_of(start, 8), SMALL_ROWS), :]


def add_kernel(a_ref, b_ref, out_ref):
    out_ref[...] = a_ref[...] + b_ref[...]


def unpack_kernel(kept_ref, other_ref, gmq_ref, gmk_ref, gains_ref, pack):
    n = kept_ref.shape[1] // 128
    for value, core in ((kept_ref[...], my_core()), (other_ref[...], 1 - my_core())):
        for c in range(n):
            start = core * (n * SMALL_ROWS) + c * SMALL_ROWS
            pack[pl.ds(pl.multiple_of(start, 8), SMALL_ROWS), :] = value[:, 128 * c : 128 * c + 128]
    heads = gmq_ref.shape[0]
    for h in range(heads):
        both = pack[64 * h : 64 * h + 64, :]
        gmq_ref[h] = both[:, :64]
        gmk_ref[h] = both[:, 64:]
    gains_ref[...] = pack[64 * heads : 64 * heads + 16, :]


ORDERS = ((0, 1, 2, 3), (1, 2, 0, 3), (2, 0, 1, 3))
SMALL_ORDER = (3, 0, 1, 2)


def send_kernel(kinds, x_ref, *refs):
    out_ref = refs[-1]
    for i, kind in enumerate(kinds):
        out_ref[i] = mm(x_ref[0, kind], refs[i][...])


def wave_kernel(plan, *refs):
    i = pl.program_id(0)

    @pl.when(i == 0)
    def _():
        for kept, got, at, count, send, base, keep in plan["folds"]:
            rows = refs[kept].shape[0] // count
            half = rows // 2
            for p in range(count):
                total = (refs[kept][rows * p : rows * p + rows, :]
                         + refs[got][at + rows * p : at + rows * p + rows, :])
                refs[send][base + half * p : base + half * p + half, :] = total[half:]
                refs[keep][half * p : half * p + half, :] = total[:half]
        for whence, out in plan["copies"]:
            refs[out][:, : refs[whence].shape[1]] = refs[whence][...]
        for kept, got, at, out, block in plan["ends"]:
            rows, width = refs[out].shape[0], refs[kept].shape[1]
            first, piece = block
            refs[out][:, width * first : width * first + width] = (
                refs[kept][rows * piece : rows * piece + rows, :]
                + refs[got][at + rows * piece : at + rows * piece + rows, :]
            )
        for kept, got, at, send, base, keep in plan["smalls"]:
            rows = refs[kept].shape[0]
            total = refs[kept][...] + refs[got][at : at + rows, :]
            refs[keep][...] = total
            refs[send][base : base + rows, :] = total

    for step, (x, entry, y, r, send, base, keep, at) in enumerate(plan["joins"]):

        @pl.when(i == step)
        def _():
            value = mm(refs[x][1, entry], refs[y][...]) + refs[r][0]
            half = value.shape[0] // 2
            refs[send][base : base + half, :] = value[half:]
            refs[keep][at : at + half, :] = value[:half]


def core_hop(v):
    return lax.ppermute(v, "batch", [(0, 1), (1, 0)])


def local(inputs, w_qkv, w_out, w_fc, w_proj, map_query, map_key, gain_attn, gain_mlp,
          starts, key_mask, cotangent):
    T, D = inputs.shape[1], inputs.shape[2]
    H = map_query.shape[0]
    FF = w_fc.shape[1]
    n_seq = lax.axis_size("seq")
    planes = n_seq // 4
    quads = H // 4
    QW, FW = 4 * 64, 4 * 128
    half_rows = D // 2
    per = H // 4
    seq = lax.axis_index("seq")
    tok = None
    x, cot = inputs[0], cotangent[0]
    gain_a, gain_m = gain_attn, gain_mlp
    direct = n_seq == 16

    def hop(v, bit):
        return lax.ppermute(v, "seq", [(i, i ^ (1 << bit)) for i in range(n_seq)])

    def to_member(v, k):
        return lax.ppermute(v, "seq", [(i, i ^ k) for i in range(n_seq)])

    def shift(v, by):
        return lax.ppermute(v, "seq", [(i, (i + by) % n_seq) for i in range(n_seq)])

    qcol = pl.BlockSpec((T, QW), lambda j: (0, j))
    fcol = pl.BlockSpec((T, FW), lambda j: (0, j))
    col128 = whole((T, 128))
    square = whole((T, T))
    full = whole((T, D))
    row = whole((1, D))
    line = whole((D,))
    maps = pl.BlockSpec((4, 64, 64), lambda j: (j, 0, 0))
    piece = (per, STATE_ROWS, 128)
    piece_spec = whole(piece)
    map_scr = pltpu.VMEM((QW, FW), BF16)
    state_scr = pltpu.VMEM((H, STATE_ROWS, 128), F32)

    def w_cols(part):
        return pl.BlockSpec((D, QW), lambda j: (0, part * quads + j))

    (attn, k, v, fk, s0, s1, s2, s3, allow, allow_t, tail, contin), tok = run(
        keys_kernel, tok, (quads,),
        [(Held(x), full), (Held(gain_a), line), (Held(w_qkv), w_cols(1)), (Held(w_qkv), w_cols(2)), (Held(map_key), maps),
         (Held(key_mask), whole((1, T))), (starts, pl.BlockSpec(memory_space=pltpu.SMEM))],
        [((T, D), BF16, full), ((T, D), BF16, qcol), ((T, D), BF16, qcol), ((T, 2 * D), BF16, fcol)]
        + [(piece, F32, piece_spec)] * 4
        + [((T, T), F32, square)] * 2 + [((T, 128), F32, col128)] * 2,
        [map_scr, state_scr], us=8.0)

    def plane_exchange(pieces):
        return [pieces[0]] + [to_member(pieces[k], k) for k in range(1, 4)]

    def plane_total(own, tok):
        (total,), tok = run(
            plane_sum_kernel, tok, (1,), [(p, piece_spec) for p in own], [(piece, F32, piece_spec)])
        return total, tok

    def across(total, backward):
        if planes <= 4:
            return [shift(total, (-4 if backward else 4) * i) for i in range(1, planes)]
        every = lax.all_gather(total, "seq").reshape((planes, 4) + piece)
        mine = lax.dynamic_index_in_dim(every, seq & 3, 1, keepdims=False)
        place = jnp.arange(planes)
        want = place > (seq >> 2) if backward else place < (seq >> 2)
        return [jnp.sum(jnp.where(want[:, None, None, None], mine, 0.0), axis=0)]

    def scanned(own, others, backward, tok):
        return run(
            functools.partial(scan_kernel, backward, planes if planes <= 4 else None), tok, (1,),
            [(p, piece_spec) for p in own + others], [(piece, F32, piece_spec)] * 4)

    def later(own, others, tok):
        pair = (2 * per,) + piece[1:]
        (mine, x_pair, y_one), tok = run(
            functools.partial(later_kernel, planes if planes <= 4 else None), tok, (1,),
            [(p, piece_spec) for p in own + others],
            [(piece, F32, piece_spec), (pair, F32, whole(pair)), (piece, F32, piece_spec)])
        x_pair, y_one = to_member(x_pair, 1), to_member(y_one, 2)
        return [mine, x_pair, y_one, to_member(x_pair[per:], 2)], tok

    def turn(x, kinds, tok):
        shape = (2, len(kinds), half_rows, T)
        if not direct:
            return jnp.zeros(shape, BF16), tok
        (out,), tok = run(
            functools.partial(turn_kernel, kinds), tok, (1,), [(x, full)], [(shape, BF16, whole(shape))],
            [pltpu.VMEM((half_rows, T), F32)])
        return out, tok

    own = plane_exchange([s0, s1, s2, s3])

    (q, fq, nd), tok = run(
        queries_kernel, tok, (quads,),
        [(attn, full), (w_qkv, w_cols(0)), (map_query, maps), (fk, fcol), (v, qcol), (allow, square)],
        [((T, D), BF16, qcol), ((T, 2 * D), BF16, fcol), ((T, 2 * D), F32, fcol)],
        [map_scr], us=9.0)
    total, tok = plane_total(own, tok)
    others = across(total, False)
    (ga,), tok = run(
        act_back_kernel, tok, (FF // D,), [(cot, full), (w_proj, pl.BlockSpec((D, D), lambda j: (j, 0)))],
        [((T, FF), F32, whole((T, FF)), Near)], us=4.0)
    carried, tok = scanned(own, others, False, tok)
    carry = plane_exchange(carried)
    cot_t, tok = turn(cot, (0, 1, 2), tok)
    attn_t, tok = turn(attn, (0, 1, 2), tok)

    (mixed, mf, rden, hidden, mlp_in), tok = run(
        mix_kernel, tok, (quads,),
        [(x, full), (nd, fcol), (fq, fcol)] + [(c, piece_spec) for c in carry]
        + [(contin, col128), (w_out, pl.BlockSpec((QW, D), lambda j: (j, 0))), (Held(gain_m), line)],
        [((T, D), BF16, qcol), ((T, D), F32, qcol), ((T, D), F32, qcol), ((T, D), F32, full),
         ((T, D), BF16, full)],
        [state_scr], us=4.5)
    mlp_t, tok = turn(mlp_in, (0, 1, 2), tok)

    n_ff = FF // D
    turned_spec = whole((2, 3, half_rows, T))
    send_shape = (2, n_ff, half_rows, D)
    (act, gp, send_mlp), tok = run(
        mlp_kernel, tok, (n_ff,),
        [(mlp_in, full), (ga, columns(T, D)), (mlp_t, turned_spec), (cot_t, turned_spec), (Held(w_fc), columns(D, D))],
        [((T, FF), BF16, columns(T, D), Near)] * 2
        + [(send_shape, F32, pl.BlockSpec((2, 1, half_rows, D), lambda j: (0, j, 0, 0)), True)], us=10.0)
    if direct:
        recv_mlp = core_hop(send_mlp.array).reshape(2 * n_ff, half_rows, D)
    (output, gh, gh_low, gg_mlp), tok = run(
        mlp_out_kernel, tok, (quads,),
        [(act, whole((T, FF))), (gp, whole((T, FF))), (Held(w_fc), pl.BlockSpec((QW, FF), lambda j: (j, 0))),
         (Held(w_proj), columns(FF, QW)), (hidden, qcol), (hidden, full), (Held(cot), full), (Held(gain_m), line)],
        [((T, D), F32, qcol), ((T, D), F32, full), ((T, D), BF16, full), ((1, D), F32, row)],
        [pltpu.VMEM((quads, T, QW), F32)], us=8.0)
    def send_half(x_t, kinds, ys, tok):
        shape = (len(kinds), half_rows, D)
        (out,), tok = run(
            functools.partial(send_kernel, kinds), tok, (1,),
            [(x_t, whole(x_t.shape))] + [(y, full) for y in ys], [(shape, F32, whole(shape))], us=30.0)
        return core_hop(out), tok

    class Group:
        def __init__(self, counts, layout, widths):
            self.counts, self.layout, self.widths = counts, layout, widths
            self.stage, self.small = -1, None

    def wave(folds, join, tok, us=30.0):
        ins, outs, sends = [], [], {}
        plan = {"folds": [], "ends": [], "smalls": [], "joins": [], "copies": []}
        after = []

        def take(array, spec=None):
            for n, (other, other_spec) in enumerate(ins):
                if other is array and spec is None:
                    return n
            ins.append((array, spec or whole(array.shape)))
            return len(ins) - 1

        def place(bit, rows):
            base = sends.get(bit, 0)
            sends[bit] = base + rows
            return base

        def give(shape, put, not_last=True):
            outs.append((shape, F32, whole(shape), not_last and Near))
            after.append((len(outs) - 1, put))
            return ("out", len(outs) - 1)

        steps = 1
        for g in folds:
            g.stage += 1
            if g.stage == 4:
                rows = half_rows // 16
                g.result = [None] * len(g.widths)
                made = []
                if g is main:
                    plan["copies"] = [(take(early.result[0]), ("out", len(outs)))]
                for n, width in enumerate(g.widths):
                    def put(array, n=n, g=g):
                        g.result[n] = array
                    made.append(give((rows, width), put, False))
                n = 0
                for kind in range(3):
                    if g.counts[kind] == 0:
                        continue
                    got, at = g.got[kind]
                    for p in range(g.counts[kind]):
                        out, block = g.layout[n]
                        plan["ends"].append((take(g.keeps[kind]), take(got), at, made[out], (block, p)))
                        n += 1
            else:
                old_keeps, g.keeps = g.keeps, [None] * 3
                old_got, g.got = g.got, [None] * 3
                for kind in range(3):
                    if g.counts[kind] == 0:
                        continue
                    bit = ORDERS[kind][g.stage]
                    rows = old_keeps[kind].shape[0] // 2
                    base = place(bit, rows)
                    def put(array, kind=kind, g=g):
                        g.keeps[kind] = array
                    keep = give((rows, D), put)
                    got, at = old_got[kind]
                    plan["folds"].append(
                        (take(old_keeps[kind]), take(got), at, g.counts[kind], ("send", bit), base, keep))
                    g.got[kind] = (bit, base)
            if g.small is not None and g.stage < 4:
                got, at = g.small_got
                bit = SMALL_ORDER[g.stage]
                base = place(bit, SMALL_ROWS)
                def put(array, g=g):
                    g.small = array
                keep = give(small_shape, put)
                plan["smalls"].append((take(g.small), take(got), at, ("send", bit), base, keep))
                g.small_got = (bit, base)
        if join is not None:
            g, xs, ys, segments, small = join
            g.stage = 0
            g.keeps, g.got, offset = [None] * 3, [None] * 3, [0, 0, 0]
            at_x = [take(x) for x in xs]
            at_y, at_r = [], []
            for n, (y, r, block, y_block) in enumerate(ys):
                mine = [i for i, seg in enumerate(segments) if seg[2] == n]
                first, count = mine[0], len(mine)
                at_y.append(take(y, pl.BlockSpec(
                    (T, D), lambda i, first=first, count=count, block=y_block:
                    (0, block + jnp.clip(i - first, 0, count - 1)))))
                at_r.append(take(r, pl.BlockSpec(
                    (1, half_rows, D), lambda i, first=first, count=count, block=block:
                    (block + jnp.clip(i - first, 0, count - 1), 0, 0))))
            half = half_rows // 2
            for kind in range(3):
                if g.counts[kind] == 0:
                    continue
                bit = ORDERS[kind][0]
                g.got[kind] = (bit, place(bit, half * g.counts[kind]))
                def put(array, kind=kind, g=g):
                    g.keeps[kind] = array
                g.keeps[kind] = give((half * g.counts[kind], D), put)
            for x, entry, y, kind in segments:
                bit, base = g.got[kind]
                plan["joins"].append(
                    (at_x[x], entry, at_y[y], at_r[y], ("send", bit), base + offset[kind], g.keeps[kind], offset[kind]))
                offset[kind] += half
            steps = len(segments)
            if small is not None:
                bit = SMALL_ORDER[0]
                base = place(bit, SMALL_ROWS)
                def put(array, g=g):
                    g.small = array
                keep = give(small_shape, put)
                plan["smalls"].append((take(small[0]), take(small[1]), 0, ("send", bit), base, keep))
                g.small, g.small_got = True, (bit, base)
        first_send = len(outs)
        bits = sorted(sends)
        for bit in bits:
            outs.append(((sends[bit], D), F32, whole((sends[bit], D)), Near))
        n_in = len(ins)

        def ref(item):
            if isinstance(item, tuple) and item[0] == "out":
                return n_in + item[1]
            if isinstance(item, tuple) and item[0] == "send":
                return n_in + first_send + bits.index(item[1])
            return item

        plan = {name: tuple(tuple(ref(x) for x in entry) for entry in entries) for name, entries in plan.items()}
        results, tok = run(functools.partial(wave_kernel, plan), tok, (steps,), ins, outs, us=us, extra=6)
        for n, put in after:
            put(results[n])
        moved = {bit: Near(hop(results[first_send + n].array, bit)) for n, bit in enumerate(bits)}
        for g in folds + ([join[0]] if join else []):
            if g.stage < 4:
                g.got = [item and (moved[item[0]], item[1]) for item in g.got]
                if g.small is not None:
                    g.small_got = (moved[g.small_got[0]], g.small_got[1])
        return tok

    small_shape = (SMALL_ROWS, D)
    early = Group((1, 1, 1), [(0, i) for i in range(3)], (3 * D,))
    main = Group((2, 2, 1), [(0, n_ff - 1)] + [(1, i) for i in range(n_ff)], (FF, FF))
    wide = Group((1, 0, 0), [(0, 0)], (D,))
    last = Group((1, 1, 1), [(0, i) for i in range(3)], (3 * D,))
    if direct:
        tok = wave([], (early, [cot_t], [(act, recv_mlp, 0, 0)], [(0, kind, 0, kind) for kind in range(3)], None), tok, 4.0)

    (gn, gd, gd_t, s0, s1, s2, s3), tok = run(
        numer_back_kernel, tok, (quads,),
        [(gh_low, full), (w_out, pl.BlockSpec((QW, D), lambda j: (j, 0))), (mf, qcol), (rden, qcol),
         (fq, fcol), (contin, col128)],
        [((T, D), BF16, qcol), ((T, D), F32, qcol),
         ((8 * H, T), F32, pl.BlockSpec((32, T), lambda j: (j, 0)))] + [(piece, F32, piece_spec)] * 4,
        [state_scr], us=5.0)
    own = plane_exchange([s0, s1, s2, s3])
    if direct:
        tok = wave(
            [early],
            (main, [cot_t, mlp_t], [(act, recv_mlp, n_ff - 1, n_ff - 1), (gp, recv_mlp, n_ff, 0)],
             [(0, 0, 0, 0)] + [(1, kind, 1, kind) for kind in (0, 1, 1, 2)], None), tok, 7.0)
    total, tok = plane_total(own, tok)
    others = across(total, True)

    def fixed(shape, quad):
        return pl.BlockSpec(shape, lambda i: (0, quad))

    def fixed_rows(shape, quad):
        return pl.BlockSpec(shape, lambda i: (quad,) + (0,) * (len(shape) - 1))

    def scores_back(quad, before, tok):
        ins = [(q, fixed((T, QW), quad)), (fq, fixed((T, FW), quad)), (fk, fixed((T, FW), quad)),
               (v, fixed((T, QW), quad)), (gn, fixed((T, QW), quad)), (gd, fixed((T, QW), quad)),
               (gd_t, fixed_rows((32, T), quad))] + [(c, piece_spec) for c in carry]
        ins += [(allow, square), (allow_t, square), (contin, col128), (map_query, fixed_rows((4, 64, 64), quad))]
        aliases = {len(ins) + i: i for i in range(4)} if before else None
        ins += [(a, ANYWHERE) for a in before]
        return run(
            functools.partial(scores_back_kernel, quad), tok, (1,), ins,
            [((T, D), BF16, fixed((T, QW), quad)), ((T, 2 * D), F32, fixed((T, FW), quad)),
             ((T, D), F32, fixed((T, QW), quad)), ((D, 128), F32, fixed_rows((QW, 128), quad))],
            [map_scr, state_scr, pltpu.VMEM((T, FW), BF16)], extra=7, aliases=aliases, us=4.5)

    backs, tok = scores_back(0, [], tok)
    backs, tok = scores_back(1, backs, tok)
    backs, tok = scores_back(2, backs, tok)
    gq, gfk, gv_f, gmq = backs
    upstream, tok = later(own, others, tok)
    if direct:
        mixed_t, tok = turn(mixed, (0,), tok)
        recv_out, tok = send_half(mixed_t, (0,), [gh_low], tok)
        tok = wave(
            [early, main], (wide, [mixed_t], [(gh_low, recv_out, 0, 0)], [(0, 0, 0, 0)], None), tok, 2.0)

    (gk, gv, gmk), tok = run(
        keys_back_kernel, tok, (quads,),
        [(k, qcol), (fk, fcol), (v, qcol), (gfk, fcol), (gv_f, qcol)] + [(c, piece_spec) for c in upstream]
        + [(tail, col128), (map_key, maps)],
        [((T, D), BF16, qcol), ((T, D), BF16, qcol),
         ((D, 128), F32, pl.BlockSpec((QW, 128), lambda j: (j, 0)))],
        [map_scr, state_scr, pltpu.VMEM((T, FW), BF16)], us=60.0)
    if direct:
        recv_qkv, tok = send_half(attn_t, (0, 1, 2), [gq, gk, gv], tok)

    small_spec = whole(small_shape)
    packed = 2 * SMALL_ROWS * (D // 128)
    (gx, keep, send), tok = run(
        inputs_back_kernel, tok, (3,),
        [(gq, full), (gk, full), (gv, full), (w_qkv, columns(D, D)), (x, full), (gh, full), (Held(gain_a), line),
         (gg_mlp, row), (gmq, whole((D, 128))), (gmk, whole((D, 128)))],
        [((T, D), F32, full)] + [(small_shape, F32, small_spec)] * 2,
        [pltpu.VMEM((T, D), F32), pltpu.VMEM((packed, 128), F32)], us=60.0)

    got = core_hop(send)
    if direct:
        tok = wave(
            [], (last, [attn_t], [(gq, recv_qkv, 0, 0), (gk, recv_qkv, 1, 0), (gv, recv_qkv, 2, 0)],
                 [(0, kind, kind, kind) for kind in range(3)], (keep, got)), tok, 4.0)
        tok = wave([early, main, wide], None, tok)
        tok = wave([last], None, tok)
        tok = wave([early, main, wide], None, tok)
        tok = wave([last], None, tok)
        tok = wave([main, wide], None, tok)
        tok = wave([last], None, tok)
        (mine,), tok = run(
            add_kernel, tok, (1,), [(last.small, small_spec), (last.small_got[0], small_spec)],
            [(small_shape, F32, small_spec, Near)], us=0.1)
        got = core_hop(mine.array)
        tok = wave([wide, last], None, tok)
        (grad_w_qkv,) = last.result
        grad_proj_rows, grad_w_fc = main.result
        (grad_w_out,) = wide.result
    else:
        mine = lax.psum(keep + got, "seq")
        got = core_hop(mine)
        summed = lax.psum_scatter(
            jnp.concatenate(
                [tn(attn, gq), tn(attn, gk), tn(attn, gv), tn(mixed, gh_low), tn(mlp_in, gp.array), tn(cot, act.array)],
                axis=1,
            ),
            ("batch", "seq"), scatter_dimension=0, tiled=True)
        grad_w_qkv = summed[:, : 3 * D]
        grad_w_out = summed[:, 3 * D : 4 * D]
        grad_w_fc = summed[:, 4 * D : 4 * D + FF]
        grad_proj_rows = summed[:, 4 * D + FF :]

    heads_shape = (H, 64, 64)
    (grad_map_query, grad_map_key, gains), tok = run(
        unpack_kernel, tok, (1,), [(mine, small_spec), (got, small_spec)],
        [(heads_shape, F32, whole(heads_shape))] * 2 + [((16, 128), F32, whole((16, 128)))],
        [pltpu.VMEM((packed, 128), F32)], us=0.1)
    n = D // 128
    return (
        output[None],
        gx[None],
        grad_w_qkv,
        grad_w_out,
        grad_w_fc,
        grad_proj_rows.T,
        grad_map_query,
        grad_map_key,
        gains[:n].reshape(D),
        gains[n : 2 * n].reshape(D),
    )


def solution(mesh):
    tokens = P("batch", "seq", None)
    flags = P("batch", "seq")
    rows = P(("batch", "seq"), None)
    return jax.shard_map(
        local,
        mesh=mesh,
        in_specs=(tokens,) + (P(),) * 8 + (flags, flags, tokens),
        out_specs=(tokens, tokens, rows, rows, rows, P(None, ("batch", "seq")), P(), P(), P(), P()),
        check_vma=False,
    )
```

```python
import functools

import jax
import jax.numpy as jnp
from jax import lax
from jax.experimental import pallas as pl
from jax.experimental.pallas import tpu as pltpu
from jax.sharding import PartitionSpec as P

EPSILON = 1e-05
F32 = jnp.float32
BF16 = jnp.bfloat16
STATE_ROWS = 72
SMALL_ROWS = 72
MIB = 1024 * 1024


def mm(a, b):
    return lax.dot_general(a, b, (((1,), (0,)), ((), ())), preferred_element_type=F32)


def nt(a, b):
    return lax.dot_general(a, b, (((1,), (1,)), ((), ())), preferred_element_type=F32)


def tn(a, b):
    return lax.dot_general(a, b, (((0,), (0,)), ((), ())), preferred_element_type=F32)


def split(v):
    high = v.astype(BF16)
    return high, (v - high.astype(F32)).astype(BF16)


def iota(shape, dim):
    return lax.broadcasted_iota(jnp.int32, shape, dim)


def segment_ones(width):
    shape = (width, width)
    return (iota(shape, 0) // 64 == iota(shape, 1) // 64).astype(BF16)


def segment_sum(v, ones):
    high, low = split(v)
    return mm(high, ones) + mm(low, ones)


def moments(x):
    centre = jnp.mean(x, axis=-1, keepdims=True)
    offsets = x - centre
    variance = jnp.mean(offsets * offsets, axis=-1, keepdims=True)
    scale = lax.rsqrt(variance + EPSILON)
    return offsets * scale, scale


def norm_back(grad, normed, scale, gain):
    dn = grad * gain
    first = jnp.mean(dn, axis=-1, keepdims=True)
    second = jnp.mean(dn * normed, axis=-1, keepdims=True)
    return (dn - first - normed * second) * scale


def fill_maps(scr, map_ref):
    scr[...] = jnp.zeros(scr.shape, scr.dtype)
    for h in range(4):
        m = map_ref[h].astype(F32)
        scr[64 * h : 64 * h + 64, 128 * h : 128 * h + 128] = jnp.concatenate(
            [m, -m], axis=1
        ).astype(scr.dtype)


def half_sums(v, low_half):
    top = jnp.sum(jnp.where(low_half, v, 0.0), axis=1, keepdims=True)
    bottom = jnp.sum(jnp.where(low_half, 0.0, v), axis=1, keepdims=True)
    return jnp.where(low_half, top, bottom)


def features(pre):
    low_half = iota(pre.shape, 1) < 64
    top = jnp.max(jnp.where(low_half, pre, -jnp.inf), axis=1, keepdims=True)
    bottom = jnp.max(jnp.where(low_half, -jnp.inf, pre), axis=1, keepdims=True)
    e = jnp.exp(pre - jnp.where(low_half, top, bottom))
    return e / half_sums(e, low_half)


def features_back(feat, grad, ones):
    low_half = iota(feat.shape, 1) < 64
    weighted = feat * grad
    mass = mm(feat.astype(BF16), ones)
    part = weighted - feat * (half_sums(weighted, low_half) / mass)
    return part - pltpu.roll(part, 64, 1)


def whole(shape):
    return pl.BlockSpec(shape, lambda *_: (0,) * len(shape))


def columns(rows, width):
    return pl.BlockSpec((rows, width), lambda j: (0, j))


ANYWHERE = pl.BlockSpec(memory_space=pl.ANY)


def my_core():
    return lax.axis_index("batch")


def my_seq():
    return lax.axis_index("seq")


def nbytes(shape, dtype):
    total = jnp.dtype(dtype).itemsize
    for n in shape:
        total *= n
    return total


class Held:
    def __init__(self, array):
        self.array, self.shape, self.dtype = array, array.shape, array.dtype


class Near(Held):
    pass


def run(kernel, tok, grid, ins, outs, scratch=(), extra=3, aliases=None, us=1.0):
    n_in, n_out = len(ins), len(outs)
    linked = tok is not None
    outs = [tuple(out) + (False,) * (4 - len(out)) for out in outs]

    def body(*refs):
        kernel(*refs[:n_in], *refs[n_in + linked : n_in + linked + n_out], *refs[n_in + linked + n_out + 1 :])

    held = 0
    arrays = []
    for array, spec in ins:
        near = isinstance(array, Near)
        if spec.block_shape is not None and not (near and spec.block_shape == array.shape):
            held += (1 if spec.block_shape == array.shape else 2) * nbytes(spec.block_shape, array.dtype)
        if isinstance(array, Held):
            array = pltpu.with_memory_space_constraint(array.array, pltpu.VMEM if near else pltpu.HBM)
        arrays.append(array)
    for shape, dtype, spec, stays in outs:
        if not (stays is Near and spec.block_shape == shape):
            held += (1 if spec.block_shape == shape else 2) * nbytes(spec.block_shape, dtype)
    for item in scratch:
        held += nbytes(item.shape, item.dtype)
    result = pl.pallas_call(
        body,
        grid=grid,
        in_specs=[spec for _, spec in ins] + [ANYWHERE] * linked,
        out_specs=[spec for _, _, spec, _ in outs] + [ANYWHERE],
        scratch_shapes=list(scratch),
        out_shape=[
            pltpu.VMEM(shape, dtype) if stays is Near
            else pltpu.HBM(shape, dtype) if stays else jax.ShapeDtypeStruct(shape, dtype)
            for shape, dtype, _, stays in outs
        ]
        + [jax.ShapeDtypeStruct((8, 128), F32)],
        input_output_aliases=aliases or {},
        cost_estimate=pl.CostEstimate(flops=int(us * 1.15e9), bytes_accessed=0, transcendentals=0),
        compiler_params=pltpu.CompilerParams(vmem_limit_bytes=min(held + extra * MIB, 60 * MIB)),
    )(*arrays, *([tok] if linked else []))
    results = [Near(r) if out[3] is Near else Held(r) if out[3] else r for r, out in zip(result, outs)]
    return results, result[-1]


def keys_kernel(x_ref, gain_ref, wk_ref, wv_ref, map_ref, mask_ref, starts_ref,
                attn_ref, k_ref, v_ref, fk_ref, p0, p1, p2, p3,
                allow_ref, allow_t_ref, tail_ref, contin_ref,
                map_scr, state_scr):
    j = pl.program_id(0)
    tokens = x_ref.shape[0]
    n_flags = starts_ref.shape[1]
    unit = tokens // n_flags

    def seg(shape, dim):
        place = iota(shape, dim)
        total = jnp.zeros(shape, jnp.int32)
        for u in range(n_flags):
            total = total + jnp.where(place >= unit * u, starts_ref[0, u], 0)
        return total

    @pl.when(j == 0)
    def _():
        normed, _ = moments(x_ref[...].astype(F32))
        attn_ref[...] = (normed * gain_ref[...].reshape(1, -1)).astype(BF16)
        last = starts_ref[0, 0]
        for u in range(1, n_flags):
            last = last + starts_ref[0, u]
        mask_row = mask_ref[...].astype(F32)
        mask_col = jnp.transpose(jnp.broadcast_to(mask_row, (128, tokens)))
        seg_col = seg((tokens, 128), 0)
        tail_ref[...] = jnp.where(seg_col == last, mask_col, 0.0)
        contin_ref[...] = jnp.where(seg_col == 0, 1.0, 0.0)
        square = (tokens, tokens)
        same = seg(square, 0) == seg(square, 1)
        allow_ref[...] = jnp.where(same & (iota(square, 1) <= iota(square, 0)), mask_row, 0.0)
        wide_mask = jnp.concatenate([mask_col] * (tokens // 128), axis=1)
        allow_t_ref[...] = jnp.where(same & (iota(square, 0) <= iota(square, 1)), wide_mask, 0.0)

    fill_maps(map_scr, map_ref)
    attn = attn_ref[...]
    k4 = mm(attn, wk_ref[...]).astype(BF16)
    v4 = mm(attn, wv_ref[...]).astype(BF16)
    k_ref[...] = k4
    v_ref[...] = v4
    pre = mm(k4, map_scr[...])
    ones = segment_ones(128)
    v_t = jnp.transpose(v4.astype(F32)).astype(BF16)
    tail = tail_ref[...]
    row_ones = jnp.ones((16, tokens), BF16)
    for h in range(4):
        feat = features(pre[:, 128 * h : 128 * h + 128]).astype(BF16)
        fk_ref[:, 128 * h : 128 * h + 128] = feat
        kept = (feat.astype(F32) * tail).astype(BF16)
        rows = jnp.concatenate([v_t[64 * h : 64 * h + 64], row_ones], axis=0)
        state_scr[4 * j + h] = mm(rows, kept)[0:STATE_ROWS]

    @pl.when(j == pl.num_programs(0) - 1)
    def _():
        for k, piece in enumerate((p0, p1, p2, p3)):
            n = piece.shape[0]
            piece[...] = state_scr[pl.ds(((my_seq() & 3) ^ k) * n, n)]


def queries_kernel(attn_ref, wq_ref, map_ref, fk_ref, v_ref, allow_ref,
                   q_ref, fq_ref, nd_ref, map_scr):
    tokens = attn_ref.shape[0]
    half = tokens // 2
    fill_maps(map_scr, map_ref)
    q4 = mm(attn_ref[...], wq_ref[...]).astype(BF16)
    q_ref[...] = q4
    pre = mm(q4, map_scr[...])
    ones = segment_ones(128)
    low_half = iota((tokens, 128), 1) < 64
    for h in range(4):
        lanes = slice(128 * h, 128 * h + 128)
        feat = features(pre[:, lanes]).astype(BF16)
        fq_ref[:, lanes] = feat
        fk = fk_ref[:, lanes]
        pair = v_ref[:, 128 * (h // 2) : 128 * (h // 2) + 128].astype(F32)
        if h % 2:
            pair = pltpu.roll(pair, 64, 1)
        wide = jnp.where(low_half, pair, 1.0).astype(BF16)
        first = nt(feat[:half], fk[:half]) * allow_ref[:half, :half]
        nd_ref[:half, lanes] = mm(first.astype(BF16), wide[:half])
        second = nt(feat[half:], fk) * allow_ref[half:, :]
        nd_ref[half:, lanes] = mm(second.astype(BF16), wide)


def plane_sum_kernel(*refs):
    *pieces, out = refs
    total = pieces[0][...]
    for piece in pieces[1:]:
        total = total + piece[...]
    out[...] = total


def scan_kernel(backward, planes, *refs):
    own = refs[:4]
    others = refs[4:-4]
    outs = refs[-4:]
    member, plane = my_seq() & 3, my_seq() >> 2
    total = jnp.zeros(own[0].shape, F32)
    for i, other in enumerate(others):
        if planes is None:
            total = total + other[...]
        else:
            there = plane + i + 1 < planes if backward else plane - i - 1 >= 0
            total = total + jnp.where(there, other[...], 0.0)
    for k, out in enumerate(outs):
        value = total
        target = member ^ k
        for i, piece in enumerate(own):
            source = member ^ i
            counts = source > target if backward else source < target
            value = value + jnp.where(counts, piece[...], 0.0)
        out[...] = value


def later_kernel(planes, own0, own1, own2, own3, *refs):
    own, others, (mine, x_pair, y_one) = (own0, own1, own2, own3), refs[:-3], refs[-3:]
    member, plane = my_seq() & 3, my_seq() >> 2
    total = jnp.zeros(own0.shape, F32)
    for i, other in enumerate(others):
        if planes is None:
            total = total + other[...]
        else:
            total = total + jnp.where(plane + i + 1 < planes, other[...], 0.0)
    n = own0.shape[0]
    for k in range(4):
        value = total
        for i, piece in enumerate(own):
            value = value + jnp.where((member ^ i) > (member ^ k), piece[...], 0.0)
        if k == 0:
            mine[...] = value
        elif k == 2:
            y_one[...] = value
        else:
            x_pair[n * (k // 2) : n * (k // 2) + n] = value


def place_heads(scr, pieces):
    for k, piece in enumerate(pieces):
        n = piece.shape[0]
        scr[pl.ds(((my_seq() & 3) ^ k) * n, n)] = piece[...]


def mix_kernel(x_ref, nd_ref, fq_ref, c0, c1, c2, c3, contin_ref, wo_ref, gain_ref,
               mixed_ref, mf_ref, rden_ref, hidden_ref, mlp_ref, carry_scr):
    j = pl.program_id(0)
    tokens = x_ref.shape[0]
    low_half = iota((tokens, 128), 1) < 64

    @pl.when(j == 0)
    def _():
        place_heads(carry_scr, (c0, c1, c2, c3))
        hidden_ref[...] = x_ref[...].astype(F32)

    contin = contin_ref[...]
    for pair in range(2):
        quotients, inverses = [], []
        for side in range(2):
            h = 2 * pair + side
            lanes = slice(128 * h, 128 * h + 128)
            carry = carry_scr[4 * j + h]
            wide = jnp.concatenate([carry[:64], jnp.broadcast_to(carry[64:65], (64, 128))], axis=0)
            high, low = split(wide)
            fq = fq_ref[:, lanes]
            nd = nd_ref[:, lanes] + contin * (nt(fq, high) + nt(fq, low))
            inverse = 1.0 / nd
            turned = pltpu.roll(inverse, 64, 1)
            quotient = nd * turned
            if side:
                quotients.append(pltpu.roll(quotient, 64, 1))
                inverses.append(inverse)
            else:
                quotients.append(quotient)
                inverses.append(turned)
        lanes = slice(128 * pair, 128 * pair + 128)
        mf = jnp.where(low_half, *quotients)
        mf_ref[:, lanes] = mf
        mixed_ref[:, lanes] = mf.astype(BF16)
        rden_ref[:, lanes] = jnp.where(low_half, *inverses)
    hidden_ref[...] += mm(mixed_ref[...], wo_ref[...])

    @pl.when(j == pl.num_programs(0) - 1)
    def _():
        normed, _ = moments(hidden_ref[...])
        mlp_ref[...] = (normed * gain_ref[...].reshape(1, -1)).astype(BF16)


GELU_A, GELU_C = 0.044715, 0.7978845608028654


def turn_kernel(kinds, x_ref, out_ref, scr):
    rows, half = out_ref.shape[2] // 16, out_ref.shape[2]
    for side in range(2):
        core = my_core() if side else 1 - my_core()
        turned = jnp.transpose(
            x_ref[:, pl.ds(pl.multiple_of(core * half, 128), half)].astype(F32)
        )
        for at, kind in enumerate(kinds):
            for g in range(16):
                place = g ^ my_seq()
                spot = 0
                for depth, bit in enumerate(ORDERS[kind]):
                    spot = spot + (((place >> bit) & 1) << (3 - depth))
                scr[pl.ds(pl.multiple_of(spot * rows, 8), rows), :] = turned[rows * g : rows * g + rows]
            out_ref[side, at] = scr[...].astype(BF16)


def act_back_kernel(cot_ref, wp_ref, ga_ref):
    width = wp_ref.shape[0]
    start = pl.multiple_of(pl.program_id(0) * width, 128)
    ga_ref[:, pl.ds(start, width)] = nt(cot_ref[...], wp_ref[...])


def mlp_kernel(mlp_ref, ga_ref, mlp_t, cot_t, wf_ref, act_ref, gp_ref, send_ref):
    j = pl.program_id(0)
    tokens, width = mlp_ref.shape[0], wf_ref.shape[1]
    lanes = slice(0, width)
    step = tokens // 4
    for r in range(4):
        rows = slice(step * r, step * r + step)
        u = mm(mlp_ref[rows, :], wf_ref[...])
        square = u * u
        t = jnp.tanh(GELU_C * (u + GELU_A * (u * square)))
        half = 0.5 * (1.0 + t)
        act_ref[rows, lanes] = (u * half).astype(BF16)
        slope = half + (0.5 * GELU_C) * u * (1.0 - t * t) * (1.0 + (3.0 * GELU_A) * square)
        gp_ref[rows, lanes] = (ga_ref[rows, lanes] * slope).astype(BF16)
    send_ref[0, 0] = mm(cot_t[0, j % 3], act_ref[:, lanes])
    send_ref[1, 0] = mm(mlp_t[0, (j + 1) // 2], gp_ref[:, lanes])


def mlp_out_kernel(act_ref, gp_ref, wf_ref, wp_ref, part_ref, hidden_ref, cot_ref, gain_ref,
                   out_ref, gh_ref, gh_low_ref, gg_ref, back_scr):
    j = pl.program_id(0)
    out_ref[...] = part_ref[...] + mm(act_ref[...], wp_ref[...])
    back_scr[j] = nt(gp_ref[...], wf_ref[...])

    @pl.when(j == pl.num_programs(0) - 1)
    def _():
        normed, scale = moments(hidden_ref[...])
        grad = jnp.concatenate([back_scr[i] for i in range(back_scr.shape[0])], axis=1)
        gg_ref[...] = jnp.sum(grad * normed, axis=0, keepdims=True)
        gh = cot_ref[...].astype(F32) + norm_back(grad, normed, scale, gain_ref[...].reshape(1, -1))
        gh_ref[...] = gh
        gh_low_ref[...] = gh.astype(BF16)


def numer_back_kernel(gh_ref, wo_ref, mf_ref, rden_ref, fq_ref, contin_ref,
                      gn_ref, gd_ref, gd_t_ref, p0, p1, p2, p3, state_scr):
    j = pl.program_id(0)
    gm = nt(gh_ref[...], wo_ref[...]) * rden_ref[...]
    gn_ref[...] = gm.astype(BF16)
    gd = -segment_sum(gm * mf_ref[...], segment_ones(256))
    gd_ref[...] = gd
    gn_t = jnp.transpose(gm).astype(BF16)
    gd_t = jnp.transpose(gd)
    contin = contin_ref[...]
    for h in range(4):
        rows = gd_t[64 * h : 64 * h + 8]
        gd_t_ref[8 * h : 8 * h + 8, :] = rows
        kept = (fq_ref[:, 128 * h : 128 * h + 128].astype(F32) * contin).astype(BF16)
        high, low = split(rows)
        both = jnp.concatenate([high.astype(F32), low.astype(F32)], axis=0).astype(BF16)
        sums = mm(jnp.concatenate([gn_t[64 * h : 64 * h + 64], both], axis=0), kept)
        state_scr[4 * j + h, 0:64, :] = sums[0:64]
        state_scr[4 * j + h, 64:72, :] = sums[64:72] + sums[72:80]

    @pl.when(j == pl.num_programs(0) - 1)
    def _():
        for k, piece in enumerate((p0, p1, p2, p3)):
            n = piece.shape[0]
            piece[...] = state_scr[pl.ds(((my_seq() & 3) ^ k) * n, n)]


def side_rows(state, side):
    zeros = jnp.zeros((64, 128), F32)
    rows = state[:64]
    return jnp.concatenate([zeros, rows] if side else [rows, zeros], axis=0)


def scores_back_kernel(j, q_ref, fq_ref, fk_ref, v_ref, gn_ref, gd_ref, gd_t_ref,
                       c0, c1, c2, c3, allow_ref, allow_t_ref, contin_ref, map_ref, *rest):
    gq_ref, gfk_ref, gv_ref, gmap_ref, map_scr, carry_scr, d_scr = rest[-7:]
    tokens = q_ref.shape[0]
    half = tokens // 2
    place_heads(carry_scr, (c0, c1, c2, c3))

    fill_maps(map_scr, map_ref)
    ones = segment_ones(128)
    low_half = iota((tokens, 128), 1) < 64
    contin = contin_ref[...]
    for pair in range(2):
        pair_lanes = slice(128 * pair, 128 * pair + 128)
        v_pair = v_ref[:, pair_lanes]
        gn_pair = gn_ref[:, pair_lanes].astype(F32)
        gd_pair = gd_ref[:, pair_lanes]
        gd_turned = pltpu.roll(gd_pair, 64, 1)
        gv_parts = []
        for side in range(2):
            h = 2 * pair + side
            lanes = slice(128 * h, 128 * h + 128)
            mine = ~low_half if side else low_half
            gn = jnp.where(mine, gn_pair, 0.0).astype(BF16)
            gd = jnp.where(mine, gd_pair, gd_turned)
            gd_row = gd_t_ref[8 * h : 8 * h + 1, :]
            fq, fk = fq_ref[:, lanes], fk_ref[:, lanes]
            gd_few = jnp.concatenate([gd] * (half // 128), axis=1)
            gd_many = jnp.concatenate([gd] * (tokens // 128), axis=1)
            g_top = ((nt(gn[:half], v_pair[:half]) + gd_few[:half]) * allow_ref[:half, :half]).astype(BF16)
            g_bot = ((nt(gn[half:], v_pair) + gd_many[half:]) * allow_ref[half:, :]).astype(BF16)
            carry = carry_scr[4 * j + h]
            high, low = split(side_rows(carry, side))
            inter = mm(gn, high) + mm(gn, low) + gd * carry[64:65]
            gfq = jnp.concatenate([mm(g_top, fk[:half]), mm(g_bot, fk)], axis=0) + contin * inter
            d_scr[:, lanes] = features_back(fq.astype(F32), gfq, ones).astype(BF16)

            at_top, at_bot = allow_t_ref[:half, :], allow_t_ref[half:, half:]
            gt_top = ((nt(v_pair[:half], gn) + gd_row) * at_top).astype(BF16)
            gt_bot = ((nt(v_pair[half:], gn[half:]) + gd_row[:, half:]) * at_bot).astype(BF16)
            gfk_ref[:half, lanes] = mm(gt_top, fq)
            gfk_ref[half:, lanes] = mm(gt_bot, fq[half:])
            st_top = (nt(fk[:half], fq) * at_top).astype(BF16)
            st_bot = (nt(fk[half:], fq[half:]) * at_bot).astype(BF16)
            gv_parts.append(jnp.concatenate([mm(st_top, gn), mm(st_bot, gn[half:])], axis=0))
        gv_ref[:, pair_lanes] = gv_parts[0] + gv_parts[1]
    d = d_scr[...]
    gq_ref[...] = (0.5 * nt(d, map_scr[...])).astype(BF16)
    gm = tn(q_ref[...], d)
    for h in range(4):
        gmap_ref[64 * h : 64 * h + 64, :] = gm[64 * h : 64 * h + 64, 128 * h : 128 * h + 128]


def keys_back_kernel(k_ref, fk_ref, v_ref, gfk_ref, gv_ref, u0, u1, u2, u3, tail_ref, map_ref,
                     gk_ref, gvb_ref, gmap_ref, map_scr, up_scr, d_scr):
    j = pl.program_id(0)

    @pl.when(j == 0)
    def _():
        place_heads(up_scr, (u0, u1, u2, u3))

    fill_maps(map_scr, map_ref)
    ones = segment_ones(128)
    tail = tail_ref[...]
    for pair in range(2):
        pair_lanes = slice(128 * pair, 128 * pair + 128)
        v_pair = v_ref[:, pair_lanes]
        gv = gv_ref[:, pair_lanes]
        for side in range(2):
            h = 2 * pair + side
            lanes = slice(128 * h, 128 * h + 128)
            up = up_scr[4 * j + h]
            high, low = split(side_rows(up, side))
            fk = fk_ref[:, lanes]
            key_term = mm(v_pair, high) + mm(v_pair, low) + up[64:65]
            gfk = gfk_ref[:, lanes] + tail * key_term
            gv = gv + tail * (nt(fk, high) + nt(fk, low))
            d_scr[:, lanes] = features_back(fk.astype(F32), gfk, ones).astype(BF16)
        gvb_ref[:, pair_lanes] = gv.astype(BF16)
    d = d_scr[...]
    gk_ref[...] = (0.5 * nt(d, map_scr[...])).astype(BF16)
    gm = tn(k_ref[...], d)
    for h in range(4):
        gmap_ref[64 * h : 64 * h + 64, :] = gm[64 * h : 64 * h + 64, 128 * h : 128 * h + 128]


def inputs_back_kernel(gq_ref, gk_ref, gv_ref, w_ref, x_ref, gh_ref, gain_ref, gg_mlp_ref,
                       gmq_ref, gmk_ref, gx_ref, keep_ref, send_ref, acc, pack):
    j = pl.program_id(0)

    @pl.when(j == 0)
    def _():
        acc[...] = nt(gq_ref[...], w_ref[...])
        rows = gmq_ref.shape[0]
        low_half = iota(gmq_ref.shape, 1) < 64
        pack[:rows, :] = jnp.where(low_half, gmq_ref[...], pltpu.roll(gmk_ref[...], 64, 1))
        pack[rows:, :] = jnp.zeros((pack.shape[0] - rows, 128), F32)

    @pl.when(j == 1)
    def _():
        acc[...] += nt(gk_ref[...], w_ref[...])

    @pl.when(j == 2)
    def _():
        grad = acc[...] + nt(gv_ref[...], w_ref[...])
        normed, scale = moments(x_ref[...].astype(F32))
        gx_ref[...] = gh_ref[...] + norm_back(grad, normed, scale, gain_ref[...].reshape(1, -1))
        gg = jnp.sum(grad * normed, axis=0, keepdims=True)
        rows = gmq_ref.shape[0]
        n = gg.shape[1] // 128
        for i in range(n):
            pack[rows + i : rows + i + 1, :] = gg[:, 128 * i : 128 * i + 128]
            pack[rows + n + i : rows + n + i + 1, :] = gg_mlp_ref[:, 128 * i : 128 * i + 128]
        for out, core in ((keep_ref, my_core()), (send_ref, 1 - my_core())):
            for c in range(n):
                start = core * (n * SMALL_ROWS) + c * SMALL_ROWS
                out[:, 128 * c : 128 * c + 128] = pack[pl.ds(pl.multiple_of(start, 8), SMALL_ROWS), :]


def add_kernel(a_ref, b_ref, out_ref):
    out_ref[...] = a_ref[...] + b_ref[...]


def unpack_kernel(kept_ref, other_ref, gmq_ref, gmk_ref, gains_ref, pack):
    n = kept_ref.shape[1] // 128
    for value, core in ((kept_ref[...], my_core()), (other_ref[...], 1 - my_core())):
        for c in range(n):
            start = core * (n * SMALL_ROWS) + c * SMALL_ROWS
            pack[pl.ds(pl.multiple_of(start, 8), SMALL_ROWS), :] = value[:, 128 * c : 128 * c + 128]
    heads = gmq_ref.shape[0]
    for h in range(heads):
        both = pack[64 * h : 64 * h + 64, :]
        gmq_ref[h] = both[:, :64]
        gmk_ref[h] = both[:, 64:]
    gains_ref[...] = pack[64 * heads : 64 * heads + 16, :]


ORDERS = ((0, 1, 2, 3), (1, 2, 0, 3), (2, 0, 1, 3))
SMALL_ORDER = (3, 0, 1, 2)


def send_kernel(kinds, x_ref, *refs):
    out_ref = refs[-1]
    for i, kind in enumerate(kinds):
        out_ref[i] = mm(x_ref[0, kind], refs[i][...])


def wave_kernel(plan, *refs):
    i = pl.program_id(0)

    @pl.when(i == 0)
    def _():
        for kept, got, at, count, send, base, keep in plan["folds"]:
            rows = refs[kept].shape[0] // count
            half = rows // 2
            for p in range(count):
                total = (refs[kept][rows * p : rows * p + rows, :]
                         + refs[got][at + rows * p : at + rows * p + rows, :])
                refs[send][base + half * p : base + half * p + half, :] = total[half:]
                refs[keep][half * p : half * p + half, :] = total[:half]
        for whence, out in plan["copies"]:
            refs[out][:, : refs[whence].shape[1]] = refs[whence][...]
        for kept, got, at, out, block in plan["ends"]:
            rows, width = refs[out].shape[0], refs[kept].shape[1]
            first, piece = block
            refs[out][:, width * first : width * first + width] = (
                refs[kept][rows * piece : rows * piece + rows, :]
                + refs[got][at + rows * piece : at + rows * piece + rows, :]
            )
        for kept, got, at, send, base, keep in plan["smalls"]:
            rows = refs[kept].shape[0]
            total = refs[kept][...] + refs[got][at : at + rows, :]
            refs[keep][...] = total
            refs[send][base : base + rows, :] = total

    for step, (x, entry, y, r, send, base, keep, at) in enumerate(plan["joins"]):

        @pl.when(i == step)
        def _():
            value = mm(refs[x][1, entry], refs[y][...]) + refs[r][0]
            half = value.shape[0] // 2
            refs[send][base : base + half, :] = value[half:]
            refs[keep][at : at + half, :] = value[:half]


def core_hop(v):
    return lax.ppermute(v, "batch", [(0, 1), (1, 0)])


def local(inputs, w_qkv, w_out, w_fc, w_proj, map_query, map_key, gain_attn, gain_mlp,
          starts, key_mask, cotangent):
    T, D = inputs.shape[1], inputs.shape[2]
    H = map_query.shape[0]
    FF = w_fc.shape[1]
    n_seq = lax.axis_size("seq")
    planes = n_seq // 4
    quads = H // 4
    QW, FW = 4 * 64, 4 * 128
    half_rows = D // 2
    per = H // 4
    seq = lax.axis_index("seq")
    tok = None
    x, cot = inputs[0], cotangent[0]
    gain_a, gain_m = gain_attn, gain_mlp
    direct = n_seq == 16

    def hop(v, bit):
        return lax.ppermute(v, "seq", [(i, i ^ (1 << bit)) for i in range(n_seq)])

    def to_member(v, k):
        return lax.ppermute(v, "seq", [(i, i ^ k) for i in range(n_seq)])

    def shift(v, by):
        return lax.ppermute(v, "seq", [(i, (i + by) % n_seq) for i in range(n_seq)])

    qcol = pl.BlockSpec((T, QW), lambda j: (0, j))
    fcol = pl.BlockSpec((T, FW), lambda j: (0, j))
    col128 = whole((T, 128))
    square = whole((T, T))
    full = whole((T, D))
    row = whole((1, D))
    line = whole((D,))
    maps = pl.BlockSpec((4, 64, 64), lambda j: (j, 0, 0))
    piece = (per, STATE_ROWS, 128)
    piece_spec = whole(piece)
    map_scr = pltpu.VMEM((QW, FW), BF16)
    state_scr = pltpu.VMEM((H, STATE_ROWS, 128), F32)

    def w_cols(part):
        return pl.BlockSpec((D, QW), lambda j: (0, part * quads + j))

    (attn, k, v, fk, s0, s1, s2, s3, allow, allow_t, tail, contin), tok = run(
        keys_kernel, tok, (quads,),
        [(Held(x), full), (Held(gain_a), line), (Held(w_qkv), w_cols(1)), (Held(w_qkv), w_cols(2)), (Held(map_key), maps),
         (Held(key_mask), whole((1, T))), (starts, pl.BlockSpec(memory_space=pltpu.SMEM))],
        [((T, D), BF16, full), ((T, D), BF16, qcol), ((T, D), BF16, qcol), ((T, 2 * D), BF16, fcol)]
        + [(piece, F32, piece_spec)] * 4
        + [((T, T), F32, square)] * 2 + [((T, 128), F32, col128)] * 2,
        [map_scr, state_scr], us=8.0)

    def plane_exchange(pieces):
        return [pieces[0]] + [to_member(pieces[k], k) for k in range(1, 4)]

    def plane_total(own, tok):
        (total,), tok = run(
            plane_sum_kernel, tok, (1,), [(p, piece_spec) for p in own], [(piece, F32, piece_spec)])
        return total, tok

    def across(total, backward):
        if planes <= 4:
            return [shift(total, (-4 if backward else 4) * i) for i in range(1, planes)]
        every = lax.all_gather(total, "seq").reshape((planes, 4) + piece)
        mine = lax.dynamic_index_in_dim(every, seq & 3, 1, keepdims=False)
        place = jnp.arange(planes)
        want = place > (seq >> 2) if backward else place < (seq >> 2)
        return [jnp.sum(jnp.where(want[:, None, None, None], mine, 0.0), axis=0)]

    def scanned(own, others, backward, tok):
        return run(
            functools.partial(scan_kernel, backward, planes if planes <= 4 else None), tok, (1,),
            [(p, piece_spec) for p in own + others], [(piece, F32, piece_spec)] * 4)

    def later(own, others, tok):
        pair = (2 * per,) + piece[1:]
        (mine, x_pair, y_one), tok = run(
            functools.partial(later_kernel, planes if planes <= 4 else None), tok, (1,),
            [(p, piece_spec) for p in own + others],
            [(piece, F32, piece_spec), (pair, F32, whole(pair)), (piece, F32, piece_spec)])
        x_pair, y_one = to_member(x_pair, 1), to_member(y_one, 2)
        return [mine, x_pair, y_one, to_member(x_pair[per:], 2)], tok

    def turn(x, kinds, tok):
        shape = (2, len(kinds), half_rows, T)
        if not direct:
            return jnp.zeros(shape, BF16), tok
        (out,), tok = run(
            functools.partial(turn_kernel, kinds), tok, (1,), [(x, full)], [(shape, BF16, whole(shape))],
            [pltpu.VMEM((half_rows, T), F32)])
        return out, tok

    own = plane_exchange([s0, s1, s2, s3])

    (q, fq, nd), tok = run(
        queries_kernel, tok, (quads,),
        [(attn, full), (w_qkv, w_cols(0)), (map_query, maps), (fk, fcol), (v, qcol), (allow, square)],
        [((T, D), BF16, qcol), ((T, 2 * D), BF16, fcol), ((T, 2 * D), F32, fcol)],
        [map_scr], us=9.0)
    total, tok = plane_total(own, tok)
    others = across(total, False)
    (ga,), tok = run(
        act_back_kernel, tok, (FF // D,), [(cot, full), (w_proj, pl.BlockSpec((D, D), lambda j: (j, 0)))],
        [((T, FF), F32, whole((T, FF)), Near)], us=4.0)
    carried, tok = scanned(own, others, False, tok)
    carry = plane_exchange(carried)
    cot_t, tok = turn(cot, (0, 1, 2), tok)
    attn_t, tok = turn(attn, (0, 1, 2), tok)

    (mixed, mf, rden, hidden, mlp_in), tok = run(
        mix_kernel, tok, (quads,),
        [(x, full), (nd, fcol), (fq, fcol)] + [(c, piece_spec) for c in carry]
        + [(contin, col128), (w_out, pl.BlockSpec((QW, D), lambda j: (j, 0))), (Held(gain_m), line)],
        [((T, D), BF16, qcol), ((T, D), F32, qcol), ((T, D), F32, qcol), ((T, D), F32, full),
         ((T, D), BF16, full)],
        [state_scr], us=4.5)
    mlp_t, tok = turn(mlp_in, (0, 1, 2), tok)

    n_ff = FF // D
    turned_spec = whole((2, 3, half_rows, T))
    send_shape = (2, n_ff, half_rows, D)
    (act, gp, send_mlp), tok = run(
        mlp_kernel, tok, (n_ff,),
        [(mlp_in, full), (ga, columns(T, D)), (mlp_t, turned_spec), (cot_t, turned_spec), (Held(w_fc), columns(D, D))],
        [((T, FF), BF16, columns(T, D), Near)] * 2
        + [(send_shape, F32, pl.BlockSpec((2, 1, half_rows, D), lambda j: (0, j, 0, 0)), True)], us=10.0)
    if direct:
        recv_mlp = core_hop(send_mlp.array).reshape(2 * n_ff, half_rows, D)
    (output, gh, gh_low, gg_mlp), tok = run(
        mlp_out_kernel, tok, (quads,),
        [(act, whole((T, FF))), (gp, whole((T, FF))), (Held(w_fc), pl.BlockSpec((QW, FF), lambda j: (j, 0))),
         (Held(w_proj), columns(FF, QW)), (hidden, qcol), (hidden, full), (Held(cot), full), (Held(gain_m), line)],
        [((T, D), F32, qcol), ((T, D), F32, full), ((T, D), BF16, full), ((1, D), F32, row)],
        [pltpu.VMEM((quads, T, QW), F32)], us=8.0)
    def send_half(x_t, kinds, ys, tok):
        shape = (len(kinds), half_rows, D)
        (out,), tok = run(
            functools.partial(send_kernel, kinds), tok, (1,),
            [(x_t, whole(x_t.shape))] + [(y, full) for y in ys], [(shape, F32, whole(shape))], us=30.0)
        return core_hop(out), tok

    class Group:
        def __init__(self, counts, layout, widths):
            self.counts, self.layout, self.widths = counts, layout, widths
            self.stage, self.small = -1, None

    def wave(folds, join, tok, us=30.0):
        ins, outs, sends = [], [], {}
        plan = {"folds": [], "ends": [], "smalls": [], "joins": [], "copies": []}
        after = []

        def take(array, spec=None):
            for n, (other, other_spec) in enumerate(ins):
                if other is array and spec is None:
                    return n
            ins.append((array, spec or whole(array.shape)))
            return len(ins) - 1

        def place(bit, rows):
            base = sends.get(bit, 0)
            sends[bit] = base + rows
            return base

        def give(shape, put, not_last=True):
            outs.append((shape, F32, whole(shape), not_last and Near))
            after.append((len(outs) - 1, put))
            return ("out", len(outs) - 1)

        steps = 1
        for g in folds:
            g.stage += 1
            if g.stage == 4:
                rows = half_rows // 16
                g.result = [None] * len(g.widths)
                made = []
                if g is main:
                    plan["copies"] = [(take(early.result[0]), ("out", len(outs)))]
                for n, width in enumerate(g.widths):
                    def put(array, n=n, g=g):
                        g.result[n] = array
                    made.append(give((rows, width), put, False))
                n = 0
                for kind in range(3):
                    if g.counts[kind] == 0:
                        continue
                    got, at = g.got[kind]
                    for p in range(g.counts[kind]):
                        out, block = g.layout[n]
                        plan["ends"].append((take(g.keeps[kind]), take(got), at, made[out], (block, p)))
                        n += 1
            else:
                old_keeps, g.keeps = g.keeps, [None] * 3
                old_got, g.got = g.got, [None] * 3
                for kind in range(3):
                    if g.counts[kind] == 0:
                        continue
                    bit = ORDERS[kind][g.stage]
                    rows = old_keeps[kind].shape[0] // 2
                    base = place(bit, rows)
                    def put(array, kind=kind, g=g):
                        g.keeps[kind] = array
                    keep = give((rows, D), put)
                    got, at = old_got[kind]
                    plan["folds"].append(
                        (take(old_keeps[kind]), take(got), at, g.counts[kind], ("send", bit), base, keep))
                    g.got[kind] = (bit, base)
            if g.small is not None and g.stage < 4:
                got, at = g.small_got
                bit = SMALL_ORDER[g.stage]
                base = place(bit, SMALL_ROWS)
                def put(array, g=g):
                    g.small = array
                keep = give(small_shape, put)
                plan["smalls"].append((take(g.small), take(got), at, ("send", bit), base, keep))
                g.small_got = (bit, base)
        if join is not None:
            g, xs, ys, segments, small = join
            g.stage = 0
            g.keeps, g.got, offset = [None] * 3, [None] * 3, [0, 0, 0]
            at_x = [take(x) for x in xs]
            at_y, at_r = [], []
            for n, (y, r, block, y_block) in enumerate(ys):
                mine = [i for i, seg in enumerate(segments) if seg[2] == n]
                first, count = mine[0], len(mine)
                at_y.append(take(y, pl.BlockSpec(
                    (T, D), lambda i, first=first, count=count, block=y_block:
                    (0, block + jnp.clip(i - first, 0, count - 1)))))
                at_r.append(take(r, pl.BlockSpec(
                    (1, half_rows, D), lambda i, first=first, count=count, block=block:
                    (block + jnp.clip(i - first, 0, count - 1), 0, 0))))
            half = half_rows // 2
            for kind in range(3):
                if g.counts[kind] == 0:
                    continue
                bit = ORDERS[kind][0]
                g.got[kind] = (bit, place(bit, half * g.counts[kind]))
                def put(array, kind=kind, g=g):
                    g.keeps[kind] = array
                g.keeps[kind] = give((half * g.counts[kind], D), put)
            for x, entry, y, kind in segments:
                bit, base = g.got[kind]
                plan["joins"].append(
                    (at_x[x], entry, at_y[y], at_r[y], ("send", bit), base + offset[kind], g.keeps[kind], offset[kind]))
                offset[kind] += half
            steps = len(segments)
            if small is not None:
                bit = SMALL_ORDER[0]
                base = place(bit, SMALL_ROWS)
                def put(array, g=g):
                    g.small = array
                keep = give(small_shape, put)
                plan["smalls"].append((take(small[0]), take(small[1]), 0, ("send", bit), base, keep))
                g.small, g.small_got = True, (bit, base)
        first_send = len(outs)
        bits = sorted(sends)
        for bit in bits:
            outs.append(((sends[bit], D), F32, whole((sends[bit], D)), Near))
        n_in = len(ins)

        def ref(item):
            if isinstance(item, tuple) and item[0] == "out":
                return n_in + item[1]
            if isinstance(item, tuple) and item[0] == "send":
                return n_in + first_send + bits.index(item[1])
            return item

        plan = {name: tuple(tuple(ref(x) for x in entry) for entry in entries) for name, entries in plan.items()}
        results, tok = run(functools.partial(wave_kernel, plan), tok, (steps,), ins, outs, us=us, extra=6)
        for n, put in after:
            put(results[n])
        moved = {bit: Near(hop(results[first_send + n].array, bit)) for n, bit in enumerate(bits)}
        for g in folds + ([join[0]] if join else []):
            if g.stage < 4:
                g.got = [item and (moved[item[0]], item[1]) for item in g.got]
                if g.small is not None:
                    g.small_got = (moved[g.small_got[0]], g.small_got[1])
        return tok

    small_shape = (SMALL_ROWS, D)
    early = Group((1, 1, 1), [(0, i) for i in range(3)], (3 * D,))
    main = Group((2, 2, 1), [(0, n_ff - 1)] + [(1, i) for i in range(n_ff)], (FF, FF))
    wide = Group((1, 0, 0), [(0, 0)], (D,))
    last = Group((1, 1, 1), [(0, i) for i in range(3)], (3 * D,))
    if direct:
        tok = wave([], (early, [cot_t], [(act, recv_mlp, 0, 0)], [(0, kind, 0, kind) for kind in range(3)], None), tok, 4.0)

    (gn, gd, gd_t, s0, s1, s2, s3), tok = run(
        numer_back_kernel, tok, (quads,),
        [(gh_low, full), (Held(w_out), pl.BlockSpec((QW, D), lambda j: (j, 0))), (mf, qcol), (rden, qcol),
         (fq, fcol), (contin, col128)],
        [((T, D), BF16, qcol), ((T, D), F32, qcol),
         ((8 * H, T), F32, pl.BlockSpec((32, T), lambda j: (j, 0)))] + [(piece, F32, piece_spec)] * 4,
        [state_scr], us=5.0)
    own = plane_exchange([s0, s1, s2, s3])
    if direct:
        tok = wave(
            [early],
            (main, [cot_t, mlp_t], [(act, recv_mlp, n_ff - 1, n_ff - 1), (gp, recv_mlp, n_ff, 0)],
             [(0, 0, 0, 0)] + [(1, kind, 1, kind) for kind in (0, 1, 1, 2)], None), tok, 7.0)
    total, tok = plane_total(own, tok)
    others = across(total, True)

    def fixed(shape, quad):
        return pl.BlockSpec(shape, lambda i: (0, quad))

    def fixed_rows(shape, quad):
        return pl.BlockSpec(shape, lambda i: (quad,) + (0,) * (len(shape) - 1))

    def scores_back(quad, before, tok):
        ins = [(q, fixed((T, QW), quad)), (fq, fixed((T, FW), quad)), (fk, fixed((T, FW), quad)),
               (v, fixed((T, QW), quad)), (gn, fixed((T, QW), quad)), (gd, fixed((T, QW), quad)),
               (gd_t, fixed_rows((32, T), quad))] + [(c, piece_spec) for c in carry]
        ins += [(allow, square), (allow_t, square), (contin, col128), (map_query, fixed_rows((4, 64, 64), quad))]
        aliases = {len(ins) + i: i for i in range(4)} if before else None
        ins += [(a, ANYWHERE) for a in before]
        return run(
            functools.partial(scores_back_kernel, quad), tok, (1,), ins,
            [((T, D), BF16, fixed((T, QW), quad)), ((T, 2 * D), F32, fixed((T, FW), quad)),
             ((T, D), F32, fixed((T, QW), quad)), ((D, 128), F32, fixed_rows((QW, 128), quad))],
            [map_scr, state_scr, pltpu.VMEM((T, FW), BF16)], extra=7, aliases=aliases, us=4.5)

    backs, tok = scores_back(0, [], tok)
    backs, tok = scores_back(1, backs, tok)
    backs, tok = scores_back(2, backs, tok)
    gq, gfk, gv_f, gmq = backs
    upstream, tok = later(own, others, tok)
    if direct:
        mixed_t, tok = turn(mixed, (0,), tok)
        recv_out, tok = send_half(mixed_t, (0,), [gh_low], tok)
        tok = wave(
            [early, main], (wide, [mixed_t], [(gh_low, recv_out, 0, 0)], [(0, 0, 0, 0)], None), tok, 2.0)

    (gk, gv, gmk), tok = run(
        keys_back_kernel, tok, (quads,),
        [(k, qcol), (fk, fcol), (v, qcol), (gfk, fcol), (gv_f, qcol)] + [(c, piece_spec) for c in upstream]
        + [(tail, col128), (map_key, maps)],
        [((T, D), BF16, qcol), ((T, D), BF16, qcol),
         ((D, 128), F32, pl.BlockSpec((QW, 128), lambda j: (j, 0)))],
        [map_scr, state_scr, pltpu.VMEM((T, FW), BF16)], us=60.0)
    if direct:
        recv_qkv, tok = send_half(attn_t, (0, 1, 2), [gq, gk, gv], tok)

    small_spec = whole(small_shape)
    packed = 2 * SMALL_ROWS * (D // 128)
    (gx, keep, send), tok = run(
        inputs_back_kernel, tok, (3,),
        [(gq, full), (gk, full), (gv, full), (Held(w_qkv), columns(D, D)), (Held(x), full), (gh, full), (Held(gain_a), line),
         (gg_mlp, row), (gmq, whole((D, 128))), (gmk, whole((D, 128)))],
        [((T, D), F32, full)] + [(small_shape, F32, small_spec)] * 2,
        [pltpu.VMEM((T, D), F32), pltpu.VMEM((packed, 128), F32)], us=60.0)

    got = core_hop(send)
    if direct:
        tok = wave(
            [], (last, [attn_t], [(gq, recv_qkv, 0, 0), (gk, recv_qkv, 1, 0), (gv, recv_qkv, 2, 0)],
                 [(0, kind, kind, kind) for kind in range(3)], (keep, got)), tok, 4.0)
        tok = wave([early, main, wide], None, tok)
        tok = wave([last], None, tok)
        tok = wave([early, main, wide], None, tok)
        tok = wave([last], None, tok)
        tok = wave([main, wide], None, tok)
        tok = wave([last], None, tok)
        (mine,), tok = run(
            add_kernel, tok, (1,), [(last.small, small_spec), (last.small_got[0], small_spec)],
            [(small_shape, F32, small_spec, Near)], us=0.1)
        got = core_hop(mine.array)
        tok = wave([wide, last], None, tok)
        (grad_w_qkv,) = last.result
        grad_proj_rows, grad_w_fc = main.result
        (grad_w_out,) = wide.result
    else:
        mine = lax.psum(keep + got, "seq")
        got = core_hop(mine)
        summed = lax.psum_scatter(
            jnp.concatenate(
                [tn(attn, gq), tn(attn, gk), tn(attn, gv), tn(mixed, gh_low), tn(mlp_in, gp.array), tn(cot, act.array)],
                axis=1,
            ),
            ("batch", "seq"), scatter_dimension=0, tiled=True)
        grad_w_qkv = summed[:, : 3 * D]
        grad_w_out = summed[:, 3 * D : 4 * D]
        grad_w_fc = summed[:, 4 * D : 4 * D + FF]
        grad_proj_rows = summed[:, 4 * D + FF :]

    heads_shape = (H, 64, 64)
    (grad_map_query, grad_map_key, gains), tok = run(
        unpack_kernel, tok, (1,), [(mine, small_spec), (got, small_spec)],
        [(heads_shape, F32, whole(heads_shape))] * 2 + [((16, 128), F32, whole((16, 128)))],
        [pltpu.VMEM((packed, 128), F32)], us=0.1)
    n = D // 128
    return (
        output[None],
        gx[None],
        grad_w_qkv,
        grad_w_out,
        grad_w_fc,
        grad_proj_rows.T,
        grad_map_query,
        grad_map_key,
        gains[:n].reshape(D),
        gains[n : 2 * n].reshape(D),
    )


def solution(mesh):
    tokens = P("batch", "seq", None)
    flags = P("batch", "seq")
    rows = P(("batch", "seq"), None)
    return jax.shard_map(
        local,
        mesh=mesh,
        in_specs=(tokens,) + (P(),) * 8 + (flags, flags, tokens),
        out_specs=(tokens, tokens, rows, rows, rows, P(None, ("batch", "seq")), P(), P(), P(), P()),
        check_vma=False,
    )
```

```python
import functools

import jax
import jax.numpy as jnp
from jax import lax
from jax.experimental import pallas as pl
from jax.experimental.pallas import tpu as pltpu
from jax.sharding import PartitionSpec as P

EPSILON = 1e-05
F32 = jnp.float32
BF16 = jnp.bfloat16
STATE_ROWS = 72
SMALL_ROWS = 72
MIB = 1024 * 1024


def mm(a, b):
    return lax.dot_general(a, b, (((1,), (0,)), ((), ())), preferred_element_type=F32)


def nt(a, b):
    return lax.dot_general(a, b, (((1,), (1,)), ((), ())), preferred_element_type=F32)


def tn(a, b):
    return lax.dot_general(a, b, (((0,), (0,)), ((), ())), preferred_element_type=F32)


def split(v):
    high = v.astype(BF16)
    return high, (v - high.astype(F32)).astype(BF16)


def iota(shape, dim):
    return lax.broadcasted_iota(jnp.int32, shape, dim)


def segment_ones(width):
    shape = (width, width)
    return (iota(shape, 0) // 64 == iota(shape, 1) // 64).astype(BF16)


def segment_sum(v, ones):
    high, low = split(v)
    return mm(high, ones) + mm(low, ones)


def moments(x):
    centre = jnp.mean(x, axis=-1, keepdims=True)
    offsets = x - centre
    variance = jnp.mean(offsets * offsets, axis=-1, keepdims=True)
    scale = lax.rsqrt(variance + EPSILON)
    return offsets * scale, scale


def norm_back(grad, normed, scale, gain):
    dn = grad * gain
    first = jnp.mean(dn, axis=-1, keepdims=True)
    second = jnp.mean(dn * normed, axis=-1, keepdims=True)
    return (dn - first - normed * second) * scale


def fill_maps(scr, map_ref):
    scr[...] = jnp.zeros(scr.shape, scr.dtype)
    for h in range(4):
        m = map_ref[h].astype(F32)
        scr[64 * h : 64 * h + 64, 128 * h : 128 * h + 128] = jnp.concatenate(
            [m, -m], axis=1
        ).astype(scr.dtype)


def inverse_of(v):
    guess = pl.reciprocal(v, approx=True)
    return guess * (2.0 - v * guess)


def half_sums(v, low_half):
    top = jnp.sum(jnp.where(low_half, v, 0.0), axis=1, keepdims=True)
    bottom = jnp.sum(jnp.where(low_half, 0.0, v), axis=1, keepdims=True)
    return jnp.where(low_half, top, bottom)


def features(pre):
    low_half = iota(pre.shape, 1) < 64
    top = jnp.max(jnp.where(low_half, pre, -jnp.inf), axis=1, keepdims=True)
    bottom = jnp.max(jnp.where(low_half, -jnp.inf, pre), axis=1, keepdims=True)
    e = jnp.exp(pre - jnp.where(low_half, top, bottom))
    return e * inverse_of(half_sums(e, low_half))


def features_back(feat, grad, ones):
    low_half = iota(feat.shape, 1) < 64
    weighted = feat * grad
    mass = mm(feat.astype(BF16), ones)
    part = weighted - feat * (half_sums(weighted, low_half) * inverse_of(mass))
    return part - pltpu.roll(part, 64, 1)


def whole(shape):
    return pl.BlockSpec(shape, lambda *_: (0,) * len(shape))


def columns(rows, width):
    return pl.BlockSpec((rows, width), lambda j: (0, j))


ANYWHERE = pl.BlockSpec(memory_space=pl.ANY)


def my_core():
    return lax.axis_index("batch")


def my_seq():
    return lax.axis_index("seq")


def nbytes(shape, dtype):
    total = jnp.dtype(dtype).itemsize
    for n in shape:
        total *= n
    return total


class Held:
    def __init__(self, array):
        self.array, self.shape, self.dtype = array, array.shape, array.dtype


class Near(Held):
    pass


def run(kernel, tok, grid, ins, outs, scratch=(), extra=3, aliases=None, us=1.0):
    n_in, n_out = len(ins), len(outs)
    linked = tok is not None
    outs = [tuple(out) + (False,) * (4 - len(out)) for out in outs]

    def body(*refs):
        kernel(*refs[:n_in], *refs[n_in + linked : n_in + linked + n_out], *refs[n_in + linked + n_out + 1 :])

    held = 0
    arrays = []
    for array, spec in ins:
        near = isinstance(array, Near)
        if spec.block_shape is not None and not (near and spec.block_shape == array.shape):
            held += (1 if spec.block_shape == array.shape else 2) * nbytes(spec.block_shape, array.dtype)
        if isinstance(array, Held):
            array = pltpu.with_memory_space_constraint(array.array, pltpu.VMEM if near else pltpu.HBM)
        arrays.append(array)
    for shape, dtype, spec, stays in outs:
        if not (stays is Near and spec.block_shape == shape):
            held += (1 if spec.block_shape == shape else 2) * nbytes(spec.block_shape, dtype)
    for item in scratch:
        held += nbytes(item.shape, item.dtype)
    result = pl.pallas_call(
        body,
        grid=grid,
        in_specs=[spec for _, spec in ins] + [ANYWHERE] * linked,
        out_specs=[spec for _, _, spec, _ in outs] + [ANYWHERE],
        scratch_shapes=list(scratch),
        out_shape=[
            pltpu.VMEM(shape, dtype) if stays is Near
            else pltpu.HBM(shape, dtype) if stays else jax.ShapeDtypeStruct(shape, dtype)
            for shape, dtype, _, stays in outs
        ]
        + [jax.ShapeDtypeStruct((8, 128), F32)],
        input_output_aliases=aliases or {},
        cost_estimate=pl.CostEstimate(flops=int(us * 1.15e9), bytes_accessed=0, transcendentals=0),
        compiler_params=pltpu.CompilerParams(vmem_limit_bytes=min(held + extra * MIB, 60 * MIB)),
    )(*arrays, *([tok] if linked else []))
    results = [Near(r) if out[3] is Near else Held(r) if out[3] else r for r, out in zip(result, outs)]
    return results, result[-1]


def keys_kernel(x_ref, gain_ref, wk_ref, wv_ref, map_ref, mask_ref, starts_ref,
                attn_ref, k_ref, v_ref, fk_ref, p0, p1, p2, p3,
                allow_ref, allow_t_ref, tail_ref, contin_ref,
                map_scr, state_scr):
    j = pl.program_id(0)
    tokens = x_ref.shape[0]
    n_flags = starts_ref.shape[1]
    unit = tokens // n_flags

    def seg(shape, dim):
        place = iota(shape, dim)
        total = jnp.zeros(shape, jnp.int32)
        for u in range(n_flags):
            total = total + jnp.where(place >= unit * u, starts_ref[0, u], 0)
        return total

    @pl.when(j == 0)
    def _():
        normed, _ = moments(x_ref[...].astype(F32))
        attn_ref[...] = (normed * gain_ref[...].reshape(1, -1)).astype(BF16)
        last = starts_ref[0, 0]
        for u in range(1, n_flags):
            last = last + starts_ref[0, u]
        mask_row = mask_ref[...].astype(F32)
        mask_col = jnp.transpose(jnp.broadcast_to(mask_row, (128, tokens)))
        seg_col = seg((tokens, 128), 0)
        tail_ref[...] = jnp.where(seg_col == last, mask_col, 0.0)
        contin_ref[...] = jnp.where(seg_col == 0, 1.0, 0.0)
        square = (tokens, tokens)
        same = seg(square, 0) == seg(square, 1)
        allow_ref[...] = jnp.where(same & (iota(square, 1) <= iota(square, 0)), mask_row, 0.0)
        wide_mask = jnp.concatenate([mask_col] * (tokens // 128), axis=1)
        allow_t_ref[...] = jnp.where(same & (iota(square, 0) <= iota(square, 1)), wide_mask, 0.0)

    fill_maps(map_scr, map_ref)
    attn = attn_ref[...]
    k4 = mm(attn, wk_ref[...]).astype(BF16)
    v4 = mm(attn, wv_ref[...]).astype(BF16)
    k_ref[...] = k4
    v_ref[...] = v4
    pre = mm(k4, map_scr[...])
    ones = segment_ones(128)
    v_t = jnp.transpose(v4.astype(F32)).astype(BF16)
    tail = tail_ref[...]
    row_ones = jnp.ones((16, tokens), BF16)
    for h in range(4):
        feat = features(pre[:, 128 * h : 128 * h + 128]).astype(BF16)
        fk_ref[:, 128 * h : 128 * h + 128] = feat
        kept = (feat.astype(F32) * tail).astype(BF16)
        rows = jnp.concatenate([v_t[64 * h : 64 * h + 64], row_ones], axis=0)
        state_scr[4 * j + h] = mm(rows, kept)[0:STATE_ROWS]

    @pl.when(j == pl.num_programs(0) - 1)
    def _():
        for k, piece in enumerate((p0, p1, p2, p3)):
            n = piece.shape[0]
            piece[...] = state_scr[pl.ds(((my_seq() & 3) ^ k) * n, n)]


def queries_kernel(attn_ref, wq_ref, map_ref, fk_ref, v_ref, allow_ref,
                   q_ref, fq_ref, nd_ref, map_scr):
    tokens = attn_ref.shape[0]
    half = tokens // 2
    fill_maps(map_scr, map_ref)
    q4 = mm(attn_ref[...], wq_ref[...]).astype(BF16)
    q_ref[...] = q4
    pre = mm(q4, map_scr[...])
    ones = segment_ones(128)
    low_half = iota((tokens, 128), 1) < 64
    for h in range(4):
        lanes = slice(128 * h, 128 * h + 128)
        feat = features(pre[:, lanes]).astype(BF16)
        fq_ref[:, lanes] = feat
        fk = fk_ref[:, lanes]
        pair = v_ref[:, 128 * (h // 2) : 128 * (h // 2) + 128].astype(F32)
        if h % 2:
            pair = pltpu.roll(pair, 64, 1)
        wide = jnp.where(low_half, pair, 1.0).astype(BF16)
        first = nt(feat[:half], fk[:half]) * allow_ref[:half, :half]
        nd_ref[:half, lanes] = mm(first.astype(BF16), wide[:half])
        second = nt(feat[half:], fk) * allow_ref[half:, :]
        nd_ref[half:, lanes] = mm(second.astype(BF16), wide)


def plane_sum_kernel(*refs):
    *pieces, out = refs
    total = pieces[0][...]
    for piece in pieces[1:]:
        total = total + piece[...]
    out[...] = total


def scan_kernel(backward, planes, *refs):
    own = refs[:4]
    others = refs[4:-4]
    outs = refs[-4:]
    member, plane = my_seq() & 3, my_seq() >> 2
    total = jnp.zeros(own[0].shape, F32)
    for i, other in enumerate(others):
        if planes is None:
            total = total + other[...]
        else:
            there = plane + i + 1 < planes if backward else plane - i - 1 >= 0
            total = total + jnp.where(there, other[...], 0.0)
    for k, out in enumerate(outs):
        value = total
        target = member ^ k
        for i, piece in enumerate(own):
            source = member ^ i
            counts = source > target if backward else source < target
            value = value + jnp.where(counts, piece[...], 0.0)
        out[...] = value


def later_kernel(planes, own0, own1, own2, own3, *refs):
    own, others, (mine, x_pair, y_one) = (own0, own1, own2, own3), refs[:-3], refs[-3:]
    member, plane = my_seq() & 3, my_seq() >> 2
    total = jnp.zeros(own0.shape, F32)
    for i, other in enumerate(others):
        if planes is None:
            total = total + other[...]
        else:
            total = total + jnp.where(plane + i + 1 < planes, other[...], 0.0)
    n = own0.shape[0]
    for k in range(4):
        value = total
        for i, piece in enumerate(own):
            value = value + jnp.where((member ^ i) > (member ^ k), piece[...], 0.0)
        if k == 0:
            mine[...] = value
        elif k == 2:
            y_one[...] = value
        else:
            x_pair[n * (k // 2) : n * (k // 2) + n] = value


def place_heads(scr, pieces):
    for k, piece in enumerate(pieces):
        n = piece.shape[0]
        scr[pl.ds(((my_seq() & 3) ^ k) * n, n)] = piece[...]


def mix_kernel(x_ref, nd_ref, fq_ref, c0, c1, c2, c3, contin_ref, wo_ref, gain_ref,
               mixed_ref, mf_ref, rden_ref, hidden_ref, mlp_ref, carry_scr):
    j = pl.program_id(0)
    tokens = x_ref.shape[0]
    low_half = iota((tokens, 128), 1) < 64

    @pl.when(j == 0)
    def _():
        place_heads(carry_scr, (c0, c1, c2, c3))
        hidden_ref[...] = x_ref[...].astype(F32)

    contin = contin_ref[...]
    for pair in range(2):
        quotients, inverses = [], []
        for side in range(2):
            h = 2 * pair + side
            lanes = slice(128 * h, 128 * h + 128)
            carry = carry_scr[4 * j + h]
            wide = jnp.concatenate([carry[:64], jnp.broadcast_to(carry[64:65], (64, 128))], axis=0)
            high, low = split(wide)
            fq = fq_ref[:, lanes]
            nd = nd_ref[:, lanes] + contin * (nt(fq, high) + nt(fq, low))
            inverse = inverse_of(nd)
            turned = pltpu.roll(inverse, 64, 1)
            quotient = nd * turned
            if side:
                quotients.append(pltpu.roll(quotient, 64, 1))
                inverses.append(inverse)
            else:
                quotients.append(quotient)
                inverses.append(turned)
        lanes = slice(128 * pair, 128 * pair + 128)
        mf = jnp.where(low_half, *quotients)
        mf_ref[:, lanes] = mf
        mixed_ref[:, lanes] = mf.astype(BF16)
        rden_ref[:, lanes] = jnp.where(low_half, *inverses)
    hidden_ref[...] += mm(mixed_ref[...], wo_ref[...])

    @pl.when(j == pl.num_programs(0) - 1)
    def _():
        normed, _ = moments(hidden_ref[...])
        mlp_ref[...] = (normed * gain_ref[...].reshape(1, -1)).astype(BF16)


GELU_A, GELU_C = 0.044715, 0.7978845608028654


def turn_kernel(kinds, x_ref, out_ref, scr):
    rows, half = out_ref.shape[2] // 16, out_ref.shape[2]
    for side in range(2):
        core = my_core() if side else 1 - my_core()
        turned = jnp.transpose(
            x_ref[:, pl.ds(pl.multiple_of(core * half, 128), half)].astype(F32)
        )
        for at, kind in enumerate(kinds):
            for g in range(16):
                place = g ^ my_seq()
                spot = 0
                for depth, bit in enumerate(ORDERS[kind]):
                    spot = spot + (((place >> bit) & 1) << (3 - depth))
                scr[pl.ds(pl.multiple_of(spot * rows, 8), rows), :] = turned[rows * g : rows * g + rows]
            out_ref[side, at] = scr[...].astype(BF16)


def act_back_kernel(cot_ref, wp_ref, ga_ref):
    width = wp_ref.shape[0]
    start = pl.multiple_of(pl.program_id(0) * width, 128)
    ga_ref[:, pl.ds(start, width)] = nt(cot_ref[...], wp_ref[...])


def mlp_kernel(mlp_ref, ga_ref, mlp_t, cot_t, wf_ref, act_ref, gp_ref, send_ref):
    j = pl.program_id(0)
    tokens, width = mlp_ref.shape[0], wf_ref.shape[1]
    lanes = slice(0, width)
    step = tokens // 4
    for r in range(4):
        rows = slice(step * r, step * r + step)
        u = mm(mlp_ref[rows, :], wf_ref[...])
        square = u * u
        t = jnp.tanh(GELU_C * (u + GELU_A * (u * square)))
        half = 0.5 * (1.0 + t)
        act_ref[rows, lanes] = (u * half).astype(BF16)
        slope = half + (0.5 * GELU_C) * u * (1.0 - t * t) * (1.0 + (3.0 * GELU_A) * square)
        gp_ref[rows, lanes] = (ga_ref[rows, lanes] * slope).astype(BF16)
    send_ref[0, 0] = mm(cot_t[0, j % 3], act_ref[:, lanes])
    send_ref[1, 0] = mm(mlp_t[0, (j + 1) // 2], gp_ref[:, lanes])


def mlp_out_kernel(act_ref, gp_ref, wf_ref, wp_ref, part_ref, hidden_ref, cot_ref, gain_ref,
                   out_ref, gh_ref, gh_low_ref, gg_ref, back_scr):
    j = pl.program_id(0)
    out_ref[...] = part_ref[...] + mm(act_ref[...], wp_ref[...])
    back_scr[j] = nt(gp_ref[...], wf_ref[...])

    @pl.when(j == pl.num_programs(0) - 1)
    def _():
        normed, scale = moments(hidden_ref[...])
        grad = jnp.concatenate([back_scr[i] for i in range(back_scr.shape[0])], axis=1)
        gg_ref[...] = jnp.sum(grad * normed, axis=0, keepdims=True)
        gh = cot_ref[...].astype(F32) + norm_back(grad, normed, scale, gain_ref[...].reshape(1, -1))
        gh_ref[...] = gh
        gh_low_ref[...] = gh.astype(BF16)


def numer_back_kernel(gh_ref, wo_ref, mf_ref, rden_ref, fq_ref, contin_ref,
                      gn_ref, gd_ref, gd_t_ref, p0, p1, p2, p3, state_scr):
    j = pl.program_id(0)
    gm = nt(gh_ref[...], wo_ref[...]) * rden_ref[...]
    gn_ref[...] = gm.astype(BF16)
    gd = -segment_sum(gm * mf_ref[...], segment_ones(256))
    gd_ref[...] = gd
    gn_t = jnp.transpose(gm).astype(BF16)
    gd_t = jnp.transpose(gd)
    contin = contin_ref[...]
    for h in range(4):
        rows = gd_t[64 * h : 64 * h + 8]
        gd_t_ref[8 * h : 8 * h + 8, :] = rows
        kept = (fq_ref[:, 128 * h : 128 * h + 128].astype(F32) * contin).astype(BF16)
        high, low = split(rows)
        both = jnp.concatenate([high.astype(F32), low.astype(F32)], axis=0).astype(BF16)
        sums = mm(jnp.concatenate([gn_t[64 * h : 64 * h + 64], both], axis=0), kept)
        state_scr[4 * j + h, 0:64, :] = sums[0:64]
        state_scr[4 * j + h, 64:72, :] = sums[64:72] + sums[72:80]

    @pl.when(j == pl.num_programs(0) - 1)
    def _():
        for k, piece in enumerate((p0, p1, p2, p3)):
            n = piece.shape[0]
            piece[...] = state_scr[pl.ds(((my_seq() & 3) ^ k) * n, n)]


def side_rows(state, side):
    zeros = jnp.zeros((64, 128), F32)
    rows = state[:64]
    return jnp.concatenate([zeros, rows] if side else [rows, zeros], axis=0)


def scores_back_kernel(j, q_ref, fq_ref, fk_ref, v_ref, gn_ref, gd_ref, gd_t_ref,
                       c0, c1, c2, c3, allow_ref, allow_t_ref, contin_ref, map_ref, *rest):
    gq_ref, gfk_ref, gv_ref, gmap_ref, map_scr, carry_scr, d_scr = rest[-7:]
    tokens = q_ref.shape[0]
    half = tokens // 2
    place_heads(carry_scr, (c0, c1, c2, c3))

    fill_maps(map_scr, map_ref)
    ones = segment_ones(128)
    low_half = iota((tokens, 128), 1) < 64
    contin = contin_ref[...]
    for pair in range(2):
        pair_lanes = slice(128 * pair, 128 * pair + 128)
        v_pair = v_ref[:, pair_lanes]
        gn_pair = gn_ref[:, pair_lanes].astype(F32)
        gd_pair = gd_ref[:, pair_lanes]
        gd_turned = pltpu.roll(gd_pair, 64, 1)
        gv_parts = []
        for side in range(2):
            h = 2 * pair + side
            lanes = slice(128 * h, 128 * h + 128)
            mine = ~low_half if side else low_half
            gn = jnp.where(mine, gn_pair, 0.0).astype(BF16)
            gd = jnp.where(mine, gd_pair, gd_turned)
            gd_row = gd_t_ref[8 * h : 8 * h + 1, :]
            fq, fk = fq_ref[:, lanes], fk_ref[:, lanes]
            gd_few = jnp.concatenate([gd] * (half // 128), axis=1)
            gd_many = jnp.concatenate([gd] * (tokens // 128), axis=1)
            g_top = ((nt(gn[:half], v_pair[:half]) + gd_few[:half]) * allow_ref[:half, :half]).astype(BF16)
            g_bot = ((nt(gn[half:], v_pair) + gd_many[half:]) * allow_ref[half:, :]).astype(BF16)
            carry = carry_scr[4 * j + h]
            high, low = split(side_rows(carry, side))
            inter = mm(gn, high) + mm(gn, low) + gd * carry[64:65]
            gfq = jnp.concatenate([mm(g_top, fk[:half]), mm(g_bot, fk)], axis=0) + contin * inter
            d_scr[:, lanes] = features_back(fq.astype(F32), gfq, ones).astype(BF16)

            at_top, at_bot = allow_t_ref[:half, :], allow_t_ref[half:, half:]
            gt_top = ((nt(v_pair[:half], gn) + gd_row) * at_top).astype(BF16)
            gt_bot = ((nt(v_pair[half:], gn[half:]) + gd_row[:, half:]) * at_bot).astype(BF16)
            gfk_ref[:half, lanes] = mm(gt_top, fq)
            gfk_ref[half:, lanes] = mm(gt_bot, fq[half:])
            st_top = (nt(fk[:half], fq) * at_top).astype(BF16)
            st_bot = (nt(fk[half:], fq[half:]) * at_bot).astype(BF16)
            gv_parts.append(jnp.concatenate([mm(st_top, gn), mm(st_bot, gn[half:])], axis=0))
        gv_ref[:, pair_lanes] = gv_parts[0] + gv_parts[1]
    d = d_scr[...]
    gq_ref[...] = (0.5 * nt(d, map_scr[...])).astype(BF16)
    gm = tn(q_ref[...], d)
    for h in range(4):
        gmap_ref[64 * h : 64 * h + 64, :] = gm[64 * h : 64 * h + 64, 128 * h : 128 * h + 128]


def keys_back_kernel(k_ref, fk_ref, v_ref, gfk_ref, gv_ref, u0, u1, u2, u3, tail_ref, map_ref,
                     gk_ref, gvb_ref, gmap_ref, map_scr, up_scr, d_scr):
    j = pl.program_id(0)

    @pl.when(j == 0)
    def _():
        place_heads(up_scr, (u0, u1, u2, u3))

    fill_maps(map_scr, map_ref)
    ones = segment_ones(128)
    tail = tail_ref[...]
    for pair in range(2):
        pair_lanes = slice(128 * pair, 128 * pair + 128)
        v_pair = v_ref[:, pair_lanes]
        gv = gv_ref[:, pair_lanes]
        for side in range(2):
            h = 2 * pair + side
            lanes = slice(128 * h, 128 * h + 128)
            up = up_scr[4 * j + h]
            high, low = split(side_rows(up, side))
            fk = fk_ref[:, lanes]
            key_term = mm(v_pair, high) + mm(v_pair, low) + up[64:65]
            gfk = gfk_ref[:, lanes] + tail * key_term
            gv = gv + tail * (nt(fk, high) + nt(fk, low))
            d_scr[:, lanes] = features_back(fk.astype(F32), gfk, ones).astype(BF16)
        gvb_ref[:, pair_lanes] = gv.astype(BF16)
    d = d_scr[...]
    gk_ref[...] = (0.5 * nt(d, map_scr[...])).astype(BF16)
    gm = tn(k_ref[...], d)
    for h in range(4):
        gmap_ref[64 * h : 64 * h + 64, :] = gm[64 * h : 64 * h + 64, 128 * h : 128 * h + 128]


def inputs_back_kernel(gq_ref, gk_ref, gv_ref, w_ref, x_ref, gh_ref, gain_ref, gg_mlp_ref,
                       gmq_ref, gmk_ref, gx_ref, keep_ref, send_ref, acc, pack):
    j = pl.program_id(0)

    @pl.when(j == 0)
    def _():
        acc[...] = nt(gq_ref[...], w_ref[...])
        rows = gmq_ref.shape[0]
        low_half = iota(gmq_ref.shape, 1) < 64
        pack[:rows, :] = jnp.where(low_half, gmq_ref[...], pltpu.roll(gmk_ref[...], 64, 1))
        pack[rows:, :] = jnp.zeros((pack.shape[0] - rows, 128), F32)

    @pl.when(j == 1)
    def _():
        acc[...] += nt(gk_ref[...], w_ref[...])

    @pl.when(j == 2)
    def _():
        grad = acc[...] + nt(gv_ref[...], w_ref[...])
        normed, scale = moments(x_ref[...].astype(F32))
        gx_ref[...] = gh_ref[...] + norm_back(grad, normed, scale, gain_ref[...].reshape(1, -1))
        gg = jnp.sum(grad * normed, axis=0, keepdims=True)
        rows = gmq_ref.shape[0]
        n = gg.shape[1] // 128
        for i in range(n):
            pack[rows + i : rows + i + 1, :] = gg[:, 128 * i : 128 * i + 128]
            pack[rows + n + i : rows + n + i + 1, :] = gg_mlp_ref[:, 128 * i : 128 * i + 128]
        for out, core in ((keep_ref, my_core()), (send_ref, 1 - my_core())):
            for c in range(n):
                start = core * (n * SMALL_ROWS) + c * SMALL_ROWS
                out[:, 128 * c : 128 * c + 128] = pack[pl.ds(pl.multiple_of(start, 8), SMALL_ROWS), :]


def add_kernel(a_ref, b_ref, out_ref):
    out_ref[...] = a_ref[...] + b_ref[...]


def unpack_kernel(kept_ref, other_ref, gmq_ref, gmk_ref, gains_ref, pack):
    n = kept_ref.shape[1] // 128
    for value, core in ((kept_ref[...], my_core()), (other_ref[...], 1 - my_core())):
        for c in range(n):
            start = core * (n * SMALL_ROWS) + c * SMALL_ROWS
            pack[pl.ds(pl.multiple_of(start, 8), SMALL_ROWS), :] = value[:, 128 * c : 128 * c + 128]
    heads = gmq_ref.shape[0]
    for h in range(heads):
        both = pack[64 * h : 64 * h + 64, :]
        gmq_ref[h] = both[:, :64]
        gmk_ref[h] = both[:, 64:]
    gains_ref[...] = pack[64 * heads : 64 * heads + 16, :]


ORDERS = ((0, 1, 2, 3), (1, 2, 0, 3), (2, 0, 1, 3))
SMALL_ORDER = (3, 0, 1, 2)


def send_kernel(kinds, x_ref, *refs):
    out_ref = refs[-1]
    for i, kind in enumerate(kinds):
        out_ref[i] = mm(x_ref[0, kind], refs[i][...])


def wave_kernel(plan, *refs):
    i = pl.program_id(0)

    @pl.when(i == 0)
    def _():
        for kept, got, at, count, send, base, keep in plan["folds"]:
            rows = refs[kept].shape[0] // count
            half = rows // 2
            for p in range(count):
                total = (refs[kept][rows * p : rows * p + rows, :]
                         + refs[got][at + rows * p : at + rows * p + rows, :])
                refs[send][base + half * p : base + half * p + half, :] = total[half:]
                refs[keep][half * p : half * p + half, :] = total[:half]
        for whence, out in plan["copies"]:
            refs[out][:, : refs[whence].shape[1]] = refs[whence][...]
        for kept, got, at, out, block in plan["ends"]:
            rows, width = refs[out].shape[0], refs[kept].shape[1]
            first, piece = block
            refs[out][:, width * first : width * first + width] = (
                refs[kept][rows * piece : rows * piece + rows, :]
                + refs[got][at + rows * piece : at + rows * piece + rows, :]
            )
        for kept, got, at, send, base, keep in plan["smalls"]:
            rows = refs[kept].shape[0]
            total = refs[kept][...] + refs[got][at : at + rows, :]
            refs[keep][...] = total
            refs[send][base : base + rows, :] = total

    for step, (x, entry, y, r, send, base, keep, at) in enumerate(plan["joins"]):

        @pl.when(i == step)
        def _():
            value = mm(refs[x][1, entry], refs[y][...]) + refs[r][0]
            half = value.shape[0] // 2
            refs[send][base : base + half, :] = value[half:]
            refs[keep][at : at + half, :] = value[:half]


def core_hop(v):
    return lax.ppermute(v, "batch", [(0, 1), (1, 0)])


def local(inputs, w_qkv, w_out, w_fc, w_proj, map_query, map_key, gain_attn, gain_mlp,
          starts, key_mask, cotangent):
    T, D = inputs.shape[1], inputs.shape[2]
    H = map_query.shape[0]
    FF = w_fc.shape[1]
    n_seq = lax.axis_size("seq")
    planes = n_seq // 4
    quads = H // 4
    QW, FW = 4 * 64, 4 * 128
    half_rows = D // 2
    per = H // 4
    seq = lax.axis_index("seq")
    tok = None
    x, cot = inputs[0], cotangent[0]
    gain_a, gain_m = gain_attn, gain_mlp
    direct = n_seq == 16

    def hop(v, bit):
        return lax.ppermute(v, "seq", [(i, i ^ (1 << bit)) for i in range(n_seq)])

    def to_member(v, k):
        return lax.ppermute(v, "seq", [(i, i ^ k) for i in range(n_seq)])

    def shift(v, by):
        return lax.ppermute(v, "seq", [(i, (i + by) % n_seq) for i in range(n_seq)])

    qcol = pl.BlockSpec((T, QW), lambda j: (0, j))
    fcol = pl.BlockSpec((T, FW), lambda j: (0, j))
    col128 = whole((T, 128))
    square = whole((T, T))
    full = whole((T, D))
    row = whole((1, D))
    line = whole((D,))
    maps = pl.BlockSpec((4, 64, 64), lambda j: (j, 0, 0))
    piece = (per, STATE_ROWS, 128)
    piece_spec = whole(piece)
    map_scr = pltpu.VMEM((QW, FW), BF16)
    state_scr = pltpu.VMEM((H, STATE_ROWS, 128), F32)

    def w_cols(part):
        return pl.BlockSpec((D, QW), lambda j: (0, part * quads + j))

    (attn, k, v, fk, s0, s1, s2, s3, allow, allow_t, tail, contin), tok = run(
        keys_kernel, tok, (quads,),
        [(Held(x), full), (Held(gain_a), line), (Held(w_qkv), w_cols(1)), (Held(w_qkv), w_cols(2)), (Held(map_key), maps),
         (Held(key_mask), whole((1, T))), (starts, pl.BlockSpec(memory_space=pltpu.SMEM))],
        [((T, D), BF16, full), ((T, D), BF16, qcol), ((T, D), BF16, qcol), ((T, 2 * D), BF16, fcol)]
        + [(piece, F32, piece_spec)] * 4
        + [((T, T), F32, square)] * 2 + [((T, 128), F32, col128)] * 2,
        [map_scr, state_scr], us=8.0)

    def plane_exchange(pieces):
        return [pieces[0]] + [to_member(pieces[k], k) for k in range(1, 4)]

    def plane_total(own, tok):
        (total,), tok = run(
            plane_sum_kernel, tok, (1,), [(p, piece_spec) for p in own], [(piece, F32, piece_spec)])
        return total, tok

    def across(total, backward):
        if planes <= 4:
            return [shift(total, (-4 if backward else 4) * i) for i in range(1, planes)]
        every = lax.all_gather(total, "seq").reshape((planes, 4) + piece)
        mine = lax.dynamic_index_in_dim(every, seq & 3, 1, keepdims=False)
        place = jnp.arange(planes)
        want = place > (seq >> 2) if backward else place < (seq >> 2)
        return [jnp.sum(jnp.where(want[:, None, None, None], mine, 0.0), axis=0)]

    def scanned(own, others, backward, tok):
        return run(
            functools.partial(scan_kernel, backward, planes if planes <= 4 else None), tok, (1,),
            [(p, piece_spec) for p in own + others], [(piece, F32, piece_spec)] * 4)

    def later(own, others, tok):
        pair = (2 * per,) + piece[1:]
        (mine, x_pair, y_one), tok = run(
            functools.partial(later_kernel, planes if planes <= 4 else None), tok, (1,),
            [(p, piece_spec) for p in own + others],
            [(piece, F32, piece_spec), (pair, F32, whole(pair)), (piece, F32, piece_spec)])
        x_pair, y_one = to_member(x_pair, 1), to_member(y_one, 2)
        return [mine, x_pair, y_one, to_member(x_pair[per:], 2)], tok

    def turn(x, kinds, tok):
        shape = (2, len(kinds), half_rows, T)
        if not direct:
            return jnp.zeros(shape, BF16), tok
        (out,), tok = run(
            functools.partial(turn_kernel, kinds), tok, (1,), [(x, full)], [(shape, BF16, whole(shape))],
            [pltpu.VMEM((half_rows, T), F32)])
        return out, tok

    own = plane_exchange([s0, s1, s2, s3])

    (q, fq, nd), tok = run(
        queries_kernel, tok, (quads,),
        [(attn, full), (w_qkv, w_cols(0)), (map_query, maps), (fk, fcol), (v, qcol), (allow, square)],
        [((T, D), BF16, qcol), ((T, 2 * D), BF16, fcol), ((T, 2 * D), F32, fcol)],
        [map_scr], us=9.0)
    total, tok = plane_total(own, tok)
    others = across(total, False)
    (ga,), tok = run(
        act_back_kernel, tok, (FF // D,), [(cot, full), (w_proj, pl.BlockSpec((D, D), lambda j: (j, 0)))],
        [((T, FF), F32, whole((T, FF)), Near)], us=4.0)
    carried, tok = scanned(own, others, False, tok)
    carry = plane_exchange(carried)
    cot_t, tok = turn(cot, (0, 1, 2), tok)
    attn_t, tok = turn(attn, (0, 1, 2), tok)

    (mixed, mf, rden, hidden, mlp_in), tok = run(
        mix_kernel, tok, (quads,),
        [(x, full), (nd, fcol), (fq, fcol)] + [(c, piece_spec) for c in carry]
        + [(contin, col128), (w_out, pl.BlockSpec((QW, D), lambda j: (j, 0))), (Held(gain_m), line)],
        [((T, D), BF16, qcol), ((T, D), F32, qcol), ((T, D), F32, qcol), ((T, D), F32, full),
         ((T, D), BF16, full)],
        [state_scr], us=4.5)
    mlp_t, tok = turn(mlp_in, (0, 1, 2), tok)

    n_ff = FF // D
    turned_spec = whole((2, 3, half_rows, T))
    send_shape = (2, n_ff, half_rows, D)
    (act, gp, send_mlp), tok = run(
        mlp_kernel, tok, (n_ff,),
        [(mlp_in, full), (ga, columns(T, D)), (mlp_t, turned_spec), (cot_t, turned_spec), (Held(w_fc), columns(D, D))],
        [((T, FF), BF16, columns(T, D), Near)] * 2
        + [(send_shape, F32, pl.BlockSpec((2, 1, half_rows, D), lambda j: (0, j, 0, 0)), True)], us=10.0)
    if direct:
        recv_mlp = core_hop(send_mlp.array).reshape(2 * n_ff, half_rows, D)
    (output, gh, gh_low, gg_mlp), tok = run(
        mlp_out_kernel, tok, (quads,),
        [(act, whole((T, FF))), (gp, whole((T, FF))), (Held(w_fc), pl.BlockSpec((QW, FF), lambda j: (j, 0))),
         (Held(w_proj), columns(FF, QW)), (hidden, qcol), (hidden, full), (Held(cot), full), (Held(gain_m), line)],
        [((T, D), F32, qcol), ((T, D), F32, full), ((T, D), BF16, full), ((1, D), F32, row)],
        [pltpu.VMEM((quads, T, QW), F32)], us=8.0)
    def send_half(x_t, kinds, ys, tok):
        shape = (len(kinds), half_rows, D)
        (out,), tok = run(
            functools.partial(send_kernel, kinds), tok, (1,),
            [(x_t, whole(x_t.shape))] + [(y, full) for y in ys], [(shape, F32, whole(shape))], us=30.0)
        return core_hop(out), tok

    class Group:
        def __init__(self, counts, layout, widths):
            self.counts, self.layout, self.widths = counts, layout, widths
            self.stage, self.small = -1, None

    def wave(folds, join, tok, us=30.0):
        ins, outs, sends = [], [], {}
        plan = {"folds": [], "ends": [], "smalls": [], "joins": [], "copies": []}
        after = []

        def take(array, spec=None):
            for n, (other, other_spec) in enumerate(ins):
                if other is array and spec is None:
                    return n
            ins.append((array, spec or whole(array.shape)))
            return len(ins) - 1

        def place(bit, rows):
            base = sends.get(bit, 0)
            sends[bit] = base + rows
            return base

        def give(shape, put, not_last=True):
            outs.append((shape, F32, whole(shape), not_last and Near))
            after.append((len(outs) - 1, put))
            return ("out", len(outs) - 1)

        steps = 1
        for g in folds:
            g.stage += 1
            if g.stage == 4:
                rows = half_rows // 16
                g.result = [None] * len(g.widths)
                made = []
                if g is main:
                    plan["copies"] = [(take(early.result[0]), ("out", len(outs)))]
                for n, width in enumerate(g.widths):
                    def put(array, n=n, g=g):
                        g.result[n] = array
                    made.append(give((rows, width), put, False))
                n = 0
                for kind in range(3):
                    if g.counts[kind] == 0:
                        continue
                    got, at = g.got[kind]
                    for p in range(g.counts[kind]):
                        out, block = g.layout[n]
                        plan["ends"].append((take(g.keeps[kind]), take(got), at, made[out], (block, p)))
                        n += 1
            else:
                old_keeps, g.keeps = g.keeps, [None] * 3
                old_got, g.got = g.got, [None] * 3
                for kind in range(3):
                    if g.counts[kind] == 0:
                        continue
                    bit = ORDERS[kind][g.stage]
                    rows = old_keeps[kind].shape[0] // 2
                    base = place(bit, rows)
                    def put(array, kind=kind, g=g):
                        g.keeps[kind] = array
                    keep = give((rows, D), put)
                    got, at = old_got[kind]
                    plan["folds"].append(
                        (take(old_keeps[kind]), take(got), at, g.counts[kind], ("send", bit), base, keep))
                    g.got[kind] = (bit, base)
            if g.small is not None and g.stage < 4:
                got, at = g.small_got
                bit = SMALL_ORDER[g.stage]
                base = place(bit, SMALL_ROWS)
                def put(array, g=g):
                    g.small = array
                keep = give(small_shape, put)
                plan["smalls"].append((take(g.small), take(got), at, ("send", bit), base, keep))
                g.small_got = (bit, base)
        if join is not None:
            g, xs, ys, segments, small = join
            g.stage = 0
            g.keeps, g.got, offset = [None] * 3, [None] * 3, [0, 0, 0]
            at_x = [take(x) for x in xs]
            at_y, at_r = [], []
            for n, (y, r, block, y_block) in enumerate(ys):
                mine = [i for i, seg in enumerate(segments) if seg[2] == n]
                first, count = mine[0], len(mine)
                at_y.append(take(y, pl.BlockSpec(
                    (T, D), lambda i, first=first, count=count, block=y_block:
                    (0, block + jnp.clip(i - first, 0, count - 1)))))
                at_r.append(take(r, pl.BlockSpec(
                    (1, half_rows, D), lambda i, first=first, count=count, block=block:
                    (block + jnp.clip(i - first, 0, count - 1), 0, 0))))
            half = half_rows // 2
            for kind in range(3):
                if g.counts[kind] == 0:
                    continue
                bit = ORDERS[kind][0]
                g.got[kind] = (bit, place(bit, half * g.counts[kind]))
                def put(array, kind=kind, g=g):
                    g.keeps[kind] = array
                g.keeps[kind] = give((half * g.counts[kind], D), put)
            for x, entry, y, kind in segments:
                bit, base = g.got[kind]
                plan["joins"].append(
                    (at_x[x], entry, at_y[y], at_r[y], ("send", bit), base + offset[kind], g.keeps[kind], offset[kind]))
                offset[kind] += half
            steps = len(segments)
            if small is not None:
                bit = SMALL_ORDER[0]
                base = place(bit, SMALL_ROWS)
                def put(array, g=g):
                    g.small = array
                keep = give(small_shape, put)
                plan["smalls"].append((take(small[0]), take(small[1]), 0, ("send", bit), base, keep))
                g.small, g.small_got = True, (bit, base)
        first_send = len(outs)
        bits = sorted(sends)
        for bit in bits:
            outs.append(((sends[bit], D), F32, whole((sends[bit], D)), Near))
        n_in = len(ins)

        def ref(item):
            if isinstance(item, tuple) and item[0] == "out":
                return n_in + item[1]
            if isinstance(item, tuple) and item[0] == "send":
                return n_in + first_send + bits.index(item[1])
            return item

        plan = {name: tuple(tuple(ref(x) for x in entry) for entry in entries) for name, entries in plan.items()}
        results, tok = run(functools.partial(wave_kernel, plan), tok, (steps,), ins, outs, us=us, extra=6)
        for n, put in after:
            put(results[n])
        moved = {bit: Near(hop(results[first_send + n].array, bit)) for n, bit in enumerate(bits)}
        for g in folds + ([join[0]] if join else []):
            if g.stage < 4:
                g.got = [item and (moved[item[0]], item[1]) for item in g.got]
                if g.small is not None:
                    g.small_got = (moved[g.small_got[0]], g.small_got[1])
        return tok

    small_shape = (SMALL_ROWS, D)
    early = Group((1, 1, 1), [(0, i) for i in range(3)], (3 * D,))
    main = Group((2, 2, 1), [(0, n_ff - 1)] + [(1, i) for i in range(n_ff)], (FF, FF))
    wide = Group((1, 0, 0), [(0, 0)], (D,))
    last = Group((1, 1, 1), [(0, i) for i in range(3)], (3 * D,))
    if direct:
        tok = wave([], (early, [cot_t], [(act, recv_mlp, 0, 0)], [(0, kind, 0, kind) for kind in range(3)], None), tok, 4.0)

    (gn, gd, gd_t, s0, s1, s2, s3), tok = run(
        numer_back_kernel, tok, (quads,),
        [(gh_low, full), (w_out, pl.BlockSpec((QW, D), lambda j: (j, 0))), (mf, qcol), (rden, qcol),
         (fq, fcol), (contin, col128)],
        [((T, D), BF16, qcol), ((T, D), F32, qcol),
         ((8 * H, T), F32, pl.BlockSpec((32, T), lambda j: (j, 0)))] + [(piece, F32, piece_spec)] * 4,
        [state_scr], us=5.0)
    own = plane_exchange([s0, s1, s2, s3])
    if direct:
        tok = wave(
            [early],
            (main, [cot_t, mlp_t], [(act, recv_mlp, n_ff - 1, n_ff - 1), (gp, recv_mlp, n_ff, 0)],
             [(0, 0, 0, 0)] + [(1, kind, 1, kind) for kind in (0, 1, 1, 2)], None), tok, 7.0)
    total, tok = plane_total(own, tok)
    others = across(total, True)

    def fixed(shape, quad):
        return pl.BlockSpec(shape, lambda i: (0, quad))

    def fixed_rows(shape, quad):
        return pl.BlockSpec(shape, lambda i: (quad,) + (0,) * (len(shape) - 1))

    def scores_back(quad, before, tok):
        ins = [(q, fixed((T, QW), quad)), (fq, fixed((T, FW), quad)), (fk, fixed((T, FW), quad)),
               (v, fixed((T, QW), quad)), (gn, fixed((T, QW), quad)), (gd, fixed((T, QW), quad)),
               (gd_t, fixed_rows((32, T), quad))] + [(c, piece_spec) for c in carry]
        ins += [(allow, square), (allow_t, square), (contin, col128), (map_query, fixed_rows((4, 64, 64), quad))]
        aliases = {len(ins) + i: i for i in range(4)} if before else None
        ins += [(a, ANYWHERE) for a in before]
        return run(
            functools.partial(scores_back_kernel, quad), tok, (1,), ins,
            [((T, D), BF16, fixed((T, QW), quad)), ((T, 2 * D), F32, fixed((T, FW), quad)),
             ((T, D), F32, fixed((T, QW), quad)), ((D, 128), F32, fixed_rows((QW, 128), quad))],
            [map_scr, state_scr, pltpu.VMEM((T, FW), BF16)], extra=7, aliases=aliases, us=4.5)

    backs, tok = scores_back(0, [], tok)
    backs, tok = scores_back(1, backs, tok)
    backs, tok = scores_back(2, backs, tok)
    gq, gfk, gv_f, gmq = backs
    upstream, tok = later(own, others, tok)
    if direct:
        mixed_t, tok = turn(mixed, (0,), tok)
        recv_out, tok = send_half(mixed_t, (0,), [gh_low], tok)
        tok = wave(
            [early, main], (wide, [mixed_t], [(gh_low, recv_out, 0, 0)], [(0, 0, 0, 0)], None), tok, 2.0)

    (gk, gv, gmk), tok = run(
        keys_back_kernel, tok, (quads,),
        [(k, qcol), (fk, fcol), (v, qcol), (gfk, fcol), (gv_f, qcol)] + [(c, piece_spec) for c in upstream]
        + [(tail, col128), (map_key, maps)],
        [((T, D), BF16, qcol), ((T, D), BF16, qcol),
         ((D, 128), F32, pl.BlockSpec((QW, 128), lambda j: (j, 0)))],
        [map_scr, state_scr, pltpu.VMEM((T, FW), BF16)], us=60.0)
    if direct:
        recv_qkv, tok = send_half(attn_t, (0, 1, 2), [gq, gk, gv], tok)

    small_spec = whole(small_shape)
    packed = 2 * SMALL_ROWS * (D // 128)
    (gx, keep, send), tok = run(
        inputs_back_kernel, tok, (3,),
        [(gq, full), (gk, full), (gv, full), (w_qkv, columns(D, D)), (x, full), (gh, full), (Held(gain_a), line),
         (gg_mlp, row), (gmq, whole((D, 128))), (gmk, whole((D, 128)))],
        [((T, D), F32, full)] + [(small_shape, F32, small_spec)] * 2,
        [pltpu.VMEM((T, D), F32), pltpu.VMEM((packed, 128), F32)], us=60.0)

    got = core_hop(send)
    if direct:
        tok = wave(
            [], (last, [attn_t], [(gq, recv_qkv, 0, 0), (gk, recv_qkv, 1, 0), (gv, recv_qkv, 2, 0)],
                 [(0, kind, kind, kind) for kind in range(3)], (keep, got)), tok, 4.0)
        tok = wave([early, main, wide], None, tok)
        tok = wave([last], None, tok)
        tok = wave([early, main, wide], None, tok)
        tok = wave([last], None, tok)
        tok = wave([main, wide], None, tok)
        tok = wave([last], None, tok)
        (mine,), tok = run(
            add_kernel, tok, (1,), [(last.small, small_spec), (last.small_got[0], small_spec)],
            [(small_shape, F32, small_spec, Near)], us=0.1)
        got = core_hop(mine.array)
        tok = wave([wide, last], None, tok)
        (grad_w_qkv,) = last.result
        grad_proj_rows, grad_w_fc = main.result
        (grad_w_out,) = wide.result
    else:
        mine = lax.psum(keep + got, "seq")
        got = core_hop(mine)
        summed = lax.psum_scatter(
            jnp.concatenate(
                [tn(attn, gq), tn(attn, gk), tn(attn, gv), tn(mixed, gh_low), tn(mlp_in, gp.array), tn(cot, act.array)],
                axis=1,
            ),
            ("batch", "seq"), scatter_dimension=0, tiled=True)
        grad_w_qkv = summed[:, : 3 * D]
        grad_w_out = summed[:, 3 * D : 4 * D]
        grad_w_fc = summed[:, 4 * D : 4 * D + FF]
        grad_proj_rows = summed[:, 4 * D + FF :]

    heads_shape = (H, 64, 64)
    (grad_map_query, grad_map_key, gains), tok = run(
        unpack_kernel, tok, (1,), [(mine, small_spec), (got, small_spec)],
        [(heads_shape, F32, whole(heads_shape))] * 2 + [((16, 128), F32, whole((16, 128)))],
        [pltpu.VMEM((packed, 128), F32)], us=0.1)
    n = D // 128
    return (
        output[None],
        gx[None],
        grad_w_qkv,
        grad_w_out,
        grad_w_fc,
        grad_proj_rows.T,
        grad_map_query,
        grad_map_key,
        gains[:n].reshape(D),
        gains[n : 2 * n].reshape(D),
    )


def solution(mesh):
    tokens = P("batch", "seq", None)
    flags = P("batch", "seq")
    rows = P(("batch", "seq"), None)
    return jax.shard_map(
        local,
        mesh=mesh,
        in_specs=(tokens,) + (P(),) * 8 + (flags, flags, tokens),
        out_specs=(tokens, tokens, rows, rows, rows, P(None, ("batch", "seq")), P(), P(), P(), P()),
        check_vma=False,
    )
```
